32 devices in a mesh: groups: 2 (over x), cells: 16 (over z, y, core).
Axes of the slice: x: 2, y: 2, z: 4, core: 2. Of those that a mesh axis runs over, the one named last changes fastest.
Arguments:
- basis: bfloat16 [512, 64, 8, 128], P(None, ('groups', 'cells')), parts along dimension 1, may hold values from -6 to 6
- face_speed: float32 [2, 3, 64, 8, 128], P(None, None, ('groups', 'cells')), parts along dimension 2, may hold values from 0.1 to 2
- face_diffusion: float32 [2, 3, 64, 8, 128], P(None, None, ('groups', 'cells')), parts along dimension 2, may hold values from 0.05 to 1
- upwind_flag: int32 [2, 3, 64, 8, 128], P(None, None, ('groups', 'cells')), parts along dimension 2, may hold values 0 or 1
- reaction: float32 [2, 64, 8, 128], P(None, ('groups', 'cells')), parts along dimension 1, may hold values from -2 to 2
- sample_cell: int32 [32, 16, 2], P(('groups', 'cells')), parts along dimension 0, may hold values from 0 to 2047
- sample_count: int32 [32, 16], P(('groups', 'cells')), parts along dimension 0, may hold values from 1 to 2, as said below
Outputs:
- galerkin: float32 [1024, 2, 128], P(('groups', 'cells')), parts along dimension 0
- sample_rows: bfloat16 [32, 16, 2, 9, 128], P(('groups', 'cells')), parts along dimension 0
The draws below stay inside these ranges and needn't reach their ends.
There are 2 independent parts, one for each index of `groups`. The reference program is written for one: setup_inputs(seed, part) draws one part's arguments, and reference() takes and returns one part's arrays. A program takes and returns all parts, laid end to end along the dimension named above; each array names one. Nothing has to cross between parts.
Inputs may be any that keep to these rules, and one draw needn't show every extreme that they name: `sample_count`: in every draw some owner receives 2 live slots from every holding device.
All inputs are finite; a program needn't handle non-finite values. No bound on the sum of `upwind_flag` on one device may be relied on, other than what follows from the above.
Results may differ from the reference program's by a relative error of at most 0.0025.
Values may be sent and summed in bfloat16 or wider, within the bound.
No kernel may reach another device: no remote copies, remote signals or barrier semaphores. Data moves between devices by JAX's collectives and lax.ppermute only.
A program may use at most 64 MiB of HBM per device.

```python
import math
import jax
import jax.numpy as jnp
from jax import lax

M = 512
MB = 128
NPAR = 2
CX = 2
CY = 8
CZ = 128
SLOT = 2
NX = 32
N_CELLS = 16


def draw_sample_count(key, part):
    first_key = jax.random.fold_in(key, 11)
    second_key = jax.random.fold_in(key, 23)
    counts = jax.random.randint(first_key, (N_CELLS, N_CELLS), 1, SLOT + 1)
    full_owner = jax.random.randint(second_key, (), 0, N_CELLS)
    columns = lax.broadcasted_iota(jnp.int32, (N_CELLS, N_CELLS), 1)
    return jnp.where(columns == full_owner, SLOT, counts).astype(jnp.int32)


def place_ends(values, own_key, least, high):
    longest = values.shape.index(max(values.shape))
    spots = []
    for shift in (0, 1):
        where = [jax.random.randint(jax.random.fold_in(own_key, axis), (), 0, length) for axis, length in enumerate(values.shape)]
        where[longest] = (where[longest] + shift) % values.shape[longest]
        spots.append(tuple(where))
    return values.at[spots[0]].set(least).at[spots[1]].set(high)


def spiked(array, stream_key, source, target, parts, factor):
    owner, partner = [(jnp.arange(array.shape[dim]) // (array.shape[dim] // parts)).reshape([-1 if axis == dim else 1 for axis in range(array.ndim)]) for dim in (source, target)]
    chosen = jax.random.permutation(stream_key, parts)[partner]
    strong = (owner == chosen) | (owner == (partner + parts // 2) % parts)
    return jnp.where(strong, factor * array, array)


def shard_levels(rng, dims, cuts, low, high):
    def one(axis_at, shards_of):
        draws = jax.random.uniform(jax.random.fold_in(jax.random.fold_in(rng, 6), axis_at), (shards_of,), jnp.float32, low / len(cuts), high / len(cuts))
        return jnp.repeat(jnp.exp(draws), dims[axis_at] // shards_of).reshape((-1,) + (1,) * (len(dims) - axis_at - 1))

    level = one(*cuts[0])
    for cut in cuts[1:]:
        level = level * one(*cut)
    return level


def gaussian_with(rng, shape, deviation, limit, shards, heavy, held_as=jnp.bfloat16):
    drawn = deviation * jax.random.normal(rng, shape, jnp.float32)
    if shards:
        drawn = drawn * shard_levels(rng, shape, shards, -0.22, 0.18)
    return jnp.clip(spiked(drawn, jax.random.fold_in(rng, 3), *heavy), -limit, limit).astype(held_as)


def setup_inputs(seed: int = 0, part: int = 0) -> dict:
    arg_keys = jax.random.split(jax.random.key(seed), 8)
    part_splits = jax.random.split(jax.random.fold_in(arg_keys[7], part), 8)
    basis = gaussian_with(part_splits[0], (M, NX, CY, CZ), 1.0, 6.0, ((1, 16),), (1, 0, 16, 2.0))
    face_speed = jnp.clip(jnp.exp(math.log(2.0) - 2.9957323 * jax.random.uniform(part_splits[1], (NPAR, 3, NX, CY, CZ), jnp.float32) ** shard_levels(part_splits[1], (NPAR, 3, NX, CY, CZ), ((2, 16),), -0.2, 0.2)), 0.1, 2.0)
    face_diffusion = jnp.clip(jnp.exp(math.log(1.0) - 2.9957323 * jax.random.uniform(part_splits[2], (NPAR, 3, NX, CY, CZ), jnp.float32) ** shard_levels(part_splits[2], (NPAR, 3, NX, CY, CZ), ((2, 16),), -0.2, 0.2)), 0.05, 1.0)
    upwind_flag = place_ends((jax.random.randint(part_splits[3], (NPAR, 3, NX, CY, CZ), 0, 2) < 1).astype(jnp.int32), jax.random.fold_in(part_splits[3], 1), 0, 1)
    reaction = jnp.clip(jax.random.uniform(part_splits[4], (NPAR, NX, CY, CZ), jnp.float32, -2.0, 2.0) * shard_levels(part_splits[4], (NPAR, NX, CY, CZ), ((1, 16),), -0.4, 0.0), -2.0, 2.0)
    sample_cell = place_ends(jax.random.randint(part_splits[5], (N_CELLS, N_CELLS, SLOT), 0, CX * CY * CZ), jax.random.fold_in(part_splits[5], 1), 0, (CX * CY * CZ) - 1).astype(jnp.int32)
    sample_count = draw_sample_count(jax.random.fold_in(jax.random.fold_in(arg_keys[7], part), 71), part)
    return {"basis": basis, "face_speed": face_speed, "face_diffusion": face_diffusion, "upwind_flag": upwind_flag, "reaction": reaction, "sample_cell": sample_cell, "sample_count": sample_count}


def high_flux(state, neighbour, speed_face, diff_face, upwind_face):
    forward = upwind_face == 1
    signed = jnp.where(forward, speed_face, -speed_face)
    upstream = jnp.where(forward, state, neighbour)
    return signed * upstream - diff_face * (neighbour - state)


def next_cells(state, axis_pos):
    zero_layer = jnp.zeros_like(lax.slice_in_dim(state, 0, 1, axis=axis_pos))
    upper_part = lax.slice_in_dim(state, 1, state.shape[axis_pos], axis=axis_pos)
    return jnp.concatenate([upper_part, zero_layer], axis=axis_pos)


def lower_faces(fluxes, axis_pos):
    zero_layer = jnp.zeros_like(lax.slice_in_dim(fluxes, 0, 1, axis=axis_pos))
    lower_part = lax.slice_in_dim(fluxes, 0, fluxes.shape[axis_pos] - 1, axis=axis_pos)
    return jnp.concatenate([zero_layer, lower_part], axis=axis_pos)


def reference(basis, face_speed, face_diffusion, upwind_flag, reaction, sample_cell, sample_count):
    block_bf = basis[:MB]
    state = block_bf.astype(jnp.float32)
    applied_list = []
    for param in range(NPAR):
        result = reaction[param] * state
        for axis_d in range(3):
            neighbour = next_cells(state, axis_d + 1)
            upper = high_flux(state, neighbour, face_speed[param, axis_d], face_diffusion[param, axis_d], upwind_flag[param, axis_d])
            result = result + (upper - lower_faces(upper, axis_d + 1))
        applied_list.append(result.astype(jnp.bfloat16))
    total_cells = NX * CY * CZ
    volume = 1.0 / total_cells
    basis_flat = basis.reshape(M, total_cells)
    applied_flat = jnp.stack(applied_list).reshape(NPAR * MB, total_cells)
    sums = jnp.dot(basis_flat, applied_flat.T, preferred_element_type=jnp.float32)
    galerkin = volume * sums.reshape(M, NPAR, MB)
    holders = lax.broadcasted_iota(jnp.int32, sample_cell.shape, 0)
    x_glob = (holders * CX + sample_cell // (CY * CZ)).astype(jnp.int32)
    y_cell = ((sample_cell // CZ) % CY).astype(jnp.int32)
    z_cell = (sample_cell % CZ).astype(jnp.int32)
    padded = jnp.pad(block_bf, ((0, 0), (1, 1), (1, 1), (1, 1)))
    offsets = [(0, 0, 0), (-1, 0, 0), (1, 0, 0), (0, -1, 0), (0, 1, 0), (0, 0, -1), (0, 0, 1)]
    rows_list = [applied[:, x_glob, y_cell, z_cell] for applied in applied_list]
    for shift_x, shift_y, shift_z in offsets:
        rows_list.append(padded[:, x_glob + 1 + shift_x, y_cell + 1 + shift_y, z_cell + 1 + shift_z])
    stacked = jnp.transpose(jnp.stack(rows_list), (3, 2, 4, 0, 1))
    slots = lax.broadcasted_iota(jnp.int32, sample_cell.shape, 2)
    live = jnp.transpose(slots < sample_count[:, :, None], (1, 0, 2))
    sample_rows = jnp.where(live[:, :, :, None, None], stacked, jnp.zeros_like(stacked))
    return galerkin, sample_rows
```

```python
import functools

import jax
import jax.numpy as jnp
import numpy as np
from jax import lax
from jax.experimental import pallas as pl
from jax.experimental.pallas import tpu as pltpu
from jax.sharding import PartitionSpec as P

MB = 128
SPLITS = 3
BF16 = jnp.bfloat16
F32 = jnp.float32
OFFSETS = 7


def round_up(value, multiple):
    return -(-value // multiple) * multiple


def nt_dot(left, right):
    return lax.dot_general(left, right, (((1,), (1,)), ((), ())), preferred_element_type=F32)


def exact_parts(value):
    parts = []
    for _ in range(SPLITS):
        head = lax.reduce_precision(value, 8, 7)
        parts.append(head.astype(BF16))
        value = value - head
    return parts


def main_kernel(
    dims,
    odd_ref,
    basis_ref,
    inner_ref,
    outer_ref,
    speed_ref,
    diff_ref,
    flag_ref,
    react_ref,
    cell_ref,
    row_from_ref,
    payload_ref,
    coef_ref,
    prev_ref,
    halo_ref,
    applied_ref,
):
    params, layers, width_y, width_z, devices, own, slots, pad = dims
    plane = width_y * width_z
    cells = layers * plane
    odd = odd_ref[0] == 1

    halo_ref[0] = jnp.where(odd, inner_ref[:MB], outer_ref[:MB])
    halo_ref[1] = jnp.where(odd, outer_ref[:MB], inner_ref[:MB])
    tail = jnp.where(odd, inner_ref[MB:], outer_ref[MB:]).astype(F32)
    count = 2 * params
    prev = tail[:count]
    for part in range(1, SPLITS):
        prev = prev + tail[part * count : (part + 1) * count]
    signed_prev, diff_prev = prev[:params], prev[params:]
    prev_ref[:params] = jnp.maximum(signed_prev, 0.0) + diff_prev
    prev_ref[params:] = jnp.minimum(signed_prev, 0.0) - diff_prev

    y_at = lax.broadcasted_iota(jnp.int32, (width_y, width_z), 0)
    z_at = lax.broadcasted_iota(jnp.int32, (width_y, width_z), 1)
    for param in range(params):
        uppers, nexts = [], []
        for layer in range(layers):
            up_d, next_d = [], []
            for axis_d in range(3):
                forward = flag_ref[param, axis_d, layer] == 1
                speed = speed_ref[param, axis_d, layer]
                diff = diff_ref[param, axis_d, layer]
                up_d.append(jnp.where(forward, speed, 0.0) + diff)
                next_d.append(jnp.where(forward, 0.0, -speed) - diff)
            uppers.append(up_d)
            nexts.append(next_d)
        for layer in range(layers):
            diag = react_ref[param, layer]
            diag = diag + uppers[layer][0] + uppers[layer][1] + uppers[layer][2]
            if layer > 0:
                diag = diag - nexts[layer - 1][0]
                coef_ref[param, layer, 2] = -uppers[layer - 1][0]
            coef_ref[param, layer, 1] = nexts[layer][0]
            for axis_d, at, shift_axis, size in ((1, y_at, 0, width_y), (2, z_at, 1, width_z)):
                up, following = uppers[layer][axis_d], nexts[layer][axis_d]
                low_up = jnp.where(at == 0, 0.0, pltpu.roll(up, 1, shift_axis))
                low_next = jnp.where(at == 0, 0.0, pltpu.roll(following, 1, shift_axis))
                diag = diag - low_next
                coef_ref[param, layer, 1 + 2 * axis_d] = jnp.where(at == size - 1, 0.0, following)
                coef_ref[param, layer, 2 + 2 * axis_d] = -low_up
            coef_ref[param, layer, 0] = diag

    def tile(layer, y):
        lanes = slice(y * width_z, (y + 1) * width_z)
        if layer < 0:
            return halo_ref[0, :, lanes]
        if layer >= layers:
            return halo_ref[1, :, lanes]
        start = layer * plane + y * width_z
        return basis_ref[:MB, start : start + width_z]

    for layer in range(layers):
        for y in range(width_y):
            start = layer * plane + y * width_z
            state = tile(layer, y).astype(F32)
            terms = [state, tile(layer + 1, y).astype(F32), tile(layer - 1, y).astype(F32)]
            which = [0, 1, 2]
            if y < width_y - 1:
                terms.append(tile(layer, y + 1).astype(F32))
                which.append(3)
            if y > 0:
                terms.append(tile(layer, y - 1).astype(F32))
                which.append(4)
            terms.append(pltpu.roll(state, width_z - 1, 1))
            terms.append(pltpu.roll(state, 1, 1))
            which += [5, 6]
            for param in range(params):
                total = None
                for at, term in zip(which, terms):
                    if at == 2 and layer == 0:
                        coef = -prev_ref[param : param + 1, y * width_z : (y + 1) * width_z]
                    else:
                        coef = coef_ref[param, layer, at, y : y + 1, :]
                    if at == 0 and layer == 0:
                        coef = coef - prev_ref[params + param : params + param + 1, y * width_z : (y + 1) * width_z]
                    product = coef * term
                    total = product if total is None else total + product
                applied_ref[param * MB : (param + 1) * MB, start : start + width_z] = total.astype(BF16)

    sums = nt_dot(basis_ref[...], applied_ref[...]).astype(BF16)
    for owner in range(devices):
        for param in range(params):
            payload_ref[owner, param * own : (param + 1) * own, :] = sums[
                owner * own : (owner + 1) * own, param * MB : (param + 1) * MB
            ]

    samples = devices * slots
    lanes = lax.broadcasted_iota(jnp.int32, (1, width_z), 1)

    def picked(targets, place):
        return jnp.where(targets - place * width_z == lanes, 1.0, 0.0).astype(BF16)

    center = cell_ref[0 * samples : 1 * samples]
    inside = cell_ref[: 5 * samples]
    below = cell_ref[5 * samples : 6 * samples]
    above = cell_ref[6 * samples : 7 * samples]
    got_in = jnp.zeros((5 * samples, MB), F32)
    got_below = jnp.zeros((samples, MB), F32)
    got_above = jnp.zeros((samples, MB), F32)
    got_applied = jnp.zeros((samples, params * MB), F32)
    for layer in range(-1, layers + 1):
        for y in range(width_y):
            place = layer * width_y + y
            block = tile(layer, y)
            if 0 <= layer < layers:
                got_in = got_in + nt_dot(picked(inside, place), block)
                got_applied = got_applied + nt_dot(
                    picked(center, place), applied_ref[:, place * width_z : (place + 1) * width_z]
                )
            if layer < layers - 1:
                got_below = got_below + nt_dot(picked(below, place), block)
            if layer > 0:
                got_above = got_above + nt_dot(picked(above, place), block)
    pieces = [got_applied[:, param * MB : (param + 1) * MB] for param in range(params)]
    pieces += [got_in[:samples], got_below, got_above, got_in[samples:]]
    gathered = jnp.concatenate(pieces, axis=0).astype(BF16)
    columns = lax.broadcasted_iota(jnp.int32, (1, gathered.shape[0]), 1)
    order = jnp.where(row_from_ref[...] == columns, 1.0, 0.0).astype(BF16)
    ordered = jnp.dot(order, gathered, preferred_element_type=F32).astype(BF16)
    for owner in range(devices):
        payload_ref[owner, params * own :, :] = ordered[owner * pad : (owner + 1) * pad]


def shards(basis, face_speed, face_diffusion, upwind_flag, reaction, sample_cell, sample_count):
    modes, layers, width_y, width_z = basis.shape
    params = face_speed.shape[0]
    devices = lax.axis_size("cells")
    slots = sample_cell.shape[2]
    plane = width_y * width_z
    cells = layers * plane
    own = modes // devices
    rows = params + OFFSETS
    me = lax.axis_index("cells")
    odd = me % 2

    block = basis[:MB].reshape(MB, cells)
    first, last = block[:, :plane], block[:, cells - plane :]
    last_speed = face_speed[:, 0, -1]
    signed = jnp.where(upwind_flag[:, 0, -1] == 1, last_speed, -last_speed)
    faces = jnp.concatenate([signed, face_diffusion[:, 0, -1]], axis=0).reshape(2 * params, plane)
    tail = jnp.concatenate(exact_parts(faces), axis=0)
    tail = jnp.pad(tail, ((0, round_up(tail.shape[0], 16) - tail.shape[0]), (0, 0)))
    to_inner = jnp.concatenate([jnp.where(odd == 1, first, last), tail], axis=0)
    to_outer = jnp.concatenate([jnp.where(odd == 1, last, first), tail], axis=0)
    inner_pairs = [(i, i ^ 1) for i in range(devices)]
    outer_pairs = []
    for i in range(1, devices - 1, 2):
        outer_pairs += [(i, i + 1), (i + 1, i)]
    inner = lax.ppermute(to_inner, "cells", inner_pairs)
    outer = lax.ppermute(to_outer, "cells", outer_pairs)

    flat = sample_cell[0].reshape(devices * slots, 1)
    slot_at = lax.broadcasted_iota(jnp.int32, (devices, slots), 1)
    live = (slot_at < sample_count[0][:, None]).reshape(devices * slots, 1)
    y_at = flat // width_z % width_y
    z_at = flat % width_z
    nowhere = -(4 * cells)

    def target(shift, ok):
        return jnp.where(live & ok, flat + shift, nowhere)

    anywhere = live
    targets = jnp.concatenate(
        [
            target(0, anywhere),
            target(-width_z, y_at > 0),
            target(width_z, y_at < width_y - 1),
            target(-1, z_at > 0),
            target(1, z_at < width_z - 1),
            target(-plane, anywhere),
            target(plane, anywhere),
        ],
        axis=0,
    )

    samples = devices * slots
    pad = round_up(slots * rows, 8)
    row_from = np.full((devices, pad), -1, np.int32)
    for owner in range(devices):
        for slot in range(slots):
            for row in range(rows):
                row_from[owner, row * slots + slot] = row * samples + owner * slots + slot
    dims = (params, layers, width_y, width_z, devices, own, slots, pad)
    vmem = pl.BlockSpec(memory_space=pltpu.VMEM)
    payload = pl.pallas_call(
        functools.partial(main_kernel, dims),
        out_shape=jax.ShapeDtypeStruct((devices, params * own + pad, MB), BF16),
        in_specs=[pl.BlockSpec(memory_space=pltpu.SMEM)] + [vmem] * 9,
        out_specs=vmem,
        scratch_shapes=[
            pltpu.VMEM((params, layers, OFFSETS, width_y, width_z), F32),
            pltpu.VMEM((2 * params, plane), F32),
            pltpu.VMEM((2, MB, plane), BF16),
            pltpu.VMEM((params * MB, cells), BF16),
        ],
        compiler_params=pltpu.CompilerParams(vmem_limit_bytes=40 * 1024 * 1024),
        name="project",
    )(
        odd.reshape(1).astype(jnp.int32),
        basis.reshape(modes, cells),
        inner,
        outer,
        face_speed,
        face_diffusion,
        upwind_flag,
        reaction,
        targets,
        jnp.asarray(row_from.reshape(-1, 1)),
    )
    received = lax.all_to_all(payload, "cells", split_axis=0, concat_axis=0, tiled=True)
    volume = 1.0 / (layers * devices * width_y * width_z)
    summed = jnp.sum(received[:, : params * own].astype(F32), axis=0) * volume
    galerkin = jnp.transpose(summed.reshape(params, own, MB), (1, 0, 2))
    sampled = received[:, params * own : params * own + slots * rows].reshape(devices, rows, slots, MB)
    return (galerkin, jnp.transpose(sampled, (0, 2, 1, 3))[None])


def solution(mesh):
    return jax.shard_map(
        shards,
        mesh=mesh,
        in_specs=(
            P(None, ("groups", "cells"), None, None),
            P(None, None, ("groups", "cells"), None, None),
            P(None, None, ("groups", "cells"), None, None),
            P(None, None, ("groups", "cells"), None, None),
            P(None, ("groups", "cells"), None, None),
            P(("groups", "cells"), None, None),
            P(("groups", "cells"), None),
        ),
        out_specs=(
            P(("groups", "cells"), None, None),
            P(("groups", "cells"), None, None, None, None),
        ),
        check_vma=False,
    )
```

```python
import functools

import jax
import jax.numpy as jnp
import numpy as np
from jax import lax
from jax.experimental import pallas as pl
from jax.experimental.pallas import tpu as pltpu
from jax.sharding import PartitionSpec as P

MB = 128
SPLITS = 3
NARROW_STEPS = 3
BF16 = jnp.bfloat16
F32 = jnp.float32
I32 = jnp.int32
OFFSETS = 7
VMEM = pl.BlockSpec(memory_space=pltpu.VMEM)
SMEM = pl.BlockSpec(memory_space=pltpu.SMEM)
LIMIT = pltpu.CompilerParams(vmem_limit_bytes=40 * 1024 * 1024)


def nt_dot(left, right):
    return lax.dot_general(left, right, (((1,), (1,)), ((), ())), preferred_element_type=F32)


def picked(targets, start, count):
    lanes = lax.broadcasted_iota(I32, (1, count), 1) + start
    return jnp.where(targets == lanes, 1.0, 0.0).astype(BF16)


def halves(value):
    head = value.astype(BF16)
    return head, (value - head.astype(F32)).astype(BF16)


def pack_kernel(dims, odd_ref, flat_ref, speed_ref, diff_ref, flag_ref, inner_ref, outer_ref):
    params, layers, width_y, width_z, plane = dims
    odd = odd_ref[0]
    last = (layers - 1) * plane
    to_inner = pl.multiple_of((1 - odd) * last, width_z)
    to_outer = pl.multiple_of(odd * last, width_z)
    inner_ref[:MB] = flat_ref[:MB, pl.ds(to_inner, plane)]
    outer_ref[:MB] = flat_ref[:MB, pl.ds(to_outer, plane)]
    speed = speed_ref[:, 0, layers - 1].reshape(params * width_y, width_z)
    forward = flag_ref[:, 0, layers - 1].reshape(params * width_y, width_z) == 1
    signed = jnp.where(forward, speed, -speed)
    diff = diff_ref[:, 0, layers - 1].reshape(params * width_y, width_z)
    for ref in (inner_ref, outer_ref):
        ref[MB:] = jnp.zeros((params * width_y, plane), BF16)
    for at, value in enumerate((signed, diff)):
        for part in range(SPLITS):
            head = value.astype(BF16)
            value = value - head.astype(F32)
            lane = (at * SPLITS + part) * width_z
            inner_ref[MB:, lane : lane + width_z] = head
            outer_ref[MB:, lane : lane + width_z] = head


def local_kernel(
    dims,
    flat_ref,
    speed_ref,
    diff_ref,
    flag_ref,
    react_ref,
    cell_ref,
    acc_ref,
    edge_ref,
    in_ref,
    side_ref,
    center_ref,
    coef_ref,
):
    params, layers, width_y, width_z, plane, samples = dims
    y_at = lax.broadcasted_iota(I32, (width_y, width_z), 0)
    z_at = lax.broadcasted_iota(I32, (width_y, width_z), 1)
    for param in range(params):
        uppers, nexts = [], []
        for layer in range(layers):
            up_d, next_d = [], []
            for axis_d in range(3):
                forward = flag_ref[param, axis_d, layer] == 1
                speed = speed_ref[param, axis_d, layer]
                diff = diff_ref[param, axis_d, layer]
                up_d.append(jnp.where(forward, speed, 0.0) + diff)
                next_d.append(jnp.where(forward, 0.0, -speed) - diff)
            uppers.append(up_d)
            nexts.append(next_d)
        edge_ref[param] = nexts[layers - 1][0]
        for layer in range(layers):
            diag = react_ref[param, layer]
            diag = diag + uppers[layer][0] + uppers[layer][1] + uppers[layer][2]
            if layer > 0:
                diag = diag - nexts[layer - 1][0]
                coef_ref[param, layer, 2] = -uppers[layer - 1][0]
            coef_ref[param, layer, 1] = nexts[layer][0]
            for axis_d, at, shift_axis, size in ((1, y_at, 0, width_y), (2, z_at, 1, width_z)):
                up, following = uppers[layer][axis_d], nexts[layer][axis_d]
                low_up = jnp.where(at == 0, 0.0, pltpu.roll(up, 1, shift_axis))
                low_next = jnp.where(at == 0, 0.0, pltpu.roll(following, 1, shift_axis))
                diag = diag - low_next
                coef_ref[param, layer, 1 + 2 * axis_d] = jnp.where(at == size - 1, 0.0, following)
                coef_ref[param, layer, 2 + 2 * axis_d] = -low_up
            coef_ref[param, layer, 0] = diag

    def tile(layer, y):
        start = layer * plane + y * width_z
        return flat_ref[:MB, start : start + width_z].astype(F32)

    for layer in range(layers):
        for y in range(width_y):
            start = layer * plane + y * width_z
            state = tile(layer, y)
            terms = [(0, state), (5, pltpu.roll(state, width_z - 1, 1)), (6, pltpu.roll(state, 1, 1))]
            if layer < layers - 1:
                terms.append((1, tile(layer + 1, y)))
            if layer > 0:
                terms.append((2, tile(layer - 1, y)))
            if y < width_y - 1:
                terms.append((3, tile(layer, y + 1)))
            if y > 0:
                terms.append((4, tile(layer, y - 1)))
            for param in range(params):
                total = None
                for at, term in terms:
                    product = coef_ref[param, layer, at, y : y + 1, :] * term
                    total = product if total is None else total + product
                acc_ref[param * MB : (param + 1) * MB, start : start + width_z] = total

    cells = layers * plane
    block = flat_ref[:MB, :]
    inside = picked(cell_ref[: 5 * samples], 0, cells)
    center_ref[...] = inside[:samples]
    in_ref[...] = nt_dot(inside, block).astype(BF16)
    side_ref[:samples] = nt_dot(picked(cell_ref[5 * samples : 6 * samples], 0, cells), block).astype(BF16)
    side_ref[samples:] = nt_dot(picked(cell_ref[6 * samples :], 0, cells), block).astype(BF16)


def project_kernel(
    dims,
    odd_ref,
    dest_ref,
    flat_ref,
    inner_ref,
    outer_ref,
    acc_ref,
    edge_ref,
    in_ref,
    side_ref,
    center_ref,
    cell_ref,
    row_ref,
    keep_ref,
    keep_rows_ref,
    packet_ref,
    halo_ref,
    prev_ref,
    applied_ref,
    sums_ref,
):
    params, layers, width_y, width_z, plane, samples, devices, own = dims
    cells = layers * plane
    odd = odd_ref[0] == 1
    halo_ref[0] = jnp.where(odd, inner_ref[:MB], outer_ref[:MB])
    halo_ref[1] = jnp.where(odd, outer_ref[:MB], inner_ref[:MB])
    tail = jnp.where(odd, inner_ref[MB:], outer_ref[MB:]).astype(F32)
    faces = []
    for at in range(2):
        value = None
        for part in range(SPLITS):
            lane = (at * SPLITS + part) * width_z
            piece = tail[:, lane : lane + width_z]
            value = piece if value is None else value + piece
        faces.append(value)
    signed_prev, diff_prev = faces
    prev_ref[0] = -(jnp.maximum(signed_prev, 0.0) + diff_prev)
    prev_ref[1] = diff_prev - jnp.minimum(signed_prev, 0.0)

    for layer in range(layers):
        for y in range(width_y):
            start = layer * plane + y * width_z
            lanes = slice(y * width_z, (y + 1) * width_z)
            for param in range(params):
                modes = slice(param * MB, (param + 1) * MB)
                total = acc_ref[modes, start : start + width_z]
                row = param * width_y + y
                if layer == 0:
                    total = total + prev_ref[1, row : row + 1, :] * flat_ref[:MB, start : start + width_z].astype(F32)
                    total = total + prev_ref[0, row : row + 1, :] * halo_ref[0, :, lanes].astype(F32)
                if layer == layers - 1:
                    total = total + edge_ref[param, y : y + 1, :] * halo_ref[1, :, lanes].astype(F32)
                applied_ref[modes, start : start + width_z] = total.astype(BF16)

    sums = nt_dot(flat_ref[...], applied_ref[...])
    for param in range(params):
        sums_ref[pl.ds(param, sums.shape[0], stride=params), :] = sums[:, param * MB : (param + 1) * MB]
    size = own * params
    half = devices // 2
    for place in range(devices):
        start = pl.multiple_of(dest_ref[place] * size, size)
        terms = sums_ref[pl.ds(start, size), :]
        if place < half:
            keep_ref[place * size : (place + 1) * size] = terms
        else:
            head, rest = halves(terms)
            at = (place - half) * size
            packet_ref[at : at + size] = head
            packet_ref[half * size + at : half * size + at + size] = rest

    got_applied = nt_dot(center_ref[...], applied_ref[...]).astype(BF16)
    below = picked(cell_ref[5 * samples : 6 * samples], -plane, plane)
    above = picked(cell_ref[6 * samples :], cells, plane)
    got_below = nt_dot(below, halo_ref[0]).astype(BF16) + side_ref[:samples]
    got_above = nt_dot(above, halo_ref[1]).astype(BF16) + side_ref[samples:]
    pieces = [got_applied[:, param * MB : (param + 1) * MB] for param in range(params)]
    pieces += [in_ref[:samples], got_below, got_above, in_ref[samples:]]
    gathered = jnp.concatenate(pieces, axis=0)
    order = picked(row_ref[...], 0, gathered.shape[0])
    ordered = jnp.dot(order, gathered, preferred_element_type=F32).astype(BF16)
    count = ordered.shape[0] // 2
    keep_rows_ref[...] = ordered[:count]
    packet_ref[2 * half * size :] = ordered[count:]


def merge_kernel(wide_in, wide_out, keep_ref, keep_rows_ref, got_ref, shuffle_ref, keep_out, rows_out, packet_out):
    size = keep_ref.shape[0]
    half = size // 2
    total = keep_ref[...] + got_ref[:size].astype(F32)
    if wide_in:
        total = total + got_ref[size : 2 * size].astype(F32)
    keep_out[...] = total[:half]
    if wide_out:
        head, rest = halves(total[half:])
        packet_out[:half] = head
        packet_out[half : 2 * half] = rest
    else:
        packet_out[:half] = total[half:].astype(BF16)
    count = keep_rows_ref.shape[0]
    rows = jnp.concatenate([keep_rows_ref[...], got_ref[got_ref.shape[0] - count :]], axis=0)
    order = picked(shuffle_ref[...], 0, 2 * count)
    ordered = jnp.dot(order, rows, preferred_element_type=F32).astype(BF16)
    rows_out[...] = ordered[:count]
    packet_out[packet_out.shape[0] - count :] = ordered[count:]


def final_kernel(wide_in, volume, keep_ref, keep_rows_ref, got_ref, final_ref, sum_out, rows_out):
    size = keep_ref.shape[0]
    total = keep_ref[...] + got_ref[:size].astype(F32)
    if wide_in:
        total = total + got_ref[size : 2 * size].astype(F32)
    sum_out[...] = volume * total
    count = keep_rows_ref.shape[0]
    rows = jnp.concatenate([keep_rows_ref[...], got_ref[got_ref.shape[0] - count :]], axis=0)
    order = picked(final_ref[...], 0, 2 * count)
    rows_out[...] = jnp.dot(order, rows, preferred_element_type=F32).astype(BF16)


def shape(dims, dtype):
    return jax.ShapeDtypeStruct(dims, dtype)


def shards(basis, face_speed, face_diffusion, upwind_flag, reaction, sample_cell, sample_count):
    modes, layers, width_y, width_z = basis.shape
    params = face_speed.shape[0]
    devices = lax.axis_size("cells")
    slots = sample_cell.shape[2]
    plane = width_y * width_z
    cells = layers * plane
    own = modes // devices
    rows = params + OFFSETS
    samples = devices * slots
    me = lax.axis_index("cells")
    odd = (me % 2).astype(I32).reshape(1)
    steps = devices.bit_length() - 1

    flat = basis.reshape(modes, cells)
    tail = params * width_y
    halo = shape((MB + tail, plane), BF16)
    to_inner, to_outer = pl.pallas_call(
        functools.partial(pack_kernel, (params, layers, width_y, width_z, plane)),
        out_shape=(halo, halo),
        in_specs=[SMEM] + [VMEM] * 4,
        out_specs=(VMEM, VMEM),
        compiler_params=LIMIT,
        name="pack_halo",
    )(odd, flat, face_speed, face_diffusion, upwind_flag)
    inner_pairs = [(i, i ^ 1) for i in range(devices)]
    outer_pairs = []
    for i in range(1, devices - 1, 2):
        outer_pairs += [(i, i + 1), (i + 1, i)]
    outer = lax.ppermute(to_outer, "cells", outer_pairs)
    inner = lax.ppermute(to_inner, "cells", inner_pairs)

    cell = sample_cell[0].reshape(samples, 1)
    slot_at = lax.broadcasted_iota(I32, (devices, slots), 1)
    live = (slot_at < sample_count[0][:, None]).reshape(samples, 1)
    y_at = cell // width_z % width_y
    z_at = cell % width_z
    nowhere = -(4 * cells)

    def target(shift, ok):
        return jnp.where(live & ok, cell + shift, nowhere)

    targets = jnp.concatenate(
        [
            target(0, live),
            target(-width_z, y_at > 0),
            target(width_z, y_at < width_y - 1),
            target(-1, z_at > 0),
            target(1, z_at < width_z - 1),
            target(-plane, live),
            target(plane, live),
        ],
        axis=0,
    )

    block = slots * rows
    relative = np.zeros(devices, np.int32)
    came = np.zeros(devices, np.int32)
    shuffle = np.zeros((devices, block), np.int32)
    for place in range(devices):
        bits = [(place >> (steps - 1 - step)) & 1 for step in range(steps)]
        relative[place] = sum(bit << step for step, bit in enumerate(bits))
        came[relative[place]] = (bits[-1] << (steps - 1)) + (place >> 1)
        shuffle[place] = ((bits[-1] << (steps - 1)) + (place >> 1)) * block + np.arange(block)
    in_block = np.arange(block)
    by_row = (in_block // slots) * samples + in_block % slots
    dest = jnp.asarray(relative) ^ me
    row_from = (dest[:, None] * slots + jnp.asarray(by_row)[None]).reshape(-1, 1).astype(I32)
    source = jnp.asarray(came)[jnp.arange(devices) ^ me]
    final_from = (source[:, None] * block + jnp.asarray(in_block)[None]).reshape(-1, 1).astype(I32)
    shuffle = jnp.asarray(shuffle.reshape(-1, 1))

    acc, edge, got_in, got_side, center = pl.pallas_call(
        functools.partial(local_kernel, (params, layers, width_y, width_z, plane, samples)),
        out_shape=(
            shape((params * MB, cells), F32),
            shape((params, width_y, width_z), F32),
            shape((5 * samples, MB), BF16),
            shape((2 * samples, MB), BF16),
            shape((samples, cells), BF16),
        ),
        in_specs=[VMEM] * 6,
        out_specs=(VMEM,) * 5,
        scratch_shapes=[pltpu.VMEM((params, layers, OFFSETS, width_y, width_z), F32)],
        compiler_params=LIMIT,
        cost_estimate=pl.CostEstimate(flops=100_000_000, bytes_accessed=6_000_000, transcendentals=0),
        name="local_stencil",
    )(flat, face_speed, face_diffusion, upwind_flag, reaction, targets)

    size = own * params
    half = devices // 2
    count = half * block
    keep, keep_rows, packet = pl.pallas_call(
        functools.partial(project_kernel, (params, layers, width_y, width_z, plane, samples, devices, own)),
        out_shape=(
            shape((half * size, MB), F32),
            shape((count, MB), BF16),
            shape((2 * half * size + count, MB), BF16),
        ),
        in_specs=[SMEM] * 2 + [VMEM] * 10,
        out_specs=(VMEM,) * 3,
        scratch_shapes=[
            pltpu.VMEM((2, MB, plane), BF16),
            pltpu.VMEM((2, tail, width_z), F32),
            pltpu.VMEM((params * MB, cells), BF16),
            pltpu.VMEM((params * modes, MB), F32),
        ],
        compiler_params=LIMIT,
        name="project",
    )(odd, dest.astype(I32), flat, inner, outer, acc, edge, got_in, got_side, center, targets, row_from)

    wide = True
    for step in range(steps):
        got = lax.ppermute(packet, "cells", [(i, i ^ (1 << step)) for i in range(devices)])
        if step < steps - 1:
            next_wide = not 0 < step + 1 <= NARROW_STEPS
            half //= 2
            packet_rows = (2 if next_wide else 1) * half * size + count
            keep, keep_rows, packet = pl.pallas_call(
                functools.partial(merge_kernel, wide, next_wide),
                out_shape=(
                    shape((half * size, MB), F32),
                    shape((count, MB), BF16),
                    shape((packet_rows, MB), BF16),
                ),
                in_specs=[VMEM] * 4,
                out_specs=(VMEM,) * 3,
                compiler_params=LIMIT,
                name="merge",
            )(keep, keep_rows, got, shuffle)
            wide = next_wide
    volume = 1.0 / (layers * devices * width_y * width_z)
    summed, sampled = pl.pallas_call(
        functools.partial(final_kernel, wide, volume),
        out_shape=(shape((size, MB), F32), shape((2 * count, MB), BF16)),
        in_specs=[VMEM] * 4,
        out_specs=(VMEM,) * 2,
        compiler_params=LIMIT,
        name="finish",
    )(keep, keep_rows, got, final_from)
    galerkin = summed.reshape(own, params, MB)
    sampled = sampled.reshape(devices, rows, slots, MB)
    return (galerkin, jnp.transpose(sampled, (0, 2, 1, 3))[None])


def solution(mesh):
    return jax.shard_map(
        shards,
        mesh=mesh,
        in_specs=(
            P(None, ("groups", "cells"), None, None),
            P(None, None, ("groups", "cells"), None, None),
            P(None, None, ("groups", "cells"), None, None),
            P(None, None, ("groups", "cells"), None, None),
            P(None, ("groups", "cells"), None, None),
            P(("groups", "cells"), None, None),
            P(("groups", "cells"), None),
        ),
        out_specs=(
            P(("groups", "cells"), None, None),
            P(("groups", "cells"), None, None, None, None),
        ),
        check_vma=False,
    )
```

```python
import functools

import jax
import jax.numpy as jnp
import numpy as np
from jax import lax
from jax.experimental import pallas as pl
from jax.experimental.pallas import tpu as pltpu
from jax.sharding import PartitionSpec as P

MB = 128
SPLITS = 3
NARROW_STEPS = 3
BF16 = jnp.bfloat16
F32 = jnp.float32
I32 = jnp.int32
OFFSETS = 7
VMEM = pl.BlockSpec(memory_space=pltpu.VMEM)
LIMIT = pltpu.CompilerParams(vmem_limit_bytes=40 * 1024 * 1024)


def nt_dot(left, right):
    return lax.dot_general(left, right, (((1,), (1,)), ((), ())), preferred_element_type=F32)


def picked(targets, start, count):
    lanes = lax.broadcasted_iota(I32, (1, count), 1) + start
    return jnp.where(targets == lanes, 1.0, 0.0).astype(BF16)


def halves(value):
    head = value.astype(BF16)
    return head, (value - head.astype(F32)).astype(BF16)


def core():
    return lax.rem(lax.axis_index("cells"), 2)


def face_parts(speed, diff, flag):
    parts = []
    for value in (jnp.where(flag == 1, speed, -speed), diff):
        for _ in range(SPLITS):
            head = value.astype(BF16)
            value = value - head.astype(F32)
            parts.append(head)
    return parts


def pack_kernel(dims, basis_ref, speed_ref, diff_ref, flag_ref, outer_ref, speed_buf, diff_buf, flag_buf, sems):
    params, layers = dims
    last = layers - 1
    layer = core() * last
    copies = [
        pltpu.make_async_copy(basis_ref.at[pl.ds(0, MB), layer], outer_ref.at[pl.ds(0, MB)], sems.at[0]),
        pltpu.make_async_copy(speed_ref.at[:, 0, last], speed_buf, sems.at[1]),
        pltpu.make_async_copy(diff_ref.at[:, 0, last], diff_buf, sems.at[2]),
        pltpu.make_async_copy(flag_ref.at[:, 0, last], flag_buf, sems.at[3]),
    ]
    for copy in copies:
        copy.start()
    for copy in copies[1:]:
        copy.wait()
    for at, part in enumerate(face_parts(speed_buf[...], diff_buf[...], flag_buf[...])):
        outer_ref[MB + at * params : MB + (at + 1) * params] = part
    copies[0].wait()


def local_kernel(
    dims,
    flat_ref,
    speed_ref,
    diff_ref,
    flag_ref,
    react_ref,
    cell_ref,
    acc_ref,
    edge_ref,
    in_ref,
    side_ref,
    center_ref,
    inner_ref,
    coef_ref,
):
    params, layers, width_y, width_z, plane, samples = dims
    y_at = lax.broadcasted_iota(I32, (width_y, width_z), 0)
    z_at = lax.broadcasted_iota(I32, (width_y, width_z), 1)
    for param in range(params):
        uppers, nexts = [], []
        for layer in range(layers):
            up_d, next_d = [], []
            for axis_d in range(3):
                forward = flag_ref[param, axis_d, layer] == 1
                speed = speed_ref[param, axis_d, layer]
                diff = diff_ref[param, axis_d, layer]
                up_d.append(jnp.where(forward, speed, 0.0) + diff)
                next_d.append(jnp.where(forward, 0.0, -speed) - diff)
            uppers.append(up_d)
            nexts.append(next_d)
        edge_ref[param] = nexts[layers - 1][0]
        for layer in range(layers):
            diag = react_ref[param, layer]
            diag = diag + uppers[layer][0] + uppers[layer][1] + uppers[layer][2]
            if layer > 0:
                diag = diag - nexts[layer - 1][0]
                coef_ref[param, layer, 2] = -uppers[layer - 1][0]
            coef_ref[param, layer, 1] = nexts[layer][0]
            for axis_d, at, shift_axis, size in ((1, y_at, 0, width_y), (2, z_at, 1, width_z)):
                up, following = uppers[layer][axis_d], nexts[layer][axis_d]
                low_up = jnp.where(at == 0, 0.0, pltpu.roll(up, 1, shift_axis))
                low_next = jnp.where(at == 0, 0.0, pltpu.roll(following, 1, shift_axis))
                diag = diag - low_next
                coef_ref[param, layer, 1 + 2 * axis_d] = jnp.where(at == size - 1, 0.0, following)
                coef_ref[param, layer, 2 + 2 * axis_d] = -low_up
            coef_ref[param, layer, 0] = diag

    def tile(layer, y):
        start = layer * plane + y * width_z
        return flat_ref[:MB, start : start + width_z].astype(F32)

    for layer in range(layers):
        for y in range(width_y):
            start = layer * plane + y * width_z
            state = tile(layer, y)
            terms = [(0, state), (5, pltpu.roll(state, width_z - 1, 1)), (6, pltpu.roll(state, 1, 1))]
            if layer < layers - 1:
                terms.append((1, tile(layer + 1, y)))
            if layer > 0:
                terms.append((2, tile(layer - 1, y)))
            if y < width_y - 1:
                terms.append((3, tile(layer, y + 1)))
            if y > 0:
                terms.append((4, tile(layer, y - 1)))
            for param in range(params):
                total = None
                for at, term in terms:
                    product = coef_ref[param, layer, at, y : y + 1, :] * term
                    total = product if total is None else total + product
                acc_ref[param * MB : (param + 1) * MB, start : start + width_z] = total

    start = pl.multiple_of((1 - core()) * (layers - 1) * plane, plane)
    inner_ref[:MB] = flat_ref[:MB, pl.ds(start, plane)]
    inner_ref[MB:] = jnp.zeros((params * width_y, plane), BF16)
    faces = [ref[:, 0, layers - 1].reshape(params * width_y, width_z) for ref in (speed_ref, diff_ref, flag_ref)]
    for at, part in enumerate(face_parts(*faces)):
        inner_ref[MB:, at * width_z : (at + 1) * width_z] = part

    cells = layers * plane
    block = flat_ref[:MB, :]
    inside = picked(cell_ref[: 5 * samples], 0, cells)
    center_ref[...] = inside[:samples]
    in_ref[...] = nt_dot(inside, block).astype(BF16)
    side_ref[:samples] = nt_dot(picked(cell_ref[5 * samples : 6 * samples], 0, cells), block).astype(BF16)
    side_ref[samples:] = nt_dot(picked(cell_ref[6 * samples :], 0, cells), block).astype(BF16)


def finish_layer(dims, from_next, layer, faces, halo, flat_ref, acc_ref, edge_ref, applied_ref, coef_ref):
    params, layers, width_y, width_z, plane = dims
    signed = faces[0] + faces[1] + faces[2]
    diff = faces[3] + faces[4] + faces[5]
    edge = edge_ref[...].reshape(params * width_y, width_z)
    coef_ref[0] = jnp.where(from_next, edge, -(jnp.maximum(signed, 0.0) + diff))
    coef_ref[1] = jnp.where(from_next, 0.0, diff - jnp.minimum(signed, 0.0))
    for y in range(width_y):
        at = pl.multiple_of(layer * plane + y * width_z, width_z)
        lanes = slice(y * width_z, (y + 1) * width_z)
        state = flat_ref[:MB, pl.ds(at, width_z)].astype(F32)
        beside = halo[:MB, lanes].astype(F32)
        for param in range(params):
            modes = slice(param * MB, (param + 1) * MB)
            row = param * width_y + y
            total = acc_ref[modes, pl.ds(at, width_z)]
            total = total + coef_ref[1, row : row + 1, :] * state
            total = total + coef_ref[0, row : row + 1, :] * beside
            applied_ref[modes, lanes] = total.astype(BF16)


def near_kernel(dims, flat_ref, inner_ref, acc_ref, edge_ref, center_ref, cell_ref, sums_ref, picks_ref, side_ref, applied_ref, coef_ref):
    params, layers, width_y, width_z, plane, samples = dims
    odd = core() == 1
    layer = (1 - core()) * (layers - 1)
    start = pl.multiple_of(layer * plane, plane)
    faces = [inner_ref[MB:, at * width_z : (at + 1) * width_z].astype(F32) for at in range(2 * SPLITS)]
    finish_layer(dims[:5], jnp.logical_not(odd), layer, faces, inner_ref, flat_ref, acc_ref, edge_ref, applied_ref, coef_ref)
    sums_ref[...] = nt_dot(flat_ref[:, pl.ds(start, plane)], applied_ref[...])
    picks_ref[...] = nt_dot(center_ref[:, pl.ds(start, plane)], applied_ref[...])
    below = cell_ref[5 * samples : 6 * samples] + plane
    above = cell_ref[6 * samples :] - layers * plane
    side_ref[...] = nt_dot(picked(jnp.where(odd, below, above), 0, plane), inner_ref[:MB]).astype(BF16)


def project_kernel(
    dims,
    relative,
    flat_ref,
    outer_ref,
    tail_ref,
    acc_ref,
    edge_ref,
    in_ref,
    side_ref,
    center_ref,
    near_sums_ref,
    near_picks_ref,
    near_side_ref,
    cell_ref,
    row_ref,
    keep_ref,
    keep_rows_ref,
    packet_ref,
    applied_ref,
    coef_ref,
    sums_ref,
):
    params, layers, width_y, width_z, plane, samples, devices, own = dims
    odd = core() == 1
    layer = core() * (layers - 1)
    lane = pl.multiple_of(layer * plane, plane)
    faces = []
    for at in range(2 * SPLITS):
        part = tail_ref[MB + at * params : MB + (at + 1) * params].astype(F32)
        faces.append(part.reshape(params * width_y, width_z))
    finish_layer(dims[:5], odd, layer, faces, outer_ref, flat_ref, acc_ref, edge_ref, applied_ref, coef_ref)

    sums = near_sums_ref[...] + nt_dot(flat_ref[:, pl.ds(lane, plane)], applied_ref[...])
    for param in range(params):
        sums_ref[pl.ds(param, sums.shape[0], stride=params), :] = sums[:, param * MB : (param + 1) * MB]
    size = own * params
    half = devices // 2
    me = lax.axis_index("cells")
    for place in range(devices):
        start = pl.multiple_of((me ^ relative[place]) * size, size)
        terms = sums_ref[pl.ds(start, size), :]
        if place < half:
            keep_ref[place * size : (place + 1) * size] = terms
        else:
            head, rest = halves(terms)
            at = (place - half) * size
            packet_ref[at : at + size] = head
            packet_ref[half * size + at : half * size + at + size] = rest

    picks = nt_dot(center_ref[:, pl.ds(lane, plane)], applied_ref[...])
    got_applied = (near_picks_ref[...] + picks).astype(BF16)
    below = cell_ref[5 * samples : 6 * samples] + plane
    above = cell_ref[6 * samples :] - layers * plane
    far = nt_dot(picked(jnp.where(odd, above, below), 0, plane), outer_ref[...]).astype(BF16)
    near = near_side_ref[...]
    got_below = side_ref[:samples] + jnp.where(odd, near, far)
    got_above = side_ref[samples:] + jnp.where(odd, far, near)
    pieces = [got_applied[:, param * MB : (param + 1) * MB] for param in range(params)]
    pieces += [in_ref[:samples], got_below, got_above, in_ref[samples:]]
    gathered = jnp.concatenate(pieces, axis=0)
    order = picked(row_ref[...], 0, gathered.shape[0])
    ordered = jnp.dot(order, gathered, preferred_element_type=F32).astype(BF16)
    count = ordered.shape[0] // 2
    keep_rows_ref[...] = ordered[:count]
    packet_ref[2 * half * size :] = ordered[count:]


def merge_kernel(wide_in, wide_out, keep_ref, keep_rows_ref, got_ref, shuffle_ref, keep_out, rows_out, packet_out):
    size = keep_ref.shape[0]
    half = size // 2
    total = keep_ref[...] + got_ref[:size].astype(F32)
    if wide_in:
        total = total + got_ref[size : 2 * size].astype(F32)
    keep_out[...] = total[:half]
    if wide_out:
        head, rest = halves(total[half:])
        packet_out[:half] = head
        packet_out[half : 2 * half] = rest
    else:
        packet_out[:half] = total[half:].astype(BF16)
    count = keep_rows_ref.shape[0]
    rows = jnp.concatenate([keep_rows_ref[...], got_ref[got_ref.shape[0] - count :]], axis=0)
    order = picked(shuffle_ref[...], 0, 2 * count)
    ordered = jnp.dot(order, rows, preferred_element_type=F32).astype(BF16)
    rows_out[...] = ordered[:count]
    packet_out[packet_out.shape[0] - count :] = ordered[count:]


def final_kernel(wide_in, volume, keep_ref, keep_rows_ref, got_ref, final_ref, sum_out, rows_out):
    size = keep_ref.shape[0]
    total = keep_ref[...] + got_ref[:size].astype(F32)
    if wide_in:
        total = total + got_ref[size : 2 * size].astype(F32)
    sum_out[...] = volume * total
    count = keep_rows_ref.shape[0]
    rows = jnp.concatenate([keep_rows_ref[...], got_ref[got_ref.shape[0] - count :]], axis=0)
    order = picked(final_ref[...], 0, 2 * count)
    rows_out[...] = jnp.dot(order, rows, preferred_element_type=F32).astype(BF16)


def shape(dims, dtype):
    return jax.ShapeDtypeStruct(dims, dtype)


def shards(basis, face_speed, face_diffusion, upwind_flag, reaction, sample_cell, sample_count):
    modes, layers, width_y, width_z = basis.shape
    params = face_speed.shape[0]
    devices = lax.axis_size("cells")
    slots = sample_cell.shape[2]
    plane = width_y * width_z
    cells = layers * plane
    own = modes // devices
    rows = params + OFFSETS
    samples = devices * slots
    me = lax.axis_index("cells")
    steps = devices.bit_length() - 1

    tail = params * width_y
    hbm = pl.BlockSpec(memory_space=pl.ANY)
    to_outer = pl.pallas_call(
        functools.partial(pack_kernel, (params, layers)),
        out_shape=shape((MB + 2 * SPLITS * params, width_y, width_z), BF16),
        in_specs=[hbm] * 4,
        out_specs=VMEM,
        scratch_shapes=[
            pltpu.VMEM((params, width_y, width_z), F32),
            pltpu.VMEM((params, width_y, width_z), F32),
            pltpu.VMEM((params, width_y, width_z), I32),
            pltpu.SemaphoreType.DMA((4,)),
        ],
        compiler_params=LIMIT,
        name="pack_outer",
    )(basis, face_speed, face_diffusion, upwind_flag)
    inner_pairs = [(i, i ^ 1) for i in range(devices)]
    outer_pairs = []
    for i in range(1, devices - 1, 2):
        outer_pairs += [(i, i + 1), (i + 1, i)]
    outer = lax.ppermute(to_outer, "cells", outer_pairs)
    flat = basis.reshape(modes, cells)

    cell = sample_cell[0].reshape(samples, 1)
    slot_at = lax.broadcasted_iota(I32, (devices, slots), 1)
    live = (slot_at < sample_count[0][:, None]).reshape(samples, 1)
    y_at = cell // width_z % width_y
    z_at = cell % width_z
    nowhere = -(4 * cells)

    def target(shift, ok):
        return jnp.where(live & ok, cell + shift, nowhere)

    targets = jnp.concatenate(
        [
            target(0, live),
            target(-width_z, y_at > 0),
            target(width_z, y_at < width_y - 1),
            target(-1, z_at > 0),
            target(1, z_at < width_z - 1),
            target(-plane, live),
            target(plane, live),
        ],
        axis=0,
    )

    block = slots * rows
    relative = np.zeros(devices, np.int32)
    came = np.zeros(devices, np.int32)
    shuffle = np.zeros((devices, block), np.int32)
    for place in range(devices):
        bits = [(place >> (steps - 1 - step)) & 1 for step in range(steps)]
        relative[place] = sum(bit << step for step, bit in enumerate(bits))
        came[relative[place]] = (bits[-1] << (steps - 1)) + (place >> 1)
        shuffle[place] = ((bits[-1] << (steps - 1)) + (place >> 1)) * block + np.arange(block)
    in_block = np.arange(block)
    by_row = (in_block // slots) * samples + in_block % slots
    dest = jnp.asarray(relative) ^ me
    row_from = (dest[:, None] * slots + jnp.asarray(by_row)[None]).reshape(-1, 1).astype(I32)
    source = jnp.asarray(came)[jnp.arange(devices) ^ me]
    final_from = (source[:, None] * block + jnp.asarray(in_block)[None]).reshape(-1, 1).astype(I32)
    shuffle = jnp.asarray(shuffle.reshape(-1, 1))

    acc, edge, got_in, got_side, center, to_inner = pl.pallas_call(
        functools.partial(local_kernel, (params, layers, width_y, width_z, plane, samples)),
        out_shape=(
            shape((params * MB, cells), F32),
            shape((params, width_y, width_z), F32),
            shape((5 * samples, MB), BF16),
            shape((2 * samples, MB), BF16),
            shape((samples, cells), BF16),
            shape((MB + tail, plane), BF16),
        ),
        in_specs=[VMEM] * 6,
        out_specs=(VMEM,) * 6,
        scratch_shapes=[pltpu.VMEM((params, layers, OFFSETS, width_y, width_z), F32)],
        compiler_params=LIMIT,
        cost_estimate=pl.CostEstimate(flops=100_000_000, bytes_accessed=6_000_000, transcendentals=0),
        name="local_stencil",
    )(flat, face_speed, face_diffusion, upwind_flag, reaction, targets)

    inner = lax.ppermute(to_inner, "cells", inner_pairs)
    near_sums, near_picks, near_side = pl.pallas_call(
        functools.partial(near_kernel, (params, layers, width_y, width_z, plane, samples)),
        out_shape=(
            shape((modes, params * MB), F32),
            shape((samples, params * MB), F32),
            shape((samples, MB), BF16),
        ),
        in_specs=[VMEM] * 6,
        out_specs=(VMEM,) * 3,
        scratch_shapes=[pltpu.VMEM((params * MB, plane), BF16), pltpu.VMEM((2, tail, width_z), F32)],
        compiler_params=LIMIT,
        cost_estimate=pl.CostEstimate(flops=300_000_000, bytes_accessed=4_000_000, transcendentals=0),
        name="near_layer",
    )(flat, inner, acc, edge, center, targets)

    size = own * params
    half = devices // 2
    count = half * block
    keep, keep_rows, packet = pl.pallas_call(
        functools.partial(
            project_kernel,
            (params, layers, width_y, width_z, plane, samples, devices, own),
            tuple(int(value) for value in relative),
        ),
        out_shape=(
            shape((half * size, MB), F32),
            shape((count, MB), BF16),
            shape((2 * half * size + count, MB), BF16),
        ),
        in_specs=[VMEM] * 13,
        out_specs=(VMEM,) * 3,
        scratch_shapes=[
            pltpu.VMEM((params * MB, plane), BF16),
            pltpu.VMEM((2, tail, width_z), F32),
            pltpu.VMEM((params * modes, MB), F32),
        ],
        compiler_params=LIMIT,
        name="project",
    )(
        flat,
        outer[:MB].reshape(MB, plane),
        outer,
        acc,
        edge,
        got_in,
        got_side,
        center,
        near_sums,
        near_picks,
        near_side,
        targets,
        row_from,
    )

    wide = True
    for step in range(steps):
        got = lax.ppermute(packet, "cells", [(i, i ^ (1 << step)) for i in range(devices)])
        if step < steps - 1:
            next_wide = not 0 < step + 1 <= NARROW_STEPS
            half //= 2
            packet_rows = (2 if next_wide else 1) * half * size + count
            keep, keep_rows, packet = pl.pallas_call(
                functools.partial(merge_kernel, wide, next_wide),
                out_shape=(
                    shape((half * size, MB), F32),
                    shape((count, MB), BF16),
                    shape((packet_rows, MB), BF16),
                ),
                in_specs=[VMEM] * 4,
                out_specs=(VMEM,) * 3,
                compiler_params=LIMIT,
                name="merge",
            )(keep, keep_rows, got, shuffle)
            wide = next_wide
    volume = 1.0 / (layers * devices * width_y * width_z)
    summed, sampled = pl.pallas_call(
        functools.partial(final_kernel, wide, volume),
        out_shape=(shape((size, MB), F32), shape((2 * count, MB), BF16)),
        in_specs=[VMEM] * 4,
        out_specs=(VMEM,) * 2,
        compiler_params=LIMIT,
        name="finish",
    )(keep, keep_rows, got, final_from)
    galerkin = summed.reshape(own, params, MB)
    sampled = sampled.reshape(devices, rows, slots, MB)
    return (galerkin, jnp.transpose(sampled, (0, 2, 1, 3))[None])


def solution(mesh):
    return jax.shard_map(
        shards,
        mesh=mesh,
        in_specs=(
            P(None, ("groups", "cells"), None, None),
            P(None, None, ("groups", "cells"), None, None),
            P(None, None, ("groups", "cells"), None, None),
            P(None, None, ("groups", "cells"), None, None),
            P(None, ("groups", "cells"), None, None),
            P(("groups", "cells"), None, None),
            P(("groups", "cells"), None),
        ),
        out_specs=(
            P(("groups", "cells"), None, None),
            P(("groups", "cells"), None, None, None, None),
        ),
        check_vma=False,
    )
```

```python
import functools

import jax
import jax.numpy as jnp
import numpy as np
from jax import lax
from jax.experimental import pallas as pl
from jax.experimental.pallas import tpu as pltpu
from jax.sharding import PartitionSpec as P

MB = 128
SPLITS = 3
NARROW_STEPS = 3
BF16 = jnp.bfloat16
F32 = jnp.float32
I32 = jnp.int32
OFFSETS = 7
VMEM = pl.BlockSpec(memory_space=pltpu.VMEM)
ALONE = pltpu.CompilerParams(vmem_limit_bytes=60 * 1024 * 1024)
SMALL = pl.CostEstimate(flops=1, bytes_accessed=1, transcendentals=0)
LIMIT = pltpu.CompilerParams(vmem_limit_bytes=20 * 1024 * 1024)


def nt_dot(left, right):
    return lax.dot_general(left, right, (((1,), (1,)), ((), ())), preferred_element_type=F32)


def picked(targets, start, count):
    lanes = lax.broadcasted_iota(I32, (1, count), 1) + start
    return jnp.where(targets == lanes, 1.0, 0.0).astype(BF16)


def column(row):
    size = row.shape[1]
    down = lax.broadcasted_iota(I32, (size, size), 0)
    across = lax.broadcasted_iota(I32, (size, size), 1)
    spread = jnp.where(down == across, row.astype(F32), 0.0)
    return jnp.sum(spread, axis=1, keepdims=True).astype(I32)


def halves(value):
    head = value.astype(BF16)
    return head, (value - head.astype(F32)).astype(BF16)


def core():
    return lax.rem(lax.axis_index("cells"), 2)


def face_parts(speed, diff, flag):
    parts = []
    for value in (jnp.where(flag == 1, speed, -speed), diff):
        for _ in range(SPLITS):
            head = value.astype(BF16)
            value = value - head.astype(F32)
            parts.append(head)
    return parts


def pack_kernel(dims, basis_ref, speed_ref, diff_ref, flag_ref, inner_ref, outer_ref, speed_buf, diff_buf, flag_buf, sems):
    params, layers = dims
    last = layers - 1
    block = pl.ds(0, MB)
    outer = pltpu.make_async_copy(basis_ref.at[block, core() * last], outer_ref.at[block], sems.at[0])
    inner = pltpu.make_async_copy(basis_ref.at[block, (1 - core()) * last], inner_ref.at[block], sems.at[1])
    copies = [
        pltpu.make_async_copy(speed_ref.at[:, 0, last], speed_buf, sems.at[2]),
        pltpu.make_async_copy(diff_ref.at[:, 0, last], diff_buf, sems.at[3]),
        pltpu.make_async_copy(flag_ref.at[:, 0, last], flag_buf, sems.at[4]),
    ]
    for copy in copies + [outer, inner]:
        copy.start()
    for copy in copies:
        copy.wait()
    for at, part in enumerate(face_parts(speed_buf[...], diff_buf[...], flag_buf[...])):
        inner_ref[MB + at * params : MB + (at + 1) * params] = part
        outer_ref[MB + at * params : MB + (at + 1) * params] = part
    outer.wait()
    inner.wait()


def load_kernel(basis_ref, cell_ref, count_ref, after_ref, basis_out, cell_out, count_out, sems):
    del after_ref
    pairs = ((basis_ref, basis_out), (cell_ref, cell_out), (count_ref, count_out))
    copies = [pltpu.make_async_copy(source, out, sems.at[at]) for at, (source, out) in enumerate(pairs)]
    for copy in copies:
        copy.start()
    for copy in copies:
        copy.wait()


def local_kernel(
    dims,
    flat_ref,
    speed_ref,
    diff_ref,
    flag_ref,
    react_ref,
    sampled_ref,
    count_ref,
    acc_ref,
    edge_ref,
    in_ref,
    center_ref,
    cell_ref,
    coef_ref,
    pick_ref,
):
    params, layers, width_y, width_z, plane, samples = dims
    y_at = lax.broadcasted_iota(I32, (width_y, width_z), 0)
    z_at = lax.broadcasted_iota(I32, (width_y, width_z), 1)
    for param in range(params):
        uppers, nexts = [], []
        for layer in range(layers):
            up_d, next_d = [], []
            for axis_d in range(3):
                forward = flag_ref[param, axis_d, layer] == 1
                speed = speed_ref[param, axis_d, layer]
                diff = diff_ref[param, axis_d, layer]
                up_d.append(jnp.where(forward, speed, 0.0) + diff)
                next_d.append(jnp.where(forward, 0.0, -speed) - diff)
            uppers.append(up_d)
            nexts.append(next_d)
        edge_ref[param] = nexts[layers - 1][0]
        for layer in range(layers):
            diag = react_ref[param, layer]
            diag = diag + uppers[layer][0] + uppers[layer][1] + uppers[layer][2]
            if layer > 0:
                diag = diag - nexts[layer - 1][0]
                coef_ref[param, layer, 2] = -uppers[layer - 1][0]
            coef_ref[param, layer, 1] = nexts[layer][0]
            for axis_d, at, shift_axis, size in ((1, y_at, 0, width_y), (2, z_at, 1, width_z)):
                up, following = uppers[layer][axis_d], nexts[layer][axis_d]
                low_up = jnp.where(at == 0, 0.0, pltpu.roll(up, 1, shift_axis))
                low_next = jnp.where(at == 0, 0.0, pltpu.roll(following, 1, shift_axis))
                diag = diag - low_next
                coef_ref[param, layer, 1 + 2 * axis_d] = jnp.where(at == size - 1, 0.0, following)
                coef_ref[param, layer, 2 + 2 * axis_d] = -low_up
            coef_ref[param, layer, 0] = diag

    def tile(layer, y):
        start = layer * plane + y * width_z
        return flat_ref[:MB, start : start + width_z].astype(F32)

    for layer in range(layers):
        for y in range(width_y):
            start = layer * plane + y * width_z
            state = tile(layer, y)
            terms = [(0, state), (5, pltpu.roll(state, width_z - 1, 1)), (6, pltpu.roll(state, 1, 1))]
            if layer < layers - 1:
                terms.append((1, tile(layer + 1, y)))
            if layer > 0:
                terms.append((2, tile(layer - 1, y)))
            if y < width_y - 1:
                terms.append((3, tile(layer, y + 1)))
            if y > 0:
                terms.append((4, tile(layer, y - 1)))
            for param in range(params):
                total = None
                for at, term in terms:
                    product = coef_ref[param, layer, at, y : y + 1, :] * term
                    total = product if total is None else total + product
                acc_ref[param * MB : (param + 1) * MB, start : start + width_z] = total

    count = column(count_ref[...])
    slots = sampled_ref.shape[0]
    held = []
    for slot in range(slots):
        held.append(jnp.where(slot < count, column(sampled_ref[slot : slot + 1]), -4 * layers * plane))
    cell = jnp.concatenate(held, axis=0)
    cell_ref[...] = cell
    z_of = lax.broadcasted_iota(I32, (1, width_z), 1)
    for layer in range(layers):
        for y in range(width_y):
            start = layer * plane + y * width_z
            away = z_of - (cell - start)
            hits = [away == 0, away == -plane, away == plane]
            hits.append(away == -width_z if y < width_y - 1 else None)
            hits.append(away == width_z if y > 0 else None)
            hits.append((away == -1) & (z_of < width_z - 1))
            hits.append((away == 1) & (z_of > 0))
            for at, hit in enumerate(hits):
                value = jnp.zeros((samples, width_z), BF16)
                if hit is not None:
                    value = jnp.where(hit, 1.0, 0.0).astype(BF16)
                pick_ref[at * samples : (at + 1) * samples, start : start + width_z] = value
    center_ref[...] = pick_ref[:samples]
    in_ref[...] = nt_dot(pick_ref[...], flat_ref[:MB, :]).astype(BF16)


def finish_layer(dims, from_next, layer, halo_ref, flat_ref, acc_ref, edge_ref, applied_ref, coef_ref, spread_ref, beside_ref):
    params, layers, width_y, width_z, plane = dims
    faces = []
    for at in range(2 * SPLITS):
        part = halo_ref[MB + at * params : MB + (at + 1) * params].astype(F32)
        faces.append(part.reshape(params * width_y, width_z))
    signed = faces[0] + faces[1] + faces[2]
    diff = faces[3] + faces[4] + faces[5]
    edge = edge_ref[...].reshape(params * width_y, width_z)
    coef_ref[0] = jnp.where(from_next, edge, -(jnp.maximum(signed, 0.0) + diff))
    coef_ref[1] = jnp.where(from_next, 0.0, diff - jnp.minimum(signed, 0.0))
    spread_ref[...] = halo_ref[:MB].astype(F32).reshape(MB * width_y, width_z)
    for y in range(width_y):
        at = pl.multiple_of(layer * plane + y * width_z, width_z)
        lanes = slice(y * width_z, (y + 1) * width_z)
        state = flat_ref[:MB, pl.ds(at, width_z)].astype(F32)
        beside = spread_ref[pl.ds(y, MB, stride=width_y), :]
        beside_ref[:, lanes] = beside.astype(BF16)
        for param in range(params):
            modes = slice(param * MB, (param + 1) * MB)
            row = param * width_y + y
            total = acc_ref[modes, pl.ds(at, width_z)]
            total = total + coef_ref[1, row : row + 1, :] * state
            total = total + coef_ref[0, row : row + 1, :] * beside
            applied_ref[modes, lanes] = total.astype(BF16)


def near_kernel(dims, flat_ref, inner_ref, acc_ref, edge_ref, center_ref, cell_ref, sums_ref, picks_ref, side_ref, *scratch):
    params, layers, width_y, width_z, plane, samples = dims
    odd = core() == 1
    layer = (1 - core()) * (layers - 1)
    start = pl.multiple_of(layer * plane, plane)
    finish_layer(dims[:5], jnp.logical_not(odd), layer, inner_ref, flat_ref, acc_ref, edge_ref, *scratch)
    applied_ref, beside_ref = scratch[0], scratch[3]
    sums_ref[...] = nt_dot(flat_ref[:, pl.ds(start, plane)], applied_ref[...])
    picks_ref[...] = nt_dot(center_ref[:, pl.ds(start, plane)], applied_ref[...])
    below = cell_ref[...]
    above = below - (layers - 1) * plane
    side_ref[...] = nt_dot(picked(jnp.where(odd, below, above), 0, plane), beside_ref[...]).astype(BF16)


def project_kernel(
    dims,
    relative,
    flat_ref,
    outer_ref,
    acc_ref,
    edge_ref,
    in_ref,
    center_ref,
    near_sums_ref,
    near_picks_ref,
    near_side_ref,
    cell_ref,
    table_ref,
    keep_ref,
    keep_rows_ref,
    packet_ref,
    sums_ref,
    *scratch,
):
    params, layers, width_y, width_z, plane, samples, devices, own = dims
    odd = core() == 1
    layer = core() * (layers - 1)
    lane = pl.multiple_of(layer * plane, plane)
    finish_layer(dims[:5], odd, layer, outer_ref, flat_ref, acc_ref, edge_ref, *scratch)
    applied_ref, beside_ref = scratch[0], scratch[3]

    sums = near_sums_ref[...] + nt_dot(flat_ref[:, pl.ds(lane, plane)], applied_ref[...])
    for param in range(params):
        sums_ref[pl.ds(param, sums.shape[0], stride=params), :] = sums[:, param * MB : (param + 1) * MB]
    size = own * params
    half = devices // 2
    me = lax.axis_index("cells")
    for place in range(devices):
        start = pl.multiple_of((me ^ relative[place]) * size, size)
        terms = sums_ref[pl.ds(start, size), :]
        if place < half:
            keep_ref[place * size : (place + 1) * size] = terms
        else:
            head, rest = halves(terms)
            at = (place - half) * size
            packet_ref[at : at + size] = head
            packet_ref[half * size + at : half * size + at + size] = rest

    picks = nt_dot(center_ref[:, pl.ds(lane, plane)], applied_ref[...])
    got_applied = (near_picks_ref[...] + picks).astype(BF16)
    below = cell_ref[...]
    above = below - (layers - 1) * plane
    far = nt_dot(picked(jnp.where(odd, above, below), 0, plane), beside_ref[...]).astype(BF16)
    near = near_side_ref[...]
    got_below = in_ref[samples : 2 * samples] + jnp.where(odd, near, far)
    got_above = in_ref[2 * samples : 3 * samples] + jnp.where(odd, far, near)
    pieces = [got_applied[:, param * MB : (param + 1) * MB] for param in range(params)]
    pieces += [in_ref[:samples], got_below, got_above, in_ref[3 * samples :]]
    gathered = jnp.concatenate(pieces, axis=0)
    order = picked((table_ref[:, 1:2] ^ me) + table_ref[:, 2:3], 0, gathered.shape[0])
    ordered = jnp.dot(order, gathered, preferred_element_type=F32).astype(BF16)
    count = ordered.shape[0] // 2
    keep_rows_ref[...] = ordered[:count]
    packet_ref[2 * half * size :] = ordered[count:]


def merge_kernel(wide_in, wide_out, keep_ref, keep_rows_ref, got_ref, table_ref, keep_out, rows_out, packet_out):
    size = keep_ref.shape[0]
    half = size // 2
    total = keep_ref[...] + got_ref[:size].astype(F32)
    if wide_in:
        total = total + got_ref[size : 2 * size].astype(F32)
    keep_out[...] = total[:half]
    if wide_out:
        head, rest = halves(total[half:])
        packet_out[:half] = head
        packet_out[half : 2 * half] = rest
    else:
        packet_out[:half] = total[half:].astype(BF16)
    count = keep_rows_ref.shape[0]
    rows = jnp.concatenate([keep_rows_ref[...], got_ref[got_ref.shape[0] - count :]], axis=0)
    order = picked(table_ref[:, 0:1], 0, 2 * count)
    ordered = jnp.dot(order, rows, preferred_element_type=F32).astype(BF16)
    rows_out[...] = ordered[:count]
    packet_out[packet_out.shape[0] - count :] = ordered[count:]


def final_kernel(wide_in, volume, steps, block, keep_ref, keep_rows_ref, got_ref, table_ref, sum_out, rows_out):
    size = keep_ref.shape[0]
    total = keep_ref[...] + got_ref[:size].astype(F32)
    if wide_in:
        total = total + got_ref[size : 2 * size].astype(F32)
    sum_out[...] = volume * total
    count = keep_rows_ref.shape[0]
    rows = jnp.concatenate([keep_rows_ref[...], got_ref[got_ref.shape[0] - count :]], axis=0)
    me = lax.axis_index("cells")
    mine = (me >> (steps - 1)) << (steps - 1)
    for step in range(steps - 1):
        mine = mine + (((me >> step) & 1) << (steps - 2 - step))
    order = picked((table_ref[:, 3:4] ^ mine) * block + table_ref[:, 4:5], 0, 2 * count)
    rows_out[...] = jnp.dot(order, rows, preferred_element_type=F32).astype(BF16)


def shape(dims, dtype):
    return jax.ShapeDtypeStruct(dims, dtype)


def shards(basis, face_speed, face_diffusion, upwind_flag, reaction, sample_cell, sample_count):
    modes, layers, width_y, width_z = basis.shape
    params = face_speed.shape[0]
    devices = lax.axis_size("cells")
    slots = sample_cell.shape[2]
    plane = width_y * width_z
    cells = layers * plane
    own = modes // devices
    rows = params + OFFSETS
    samples = devices * slots
    steps = devices.bit_length() - 1

    tail = params * width_y
    hbm = pl.BlockSpec(memory_space=pltpu.HBM)
    planes = 2 * SPLITS * params
    packed = shape((MB + planes, width_y, width_z), BF16)
    to_inner, to_outer = pl.pallas_call(
        functools.partial(pack_kernel, (params, layers)),
        out_shape=(packed, packed),
        in_specs=[hbm] * 4,
        out_specs=(VMEM, VMEM),
        scratch_shapes=[
            pltpu.VMEM((params, width_y, width_z), F32),
            pltpu.VMEM((params, width_y, width_z), F32),
            pltpu.VMEM((params, width_y, width_z), I32),
            pltpu.SemaphoreType.DMA((5,)),
        ],
        compiler_params=ALONE,
        name="pack_halo",
    )(basis, face_speed, face_diffusion, upwind_flag)
    inner_pairs = [(i, i ^ 1) for i in range(devices)]
    outer_pairs = []
    for i in range(1, devices - 1, 2):
        outer_pairs += [(i, i + 1), (i + 1, i)]
    inner = lax.ppermute(to_inner, "cells", inner_pairs)
    outer = lax.ppermute(to_outer, "cells", outer_pairs)

    loaded, cells_in, counts_in = pl.pallas_call(
        load_kernel,
        out_shape=(shape(basis.shape, BF16), shape((slots, devices), I32), shape((1, devices), I32)),
        in_specs=[hbm] * 3 + [VMEM],
        out_specs=(VMEM,) * 3,
        scratch_shapes=[pltpu.SemaphoreType.DMA((3,))],
        compiler_params=LIMIT,
        name="load",
    )(basis, sample_cell[0].T, sample_count, to_outer)
    flat = loaded.reshape(modes, cells)

    block = slots * rows
    relative = [sum(((place >> (steps - 1 - step)) & 1) << step for step in range(steps)) for place in range(devices)]
    block = slots * rows
    table = np.zeros((devices, block, 8), np.int32)
    in_block = np.arange(block)
    for place in range(devices):
        turned = ((place & 1) << (steps - 1)) + (place >> 1)
        table[place, :, 0] = turned * block + in_block
        table[place, :, 1] = relative[place]
        table[place, :, 2] = (in_block // slots) * samples + (in_block % slots) * devices
        table[relative[place], :, 3] = turned
        table[place, :, 4] = in_block
    table = jnp.asarray(table.reshape(devices * block, 8))

    acc, edge, got_in, center, cell = pl.pallas_call(
        functools.partial(local_kernel, (params, layers, width_y, width_z, plane, samples)),
        out_shape=(
            shape((params * MB, cells), F32),
            shape((params, width_y, width_z), F32),
            shape((OFFSETS * samples, MB), BF16),
            shape((samples, cells), BF16),
            shape((samples, 1), I32),
        ),
        in_specs=[VMEM] * 7,
        out_specs=(VMEM,) * 5,
        scratch_shapes=[
            pltpu.VMEM((params, layers, OFFSETS, width_y, width_z), F32),
            pltpu.VMEM((OFFSETS * samples, cells), BF16),
        ],
        compiler_params=LIMIT,
        cost_estimate=SMALL,
        name="local_stencil",
    )(flat, face_speed, face_diffusion, upwind_flag, reaction, cells_in, counts_in)

    finish_scratch = [
        pltpu.VMEM((params * MB, plane), BF16),
        pltpu.VMEM((2, tail, width_z), F32),
        pltpu.VMEM((MB * width_y, width_z), F32),
        pltpu.VMEM((MB, plane), BF16),
    ]
    near_sums, near_picks, near_side = pl.pallas_call(
        functools.partial(near_kernel, (params, layers, width_y, width_z, plane, samples)),
        out_shape=(
            shape((modes, params * MB), F32),
            shape((samples, params * MB), F32),
            shape((samples, MB), BF16),
        ),
        in_specs=[VMEM] * 6,
        out_specs=(VMEM,) * 3,
        scratch_shapes=finish_scratch,
        compiler_params=LIMIT,
        cost_estimate=SMALL,
        name="near_layer",
    )(flat, inner, acc, edge, center, cell)

    size = own * params
    half = devices // 2
    count = half * block
    keep, keep_rows, packet = pl.pallas_call(
        functools.partial(
            project_kernel,
            (params, layers, width_y, width_z, plane, samples, devices, own),
            relative,
        ),
        out_shape=(
            shape((half * size, MB), F32),
            shape((count, MB), BF16),
            shape((2 * half * size + count, MB), BF16),
        ),
        in_specs=[VMEM] * 11,
        out_specs=(VMEM,) * 3,
        scratch_shapes=[pltpu.VMEM((params * modes, MB), F32)] + finish_scratch,
        compiler_params=LIMIT,
        name="project",
    )(
        flat,
        outer,
        acc,
        edge,
        got_in,
        center,
        near_sums,
        near_picks,
        near_side,
        cell,
        table,
    )

    wide = True
    for step in range(steps):
        got = lax.ppermute(packet, "cells", [(i, i ^ (1 << step)) for i in range(devices)])
        if step < steps - 1:
            next_wide = not 0 < step + 1 <= NARROW_STEPS
            half //= 2
            packet_rows = (2 if next_wide else 1) * half * size + count
            keep, keep_rows, packet = pl.pallas_call(
                functools.partial(merge_kernel, wide, next_wide),
                out_shape=(
                    shape((half * size, MB), F32),
                    shape((count, MB), BF16),
                    shape((packet_rows, MB), BF16),
                ),
                in_specs=[VMEM] * 4,
                out_specs=(VMEM,) * 3,
                compiler_params=LIMIT,
                name="merge",
            )(keep, keep_rows, got, table)
            wide = next_wide
    volume = 1.0 / (layers * devices * width_y * width_z)
    summed, sampled = pl.pallas_call(
        functools.partial(final_kernel, wide, volume, steps, block),
        out_shape=(shape((size, MB), F32), shape((2 * count, MB), BF16)),
        in_specs=[VMEM] * 4,
        out_specs=(VMEM,) * 2,
        compiler_params=LIMIT,
        name="finish",
    )(keep, keep_rows, got, table)
    galerkin = summed.reshape(own, params, MB)
    sampled = sampled.reshape(devices, rows, slots, MB)
    return (galerkin, jnp.transpose(sampled, (0, 2, 1, 3))[None])


def solution(mesh):
    return jax.shard_map(
        shards,
        mesh=mesh,
        in_specs=(
            P(None, ("groups", "cells"), None, None),
            P(None, None, ("groups", "cells"), None, None),
            P(None, None, ("groups", "cells"), None, None),
            P(None, None, ("groups", "cells"), None, None),
            P(None, ("groups", "cells"), None, None),
            P(("groups", "cells"), None, None),
            P(("groups", "cells"), None),
        ),
        out_specs=(
            P(("groups", "cells"), None, None),
            P(("groups", "cells"), None, None, None, None),
        ),
        check_vma=False,
    )
```

```python
import functools

import jax
import jax.numpy as jnp
import numpy as np
from jax import lax
from jax.experimental import pallas as pl
from jax.experimental.pallas import tpu as pltpu
from jax.sharding import PartitionSpec as P

MB = 128
SPLITS = 3
NARROW_STEPS = 1
DIRECT = 4
ORDER = (3, 2, 1)
BF16 = jnp.bfloat16
F32 = jnp.float32
I32 = jnp.int32
OFFSETS = 7
VMEM = pl.BlockSpec(memory_space=pltpu.VMEM)
ALONE = pltpu.CompilerParams(vmem_limit_bytes=60 * 1024 * 1024)
SMALL = pl.CostEstimate(flops=1, bytes_accessed=1, transcendentals=0)
LIMIT = pltpu.CompilerParams(vmem_limit_bytes=20 * 1024 * 1024)


def nt_dot(left, right):
    return lax.dot_general(left, right, (((1,), (1,)), ((), ())), preferred_element_type=F32)


def picked(targets, start, count):
    lanes = lax.broadcasted_iota(I32, (1, count), 1) + start
    return jnp.where(targets == lanes, 1.0, 0.0).astype(BF16)


def column(row):
    size = row.shape[1]
    down = lax.broadcasted_iota(I32, (size, size), 0)
    across = lax.broadcasted_iota(I32, (size, size), 1)
    spread = jnp.where(down == across, row.astype(F32), 0.0)
    return jnp.sum(spread, axis=1, keepdims=True).astype(I32)


def round_up(value, multiple):
    return -(-value // multiple) * multiple


def halves(value):
    head = value.astype(BF16)
    return head, (value - head.astype(F32)).astype(BF16)


def core():
    return lax.rem(lax.axis_index("cells"), 2)


def face_parts(speed, diff, flag):
    parts = []
    for value in (jnp.where(flag == 1, speed, -speed), diff):
        for _ in range(SPLITS):
            head = value.astype(BF16)
            value = value - head.astype(F32)
            parts.append(head)
    return parts


def pack_kernel(dims, basis_ref, speed_ref, diff_ref, flag_ref, inner_ref, outer_ref, speed_buf, diff_buf, flag_buf, sems):
    params, layers = dims
    last = layers - 1
    block = pl.ds(0, MB)
    outer = pltpu.make_async_copy(basis_ref.at[block, core() * last], outer_ref.at[block], sems.at[0])
    inner = pltpu.make_async_copy(basis_ref.at[block, (1 - core()) * last], inner_ref.at[block], sems.at[1])
    copies = [
        pltpu.make_async_copy(speed_ref.at[:, 0, last], speed_buf, sems.at[2]),
        pltpu.make_async_copy(diff_ref.at[:, 0, last], diff_buf, sems.at[3]),
        pltpu.make_async_copy(flag_ref.at[:, 0, last], flag_buf, sems.at[4]),
    ]
    for copy in copies + [outer, inner]:
        copy.start()
    for copy in copies:
        copy.wait()
    for at, part in enumerate(face_parts(speed_buf[...], diff_buf[...], flag_buf[...])):
        inner_ref[MB + at * params : MB + (at + 1) * params] = part
        outer_ref[MB + at * params : MB + (at + 1) * params] = part
    outer.wait()
    inner.wait()


def load_kernel(basis_ref, cell_ref, count_ref, after_ref, basis_out, cell_out, count_out, sems):
    del after_ref
    pairs = ((basis_ref, basis_out), (cell_ref, cell_out), (count_ref, count_out))
    copies = [pltpu.make_async_copy(source, out, sems.at[at]) for at, (source, out) in enumerate(pairs)]
    for copy in copies:
        copy.start()
    for copy in copies:
        copy.wait()


def local_kernel(
    dims,
    flat_ref,
    speed_ref,
    diff_ref,
    flag_ref,
    react_ref,
    sampled_ref,
    count_ref,
    acc_ref,
    edge_ref,
    in_ref,
    center_ref,
    cell_ref,
    coef_ref,
    pick_ref,
):
    params, layers, width_y, width_z, plane, samples = dims
    y_at = lax.broadcasted_iota(I32, (width_y, width_z), 0)
    z_at = lax.broadcasted_iota(I32, (width_y, width_z), 1)
    for param in range(params):
        uppers, nexts = [], []
        for layer in range(layers):
            up_d, next_d = [], []
            for axis_d in range(3):
                forward = flag_ref[param, axis_d, layer] == 1
                speed = speed_ref[param, axis_d, layer]
                diff = diff_ref[param, axis_d, layer]
                up_d.append(jnp.where(forward, speed, 0.0) + diff)
                next_d.append(jnp.where(forward, 0.0, -speed) - diff)
            uppers.append(up_d)
            nexts.append(next_d)
        edge_ref[param] = nexts[layers - 1][0]
        for layer in range(layers):
            diag = react_ref[param, layer]
            diag = diag + uppers[layer][0] + uppers[layer][1] + uppers[layer][2]
            if layer > 0:
                diag = diag - nexts[layer - 1][0]
                coef_ref[param, layer, 2] = -uppers[layer - 1][0]
            coef_ref[param, layer, 1] = nexts[layer][0]
            for axis_d, at, shift_axis, size in ((1, y_at, 0, width_y), (2, z_at, 1, width_z)):
                up, following = uppers[layer][axis_d], nexts[layer][axis_d]
                low_up = jnp.where(at == 0, 0.0, pltpu.roll(up, 1, shift_axis))
                low_next = jnp.where(at == 0, 0.0, pltpu.roll(following, 1, shift_axis))
                diag = diag - low_next
                coef_ref[param, layer, 1 + 2 * axis_d] = jnp.where(at == size - 1, 0.0, following)
                coef_ref[param, layer, 2 + 2 * axis_d] = -low_up
            coef_ref[param, layer, 0] = diag

    def tile(layer, y):
        start = layer * plane + y * width_z
        return flat_ref[:MB, start : start + width_z].astype(F32)

    for layer in range(layers):
        for y in range(width_y):
            start = layer * plane + y * width_z
            state = tile(layer, y)
            terms = [(0, state), (5, pltpu.roll(state, width_z - 1, 1)), (6, pltpu.roll(state, 1, 1))]
            if layer < layers - 1:
                terms.append((1, tile(layer + 1, y)))
            if layer > 0:
                terms.append((2, tile(layer - 1, y)))
            if y < width_y - 1:
                terms.append((3, tile(layer, y + 1)))
            if y > 0:
                terms.append((4, tile(layer, y - 1)))
            for param in range(params):
                total = None
                for at, term in terms:
                    product = coef_ref[param, layer, at, y : y + 1, :] * term
                    total = product if total is None else total + product
                acc_ref[param * MB : (param + 1) * MB, start : start + width_z] = total

    count = column(count_ref[...])
    slots = sampled_ref.shape[0]
    held = []
    for slot in range(slots):
        held.append(jnp.where(slot < count, column(sampled_ref[slot : slot + 1]), -4 * layers * plane))
    cell = jnp.concatenate(held, axis=0)
    cell_ref[...] = cell
    z_of = lax.broadcasted_iota(I32, (1, width_z), 1)
    for layer in range(layers):
        for y in range(width_y):
            start = layer * plane + y * width_z
            away = z_of - (cell - start)
            hits = [away == 0, away == -plane, away == plane]
            hits.append(away == -width_z if y < width_y - 1 else None)
            hits.append(away == width_z if y > 0 else None)
            hits.append((away == -1) & (z_of < width_z - 1))
            hits.append((away == 1) & (z_of > 0))
            for at, hit in enumerate(hits):
                value = jnp.zeros((samples, width_z), BF16)
                if hit is not None:
                    value = jnp.where(hit, 1.0, 0.0).astype(BF16)
                pick_ref[at * samples : (at + 1) * samples, start : start + width_z] = value
    center_ref[...] = pick_ref[:samples]
    in_ref[...] = nt_dot(pick_ref[...], flat_ref[:MB, :]).astype(BF16)


def finish_layer(dims, from_next, layer, halo_ref, flat_ref, acc_ref, edge_ref, applied_ref, coef_ref, spread_ref, beside_ref):
    params, layers, width_y, width_z, plane = dims
    faces = []
    for at in range(2 * SPLITS):
        part = halo_ref[MB + at * params : MB + (at + 1) * params].astype(F32)
        faces.append(part.reshape(params * width_y, width_z))
    signed = faces[0] + faces[1] + faces[2]
    diff = faces[3] + faces[4] + faces[5]
    edge = edge_ref[...].reshape(params * width_y, width_z)
    coef_ref[0] = jnp.where(from_next, edge, -(jnp.maximum(signed, 0.0) + diff))
    coef_ref[1] = jnp.where(from_next, 0.0, diff - jnp.minimum(signed, 0.0))
    spread_ref[...] = halo_ref[:MB].astype(F32).reshape(MB * width_y, width_z)
    for y in range(width_y):
        at = pl.multiple_of(layer * plane + y * width_z, width_z)
        lanes = slice(y * width_z, (y + 1) * width_z)
        state = flat_ref[:MB, pl.ds(at, width_z)].astype(F32)
        beside = spread_ref[pl.ds(y, MB, stride=width_y), :]
        beside_ref[:, lanes] = beside.astype(BF16)
        for param in range(params):
            modes = slice(param * MB, (param + 1) * MB)
            row = param * width_y + y
            total = acc_ref[modes, pl.ds(at, width_z)]
            total = total + coef_ref[1, row : row + 1, :] * state
            total = total + coef_ref[0, row : row + 1, :] * beside
            applied_ref[modes, lanes] = total.astype(BF16)


def near_kernel(dims, flat_ref, inner_ref, acc_ref, edge_ref, center_ref, cell_ref, sums_ref, picks_ref, side_ref, *scratch):
    params, layers, width_y, width_z, plane, samples = dims
    odd = core() == 1
    layer = (1 - core()) * (layers - 1)
    start = pl.multiple_of(layer * plane, plane)
    finish_layer(dims[:5], jnp.logical_not(odd), layer, inner_ref, flat_ref, acc_ref, edge_ref, *scratch)
    applied_ref, beside_ref = scratch[0], scratch[3]
    sums_ref[...] = nt_dot(flat_ref[:, pl.ds(start, plane)], applied_ref[...])
    picks_ref[...] = nt_dot(center_ref[:, pl.ds(start, plane)], applied_ref[...])
    below = cell_ref[...]
    above = below - (layers - 1) * plane
    side_ref[...] = nt_dot(picked(jnp.where(odd, below, above), 0, plane), beside_ref[...]).astype(BF16)


def project_kernel(
    dims,
    relative,
    flat_ref,
    outer_ref,
    acc_ref,
    edge_ref,
    in_ref,
    center_ref,
    near_sums_ref,
    near_picks_ref,
    near_side_ref,
    cell_ref,
    table_ref,
    keep_ref,
    keep_rows_ref,
    packet_ref,
    sums_ref,
    *scratch,
):
    params, layers, width_y, width_z, plane, samples, devices, own = dims
    odd = core() == 1
    layer = core() * (layers - 1)
    lane = pl.multiple_of(layer * plane, plane)
    finish_layer(dims[:5], odd, layer, outer_ref, flat_ref, acc_ref, edge_ref, *scratch)
    applied_ref, beside_ref = scratch[0], scratch[3]

    sums = near_sums_ref[...] + nt_dot(flat_ref[:, pl.ds(lane, plane)], applied_ref[...])
    for param in range(params):
        sums_ref[pl.ds(param, sums.shape[0], stride=params), :] = sums[:, param * MB : (param + 1) * MB]
    size = own * params
    half = devices // 2
    me = lax.axis_index("cells")
    for place in range(devices):
        start = pl.multiple_of((me ^ relative[place]) * size, size)
        terms = sums_ref[pl.ds(start, size), :]
        if place < half:
            keep_ref[place * size : (place + 1) * size] = terms
        else:
            head, rest = halves(terms)
            at = (place - half) * size
            packet_ref[at : at + size] = head
            packet_ref[half * size + at : half * size + at + size] = rest

    picks = nt_dot(center_ref[:, pl.ds(lane, plane)], applied_ref[...])
    got_applied = (near_picks_ref[...] + picks).astype(BF16)
    below = cell_ref[...]
    above = below - (layers - 1) * plane
    far = nt_dot(picked(jnp.where(odd, above, below), 0, plane), beside_ref[...]).astype(BF16)
    near = near_side_ref[...]
    got_below = in_ref[samples : 2 * samples] + jnp.where(odd, near, far)
    got_above = in_ref[2 * samples : 3 * samples] + jnp.where(odd, far, near)
    pieces = [got_applied[:, param * MB : (param + 1) * MB] for param in range(params)]
    pieces += [in_ref[:samples], got_below, got_above, in_ref[3 * samples :]]
    gathered = jnp.concatenate(pieces, axis=0)
    total_rows = gathered.shape[0]
    order = picked((table_ref[:total_rows, 1:2] ^ me) + table_ref[:total_rows, 2:3], 0, gathered.shape[0])
    ordered = jnp.dot(order, gathered, preferred_element_type=F32).astype(BF16)
    count = ordered.shape[0] // 2
    keep_rows_ref[...] = ordered[:count]
    packet_ref[2 * half * size :] = ordered[count:]


def merge_kernel(wide_in, wide_out, keep_ref, keep_rows_ref, got_ref, table_ref, keep_out, rows_out, packet_out):
    size = keep_ref.shape[0]
    half = size // 2
    total = keep_ref[...] + got_ref[:size].astype(F32)
    if wide_in:
        total = total + got_ref[size : 2 * size].astype(F32)
    keep_out[...] = total[:half]
    if wide_out:
        head, rest = halves(total[half:])
        packet_out[:half] = head
        packet_out[half : 2 * half] = rest
    else:
        packet_out[:half] = total[half:].astype(BF16)
    count = keep_rows_ref.shape[0]
    rows = jnp.concatenate([keep_rows_ref[...], got_ref[got_ref.shape[0] - count :]], axis=0)
    order = picked(table_ref[: 2 * count, 0:1], 0, 2 * count)
    ordered = jnp.dot(order, rows, preferred_element_type=F32).astype(BF16)
    rows_out[...] = ordered[:count]
    packet_out[packet_out.shape[0] - count :] = ordered[count:]


def spread_kernel(wide_in, room, keep_ref, keep_rows_ref, got_ref, table_ref, keep_out, rows_out, *packets_out):
    size = keep_ref.shape[0]
    total = keep_ref[...] + got_ref[:size].astype(F32)
    if wide_in:
        total = total + got_ref[size : 2 * size].astype(F32)
    part = size // DIRECT
    count = keep_rows_ref.shape[0]
    rows = jnp.concatenate([keep_rows_ref[...], got_ref[got_ref.shape[0] - count :]], axis=0)
    order = picked(table_ref[: DIRECT * room, 5:6], 0, 2 * count)
    ordered = jnp.dot(order, rows, preferred_element_type=F32).astype(BF16)
    keep_out[...] = total[:part]
    rows_out[...] = ordered[:room]
    for at, packet_out in enumerate(packets_out, 1):
        packet_out[:part] = total[at * part : (at + 1) * part].astype(BF16)
        packet_out[part:] = ordered[at * room : (at + 1) * room]


def final_kernel(volume, steps, block, keep_ref, keep_rows_ref, *refs):
    got_refs, table_ref, sum_out, rows_out = refs[: DIRECT - 1], refs[-3], refs[-2], refs[-1]
    size = keep_ref.shape[0]
    room = keep_rows_ref.shape[0]
    total = keep_ref[...]
    rows = [keep_rows_ref[...]] + [None] * (DIRECT - 1)
    for at, got_ref in zip(ORDER, got_refs):
        total = total + got_ref[:size].astype(F32)
        rows[at] = got_ref[size:]
    sum_out[...] = volume * total
    me = lax.axis_index("cells")
    mine = 0
    for step, place in enumerate(places(steps)):
        mine = mine + (((me >> step) & 1) << place)
    came = table_ref[: rows_out.shape[0], 3:4] ^ mine
    low = steps - 2
    start = (came >> low) * room + (came & ((1 << low) - 1)) * block
    order = picked(start + table_ref[: rows_out.shape[0], 4:5], 0, DIRECT * room)
    rows_out[...] = jnp.dot(order, jnp.concatenate(rows, axis=0), preferred_element_type=F32).astype(BF16)


def places(steps):
    return [steps - 3 - step for step in range(steps - 2)] + [steps - 1, steps - 2]


def shape(dims, dtype):
    return jax.ShapeDtypeStruct(dims, dtype)


def shards(basis, face_speed, face_diffusion, upwind_flag, reaction, sample_cell, sample_count):
    modes, layers, width_y, width_z = basis.shape
    params = face_speed.shape[0]
    devices = lax.axis_size("cells")
    slots = sample_cell.shape[2]
    plane = width_y * width_z
    cells = layers * plane
    own = modes // devices
    rows = params + OFFSETS
    samples = devices * slots
    steps = devices.bit_length() - 1

    tail = params * width_y
    hbm = pl.BlockSpec(memory_space=pltpu.HBM)
    planes = 2 * SPLITS * params
    packed = shape((MB + planes, width_y, width_z), BF16)
    to_inner, to_outer = pl.pallas_call(
        functools.partial(pack_kernel, (params, layers)),
        out_shape=(packed, packed),
        in_specs=[hbm] * 4,
        out_specs=(VMEM, VMEM),
        scratch_shapes=[
            pltpu.VMEM((params, width_y, width_z), F32),
            pltpu.VMEM((params, width_y, width_z), F32),
            pltpu.VMEM((params, width_y, width_z), I32),
            pltpu.SemaphoreType.DMA((5,)),
        ],
        compiler_params=ALONE,
        name="pack_halo",
    )(basis, face_speed, face_diffusion, upwind_flag)
    inner_pairs = [(i, i ^ 1) for i in range(devices)]
    outer_pairs = []
    for i in range(1, devices - 1, 2):
        outer_pairs += [(i, i + 1), (i + 1, i)]
    inner = lax.ppermute(to_inner, "cells", inner_pairs)
    outer = lax.ppermute(to_outer, "cells", outer_pairs)

    loaded, cells_in, counts_in = pl.pallas_call(
        load_kernel,
        out_shape=(shape(basis.shape, BF16), shape((slots, devices), I32), shape((1, devices), I32)),
        in_specs=[hbm] * 3 + [VMEM],
        out_specs=(VMEM,) * 3,
        scratch_shapes=[pltpu.SemaphoreType.DMA((3,))],
        compiler_params=LIMIT,
        name="load",
    )(basis, sample_cell[0].T, sample_count, to_outer)
    flat = loaded.reshape(modes, cells)

    block = slots * rows
    relative = [sum(((place >> (steps - 1 - step)) & 1) << step for step in range(steps)) for place in range(devices)]
    block = slots * rows
    share = devices // DIRECT * block
    room = round_up(share, 16)
    table = np.full((DIRECT * room, 8), -1, np.int32)
    in_block = np.arange(block)
    for place in range(devices):
        turned = (((place & 1) << (steps - 1)) + (place >> 1)) * block + in_block
        at = slice(place * block, (place + 1) * block)
        table[at, 0] = turned
        table[at, 1] = relative[place]
        table[at, 2] = (in_block // slots) * samples + (in_block % slots) * devices
        table[at, 3] = sum(((place >> step) & 1) << to for step, to in enumerate(places(steps)))
        table[at, 4] = in_block
        start = place * block // share * room + place * block % share
        table[start : start + block, 5] = turned
    table = jnp.asarray(table)

    acc, edge, got_in, center, cell = pl.pallas_call(
        functools.partial(local_kernel, (params, layers, width_y, width_z, plane, samples)),
        out_shape=(
            shape((params * MB, cells), F32),
            shape((params, width_y, width_z), F32),
            shape((OFFSETS * samples, MB), BF16),
            shape((samples, cells), BF16),
            shape((samples, 1), I32),
        ),
        in_specs=[VMEM] * 7,
        out_specs=(VMEM,) * 5,
        scratch_shapes=[
            pltpu.VMEM((params, layers, OFFSETS, width_y, width_z), F32),
            pltpu.VMEM((OFFSETS * samples, cells), BF16),
        ],
        compiler_params=LIMIT,
        cost_estimate=SMALL,
        name="local_stencil",
    )(flat, face_speed, face_diffusion, upwind_flag, reaction, cells_in, counts_in)

    finish_scratch = [
        pltpu.VMEM((params * MB, plane), BF16),
        pltpu.VMEM((2, tail, width_z), F32),
        pltpu.VMEM((MB * width_y, width_z), F32),
        pltpu.VMEM((MB, plane), BF16),
    ]
    near_sums, near_picks, near_side = pl.pallas_call(
        functools.partial(near_kernel, (params, layers, width_y, width_z, plane, samples)),
        out_shape=(
            shape((modes, params * MB), F32),
            shape((samples, params * MB), F32),
            shape((samples, MB), BF16),
        ),
        in_specs=[VMEM] * 6,
        out_specs=(VMEM,) * 3,
        scratch_shapes=finish_scratch,
        compiler_params=LIMIT,
        cost_estimate=SMALL,
        name="near_layer",
    )(flat, inner, acc, edge, center, cell)

    size = own * params
    half = devices // 2
    count = half * block
    keep, keep_rows, packet = pl.pallas_call(
        functools.partial(
            project_kernel,
            (params, layers, width_y, width_z, plane, samples, devices, own),
            relative,
        ),
        out_shape=(
            shape((half * size, MB), F32),
            shape((count, MB), BF16),
            shape((2 * half * size + count, MB), BF16),
        ),
        in_specs=[VMEM] * 11,
        out_specs=(VMEM,) * 3,
        scratch_shapes=[pltpu.VMEM((params * modes, MB), F32)] + finish_scratch,
        compiler_params=LIMIT,
        name="project",
    )(
        flat,
        outer,
        acc,
        edge,
        got_in,
        center,
        near_sums,
        near_picks,
        near_side,
        cell,
        table,
    )

    wide = True
    for step in range(steps - 2):
        got = lax.ppermute(packet, "cells", [(i, i ^ (1 << step)) for i in range(devices)])
        if step < steps - 3:
            next_wide = step + 1 > NARROW_STEPS
            half //= 2
            packet_rows = (2 if next_wide else 1) * half * size + count
            keep, keep_rows, packet = pl.pallas_call(
                functools.partial(merge_kernel, wide, next_wide),
                out_shape=(
                    shape((half * size, MB), F32),
                    shape((count, MB), BF16),
                    shape((packet_rows, MB), BF16),
                ),
                in_specs=[VMEM] * 4,
                out_specs=(VMEM,) * 3,
                compiler_params=LIMIT,
                name="merge",
            )(keep, keep_rows, got, table)
            wide = next_wide
    sent = shape((size + room, MB), BF16)
    keep, keep_rows, *packets = pl.pallas_call(
        functools.partial(spread_kernel, wide, room),
        out_shape=(shape((size, MB), F32), shape((room, MB), BF16)) + (sent,) * (DIRECT - 1),
        in_specs=[VMEM] * 4,
        out_specs=(VMEM,) * (DIRECT + 1),
        compiler_params=LIMIT,
        name="spread",
    )(keep, keep_rows, got, table)
    got = [None] * DIRECT
    for at in ORDER:
        mask = ((at >> 1) << (steps - 2)) | ((at & 1) << (steps - 1))
        got[at] = lax.ppermute(packets[at - 1], "cells", [(i, i ^ mask) for i in range(devices)])
    volume = 1.0 / (layers * devices * width_y * width_z)
    summed, sampled = pl.pallas_call(
        functools.partial(final_kernel, volume, steps, block),
        out_shape=(shape((size, MB), F32), shape((2 * count, MB), BF16)),
        in_specs=[VMEM] * (DIRECT + 2),
        out_specs=(VMEM,) * 2,
        compiler_params=LIMIT,
        name="finish",
    )(keep, keep_rows, *[got[at] for at in ORDER], table)
    galerkin = summed.reshape(own, params, MB)
    sampled = sampled.reshape(devices, rows, slots, MB)
    return (galerkin, jnp.transpose(sampled, (0, 2, 1, 3))[None])


def solution(mesh):
    return jax.shard_map(
        shards,
        mesh=mesh,
        in_specs=(
            P(None, ("groups", "cells"), None, None),
            P(None, None, ("groups", "cells"), None, None),
            P(None, None, ("groups", "cells"), None, None),
            P(None, None, ("groups", "cells"), None, None),
            P(None, ("groups", "cells"), None, None),
            P(("groups", "cells"), None, None),
            P(("groups", "cells"), None),
        ),
        out_specs=(
            P(("groups", "cells"), None, None),
            P(("groups", "cells"), None, None, None, None),
        ),
        check_vma=False,
    )
```

```python
import functools

import jax
import jax.numpy as jnp
import numpy as np
from jax import lax
from jax.experimental import pallas as pl
from jax.experimental.pallas import tpu as pltpu
from jax.sharding import PartitionSpec as P

MB = 128
SPLITS = 3
NARROW_STEPS = 1
DIRECT = 4
ORDER = (3, 2, 1)
BF16 = jnp.bfloat16
F32 = jnp.float32
I32 = jnp.int32
OFFSETS = 7
VMEM = pl.BlockSpec(memory_space=pltpu.VMEM)
SMALL = pl.CostEstimate(flops=1, bytes_accessed=1, transcendentals=0)
LIMIT = pltpu.CompilerParams(vmem_limit_bytes=20 * 1024 * 1024)


def nt_dot(left, right):
    return lax.dot_general(left, right, (((1,), (1,)), ((), ())), preferred_element_type=F32)


def picked(targets, start, count):
    lanes = lax.broadcasted_iota(I32, (1, count), 1) + start
    return jnp.where(targets == lanes, 1.0, 0.0).astype(BF16)


def column(row):
    size = row.shape[1]
    down = lax.broadcasted_iota(I32, (size, size), 0)
    across = lax.broadcasted_iota(I32, (size, size), 1)
    spread = jnp.where(down == across, row.astype(F32), 0.0)
    return jnp.sum(spread, axis=1, keepdims=True).astype(I32)


def round_up(value, multiple):
    return -(-value // multiple) * multiple


def halves(value):
    head = value.astype(BF16)
    return head, (value - head.astype(F32)).astype(BF16)


def core():
    return lax.rem(lax.axis_index("cells"), 2)


def face_parts(speed, diff, flag):
    parts = []
    for value in (jnp.where(flag == 1, speed, -speed), diff):
        for _ in range(SPLITS):
            head = value.astype(BF16)
            value = value - head.astype(F32)
            parts.append(head)
    return parts


def pack_kernel(dims, basis_ref, speed_ref, diff_ref, flag_ref, inner_ref, outer_ref, speed_buf, diff_buf, flag_buf, sems):
    params, layers = dims
    last = layers - 1
    block = pl.ds(0, MB)
    outer = pltpu.make_async_copy(basis_ref.at[block, core() * last], outer_ref.at[block], sems.at[0])
    inner = pltpu.make_async_copy(basis_ref.at[block, (1 - core()) * last], inner_ref.at[block], sems.at[1])
    copies = [
        pltpu.make_async_copy(speed_ref.at[:, 0, last], speed_buf, sems.at[2]),
        pltpu.make_async_copy(diff_ref.at[:, 0, last], diff_buf, sems.at[3]),
        pltpu.make_async_copy(flag_ref.at[:, 0, last], flag_buf, sems.at[4]),
    ]
    for copy in copies + [outer, inner]:
        copy.start()
    for copy in copies:
        copy.wait()
    for at, part in enumerate(face_parts(speed_buf[...], diff_buf[...], flag_buf[...])):
        inner_ref[MB + at * params : MB + (at + 1) * params] = part
        outer_ref[MB + at * params : MB + (at + 1) * params] = part
    outer.wait()
    inner.wait()


def load_kernel(basis_ref, cell_ref, count_ref, after_ref, basis_out, cell_out, count_out, sems):
    del after_ref
    pairs = ((basis_ref, basis_out), (cell_ref, cell_out), (count_ref, count_out))
    copies = [pltpu.make_async_copy(source, out, sems.at[at]) for at, (source, out) in enumerate(pairs)]
    for copy in copies:
        copy.start()
    for copy in copies:
        copy.wait()


def local_kernel(
    dims,
    flat_ref,
    speed_ref,
    diff_ref,
    flag_ref,
    react_ref,
    sampled_ref,
    count_ref,
    acc_ref,
    edge_ref,
    in_ref,
    center_ref,
    cell_ref,
    coef_ref,
    pick_ref,
):
    params, layers, width_y, width_z, plane, samples = dims
    y_at = lax.broadcasted_iota(I32, (width_y, width_z), 0)
    z_at = lax.broadcasted_iota(I32, (width_y, width_z), 1)
    for param in range(params):
        uppers, nexts = [], []
        for layer in range(layers):
            up_d, next_d = [], []
            for axis_d in range(3):
                forward = flag_ref[param, axis_d, layer] == 1
                speed = speed_ref[param, axis_d, layer]
                diff = diff_ref[param, axis_d, layer]
                up_d.append(jnp.where(forward, speed, 0.0) + diff)
                next_d.append(jnp.where(forward, 0.0, -speed) - diff)
            uppers.append(up_d)
            nexts.append(next_d)
        edge_ref[param] = nexts[layers - 1][0]
        for layer in range(layers):
            diag = react_ref[param, layer]
            diag = diag + uppers[layer][0] + uppers[layer][1] + uppers[layer][2]
            if layer > 0:
                diag = diag - nexts[layer - 1][0]
                coef_ref[param, layer, 2] = -uppers[layer - 1][0]
            coef_ref[param, layer, 1] = nexts[layer][0]
            for axis_d, at, shift_axis, size in ((1, y_at, 0, width_y), (2, z_at, 1, width_z)):
                up, following = uppers[layer][axis_d], nexts[layer][axis_d]
                low_up = jnp.where(at == 0, 0.0, pltpu.roll(up, 1, shift_axis))
                low_next = jnp.where(at == 0, 0.0, pltpu.roll(following, 1, shift_axis))
                diag = diag - low_next
                coef_ref[param, layer, 1 + 2 * axis_d] = jnp.where(at == size - 1, 0.0, following)
                coef_ref[param, layer, 2 + 2 * axis_d] = -low_up
            coef_ref[param, layer, 0] = diag

    def tile(layer, y):
        start = layer * plane + y * width_z
        return flat_ref[:MB, start : start + width_z].astype(F32)

    for layer in range(layers):
        for y in range(width_y):
            start = layer * plane + y * width_z
            state = tile(layer, y)
            terms = [(0, state), (5, pltpu.roll(state, width_z - 1, 1)), (6, pltpu.roll(state, 1, 1))]
            if layer < layers - 1:
                terms.append((1, tile(layer + 1, y)))
            if layer > 0:
                terms.append((2, tile(layer - 1, y)))
            if y < width_y - 1:
                terms.append((3, tile(layer, y + 1)))
            if y > 0:
                terms.append((4, tile(layer, y - 1)))
            for param in range(params):
                total = None
                for at, term in terms:
                    product = coef_ref[param, layer, at, y : y + 1, :] * term
                    total = product if total is None else total + product
                acc_ref[param * MB : (param + 1) * MB, start : start + width_z] = total

    count = column(count_ref[...])
    slots = sampled_ref.shape[0]
    held = []
    for slot in range(slots):
        held.append(jnp.where(slot < count, column(sampled_ref[slot : slot + 1]), -4 * layers * plane))
    cell = jnp.concatenate(held, axis=0)
    cell_ref[...] = cell
    z_of = lax.broadcasted_iota(I32, (1, width_z), 1)
    for layer in range(layers):
        for y in range(width_y):
            start = layer * plane + y * width_z
            away = z_of - (cell - start)
            hits = [away == 0, away == -plane, away == plane]
            hits.append(away == -width_z if y < width_y - 1 else None)
            hits.append(away == width_z if y > 0 else None)
            hits.append((away == -1) & (z_of < width_z - 1))
            hits.append((away == 1) & (z_of > 0))
            for at, hit in enumerate(hits):
                value = jnp.zeros((samples, width_z), BF16)
                if hit is not None:
                    value = jnp.where(hit, 1.0, 0.0).astype(BF16)
                pick_ref[at * samples : (at + 1) * samples, start : start + width_z] = value
    center_ref[...] = pick_ref[:samples]
    in_ref[...] = nt_dot(pick_ref[...], flat_ref[:MB, :]).astype(BF16)


def finish_layer(dims, from_next, layer, halo_ref, flat_ref, acc_ref, edge_ref, applied_ref, coef_ref, spread_ref, beside_ref):
    params, layers, width_y, width_z, plane = dims
    faces = []
    for at in range(2 * SPLITS):
        part = halo_ref[MB + at * params : MB + (at + 1) * params].astype(F32)
        faces.append(part.reshape(params * width_y, width_z))
    signed = faces[0] + faces[1] + faces[2]
    diff = faces[3] + faces[4] + faces[5]
    edge = edge_ref[...].reshape(params * width_y, width_z)
    coef_ref[0] = jnp.where(from_next, edge, -(jnp.maximum(signed, 0.0) + diff))
    coef_ref[1] = jnp.where(from_next, 0.0, diff - jnp.minimum(signed, 0.0))
    spread_ref[...] = halo_ref[:MB].astype(F32).reshape(MB * width_y, width_z)
    for y in range(width_y):
        at = pl.multiple_of(layer * plane + y * width_z, width_z)
        lanes = slice(y * width_z, (y + 1) * width_z)
        state = flat_ref[:MB, pl.ds(at, width_z)].astype(F32)
        beside = spread_ref[pl.ds(y, MB, stride=width_y), :]
        beside_ref[:, lanes] = beside.astype(BF16)
        for param in range(params):
            modes = slice(param * MB, (param + 1) * MB)
            row = param * width_y + y
            total = acc_ref[modes, pl.ds(at, width_z)]
            total = total + coef_ref[1, row : row + 1, :] * state
            total = total + coef_ref[0, row : row + 1, :] * beside
            applied_ref[modes, lanes] = total.astype(BF16)


def near_kernel(dims, flat_ref, inner_ref, acc_ref, edge_ref, center_ref, cell_ref, sums_ref, picks_ref, side_ref, *scratch):
    params, layers, width_y, width_z, plane, samples = dims
    odd = core() == 1
    layer = (1 - core()) * (layers - 1)
    start = pl.multiple_of(layer * plane, plane)
    finish_layer(dims[:5], jnp.logical_not(odd), layer, inner_ref, flat_ref, acc_ref, edge_ref, *scratch)
    applied_ref, beside_ref = scratch[0], scratch[3]
    sums_ref[...] = nt_dot(flat_ref[:, pl.ds(start, plane)], applied_ref[...])
    picks_ref[...] = nt_dot(center_ref[:, pl.ds(start, plane)], applied_ref[...])
    below = cell_ref[...]
    above = below - (layers - 1) * plane
    side_ref[...] = nt_dot(picked(jnp.where(odd, below, above), 0, plane), beside_ref[...]).astype(BF16)


def project_kernel(
    dims,
    relative,
    flat_ref,
    outer_ref,
    acc_ref,
    edge_ref,
    in_ref,
    center_ref,
    near_sums_ref,
    near_picks_ref,
    near_side_ref,
    cell_ref,
    table_ref,
    keep_ref,
    keep_rows_ref,
    packet_ref,
    sums_ref,
    *scratch,
):
    params, layers, width_y, width_z, plane, samples, devices, own = dims
    odd = core() == 1
    layer = core() * (layers - 1)
    lane = pl.multiple_of(layer * plane, plane)
    finish_layer(dims[:5], odd, layer, outer_ref, flat_ref, acc_ref, edge_ref, *scratch)
    applied_ref, beside_ref = scratch[0], scratch[3]

    sums = near_sums_ref[...] + nt_dot(flat_ref[:, pl.ds(lane, plane)], applied_ref[...])
    for param in range(params):
        sums_ref[pl.ds(param, sums.shape[0], stride=params), :] = sums[:, param * MB : (param + 1) * MB]
    size = own * params
    half = devices // 2
    me = lax.axis_index("cells")
    for place in range(devices):
        start = pl.multiple_of((me ^ relative[place]) * size, size)
        terms = sums_ref[pl.ds(start, size), :]
        if place < half:
            keep_ref[place * size : (place + 1) * size] = terms
        else:
            head, rest = halves(terms)
            at = (place - half) * size
            packet_ref[at : at + size] = head
            packet_ref[half * size + at : half * size + at + size] = rest

    picks = nt_dot(center_ref[:, pl.ds(lane, plane)], applied_ref[...])
    got_applied = (near_picks_ref[...] + picks).astype(BF16)
    below = cell_ref[...]
    above = below - (layers - 1) * plane
    far = nt_dot(picked(jnp.where(odd, above, below), 0, plane), beside_ref[...]).astype(BF16)
    near = near_side_ref[...]
    got_below = in_ref[samples : 2 * samples] + jnp.where(odd, near, far)
    got_above = in_ref[2 * samples : 3 * samples] + jnp.where(odd, far, near)
    pieces = [got_applied[:, param * MB : (param + 1) * MB] for param in range(params)]
    pieces += [in_ref[:samples], got_below, got_above, in_ref[3 * samples :]]
    gathered = jnp.concatenate(pieces, axis=0)
    total_rows = gathered.shape[0]
    order = picked((table_ref[:total_rows, 1:2] ^ me) + table_ref[:total_rows, 2:3], 0, gathered.shape[0])
    ordered = jnp.dot(order, gathered, preferred_element_type=F32).astype(BF16)
    count = ordered.shape[0] // 2
    keep_rows_ref[...] = ordered[:count]
    packet_ref[2 * half * size :] = ordered[count:]


def merge_kernel(wide_in, wide_out, keep_ref, keep_rows_ref, got_ref, table_ref, keep_out, rows_out, packet_out):
    size = keep_ref.shape[0]
    half = size // 2
    total = keep_ref[...] + got_ref[:size].astype(F32)
    if wide_in:
        total = total + got_ref[size : 2 * size].astype(F32)
    keep_out[...] = total[:half]
    if wide_out:
        head, rest = halves(total[half:])
        packet_out[:half] = head
        packet_out[half : 2 * half] = rest
    else:
        packet_out[:half] = total[half:].astype(BF16)
    count = keep_rows_ref.shape[0]
    rows = jnp.concatenate([keep_rows_ref[...], got_ref[got_ref.shape[0] - count :]], axis=0)
    order = picked(table_ref[: 2 * count, 0:1], 0, 2 * count)
    ordered = jnp.dot(order, rows, preferred_element_type=F32).astype(BF16)
    rows_out[...] = ordered[:count]
    packet_out[packet_out.shape[0] - count :] = ordered[count:]


def spread_kernel(wide_in, room, keep_ref, keep_rows_ref, got_ref, table_ref, keep_out, rows_out, *packets_out):
    size = keep_ref.shape[0]
    total = keep_ref[...] + got_ref[:size].astype(F32)
    if wide_in:
        total = total + got_ref[size : 2 * size].astype(F32)
    part = size // DIRECT
    count = keep_rows_ref.shape[0]
    rows = jnp.concatenate([keep_rows_ref[...], got_ref[got_ref.shape[0] - count :]], axis=0)
    order = picked(table_ref[: DIRECT * room, 5:6], 0, 2 * count)
    ordered = jnp.dot(order, rows, preferred_element_type=F32).astype(BF16)
    keep_out[...] = total[:part]
    rows_out[...] = ordered[:room]
    for at, packet_out in enumerate(packets_out, 1):
        packet_out[:part] = total[at * part : (at + 1) * part].astype(BF16)
        packet_out[part:] = ordered[at * room : (at + 1) * room]


def final_kernel(volume, steps, block, keep_ref, keep_rows_ref, *refs):
    got_refs, table_ref, sum_out, rows_out = refs[: DIRECT - 1], refs[-3], refs[-2], refs[-1]
    size = keep_ref.shape[0]
    room = keep_rows_ref.shape[0]
    total = keep_ref[...]
    rows = [keep_rows_ref[...]] + [None] * (DIRECT - 1)
    for at, got_ref in zip(ORDER, got_refs):
        total = total + got_ref[:size].astype(F32)
        rows[at] = got_ref[size:]
    sum_out[...] = volume * total
    me = lax.axis_index("cells")
    mine = 0
    for step, place in enumerate(places(steps)):
        mine = mine + (((me >> step) & 1) << place)
    came = table_ref[: rows_out.shape[0], 3:4] ^ mine
    low = steps - 2
    start = (came >> low) * room + (came & ((1 << low) - 1)) * block
    order = picked(start + table_ref[: rows_out.shape[0], 4:5], 0, DIRECT * room)
    rows_out[...] = jnp.dot(order, jnp.concatenate(rows, axis=0), preferred_element_type=F32).astype(BF16)


def places(steps):
    return [steps - 3 - step for step in range(steps - 2)] + [steps - 1, steps - 2]


def shape(dims, dtype):
    return jax.ShapeDtypeStruct(dims, dtype)


def shards(basis, face_speed, face_diffusion, upwind_flag, reaction, sample_cell, sample_count):
    modes, layers, width_y, width_z = basis.shape
    params = face_speed.shape[0]
    devices = lax.axis_size("cells")
    slots = sample_cell.shape[2]
    plane = width_y * width_z
    cells = layers * plane
    own = modes // devices
    rows = params + OFFSETS
    samples = devices * slots
    steps = devices.bit_length() - 1

    tail = params * width_y
    hbm = pl.BlockSpec(memory_space=pltpu.HBM)
    planes = 2 * SPLITS * params
    packed = shape((MB + planes, width_y, width_z), BF16)
    to_inner, to_outer = pl.pallas_call(
        functools.partial(pack_kernel, (params, layers)),
        out_shape=(packed, packed),
        in_specs=[hbm] * 4,
        out_specs=(VMEM, VMEM),
        scratch_shapes=[
            pltpu.VMEM((params, width_y, width_z), F32),
            pltpu.VMEM((params, width_y, width_z), F32),
            pltpu.VMEM((params, width_y, width_z), I32),
            pltpu.SemaphoreType.DMA((5,)),
        ],
        compiler_params=LIMIT,
        name="pack_halo",
    )(*[pltpu.with_memory_space_constraint(value, pltpu.HBM) for value in (basis, face_speed, face_diffusion, upwind_flag)])
    inner_pairs = [(i, i ^ 1) for i in range(devices)]
    outer_pairs = []
    for i in range(1, devices - 1, 2):
        outer_pairs += [(i, i + 1), (i + 1, i)]
    inner = lax.ppermute(to_inner, "cells", inner_pairs)
    outer = lax.ppermute(to_outer, "cells", outer_pairs)

    loaded, cells_in, counts_in = pl.pallas_call(
        load_kernel,
        out_shape=(shape(basis.shape, BF16), shape((slots, devices), I32), shape((1, devices), I32)),
        in_specs=[hbm] * 3 + [VMEM],
        out_specs=(VMEM,) * 3,
        scratch_shapes=[pltpu.SemaphoreType.DMA((3,))],
        compiler_params=LIMIT,
        name="load",
    )(basis, sample_cell[0].T, sample_count, to_outer)
    flat = loaded.reshape(modes, cells)

    block = slots * rows
    relative = [sum(((place >> (steps - 1 - step)) & 1) << step for step in range(steps)) for place in range(devices)]
    block = slots * rows
    share = devices // DIRECT * block
    room = round_up(share, 16)
    table = np.full((DIRECT * room, 8), -1, np.int32)
    in_block = np.arange(block)
    for place in range(devices):
        turned = (((place & 1) << (steps - 1)) + (place >> 1)) * block + in_block
        at = slice(place * block, (place + 1) * block)
        table[at, 0] = turned
        table[at, 1] = relative[place]
        table[at, 2] = (in_block // slots) * samples + (in_block % slots) * devices
        table[at, 3] = sum(((place >> step) & 1) << to for step, to in enumerate(places(steps)))
        table[at, 4] = in_block
        start = place * block // share * room + place * block % share
        table[start : start + block, 5] = turned
    table = jnp.asarray(table)

    acc, edge, got_in, center, cell = pl.pallas_call(
        functools.partial(local_kernel, (params, layers, width_y, width_z, plane, samples)),
        out_shape=(
            shape((params * MB, cells), F32),
            shape((params, width_y, width_z), F32),
            shape((OFFSETS * samples, MB), BF16),
            shape((samples, cells), BF16),
            shape((samples, 1), I32),
        ),
        in_specs=[VMEM] * 7,
        out_specs=(VMEM,) * 5,
        scratch_shapes=[
            pltpu.VMEM((params, layers, OFFSETS, width_y, width_z), F32),
            pltpu.VMEM((OFFSETS * samples, cells), BF16),
        ],
        compiler_params=LIMIT,
        cost_estimate=SMALL,
        name="local_stencil",
    )(flat, face_speed, face_diffusion, upwind_flag, reaction, cells_in, counts_in)

    finish_scratch = [
        pltpu.VMEM((params * MB, plane), BF16),
        pltpu.VMEM((2, tail, width_z), F32),
        pltpu.VMEM((MB * width_y, width_z), F32),
        pltpu.VMEM((MB, plane), BF16),
    ]
    near_sums, near_picks, near_side = pl.pallas_call(
        functools.partial(near_kernel, (params, layers, width_y, width_z, plane, samples)),
        out_shape=(
            shape((modes, params * MB), F32),
            shape((samples, params * MB), F32),
            shape((samples, MB), BF16),
        ),
        in_specs=[VMEM] * 6,
        out_specs=(VMEM,) * 3,
        scratch_shapes=finish_scratch,
        compiler_params=LIMIT,
        cost_estimate=SMALL,
        name="near_layer",
    )(flat, inner, acc, edge, center, cell)

    size = own * params
    half = devices // 2
    count = half * block
    keep, keep_rows, packet = pl.pallas_call(
        functools.partial(
            project_kernel,
            (params, layers, width_y, width_z, plane, samples, devices, own),
            relative,
        ),
        out_shape=(
            shape((half * size, MB), F32),
            shape((count, MB), BF16),
            shape((2 * half * size + count, MB), BF16),
        ),
        in_specs=[VMEM] * 11,
        out_specs=(VMEM,) * 3,
        scratch_shapes=[pltpu.VMEM((params * modes, MB), F32)] + finish_scratch,
        compiler_params=LIMIT,
        name="project",
    )(
        flat,
        outer,
        acc,
        edge,
        got_in,
        center,
        near_sums,
        near_picks,
        near_side,
        cell,
        table,
    )

    wide = True
    for step in range(steps - 2):
        got = lax.ppermute(packet, "cells", [(i, i ^ (1 << step)) for i in range(devices)])
        if step < steps - 3:
            next_wide = step + 1 > NARROW_STEPS
            half //= 2
            packet_rows = (2 if next_wide else 1) * half * size + count
            keep, keep_rows, packet = pl.pallas_call(
                functools.partial(merge_kernel, wide, next_wide),
                out_shape=(
                    shape((half * size, MB), F32),
                    shape((count, MB), BF16),
                    shape((packet_rows, MB), BF16),
                ),
                in_specs=[VMEM] * 4,
                out_specs=(VMEM,) * 3,
                compiler_params=LIMIT,
                name="merge",
            )(keep, keep_rows, got, table)
            wide = next_wide
    sent = shape((size + room, MB), BF16)
    keep, keep_rows, *packets = pl.pallas_call(
        functools.partial(spread_kernel, wide, room),
        out_shape=(shape((size, MB), F32), shape((room, MB), BF16)) + (sent,) * (DIRECT - 1),
        in_specs=[VMEM] * 4,
        out_specs=(VMEM,) * (DIRECT + 1),
        compiler_params=LIMIT,
        name="spread",
    )(keep, keep_rows, got, table)
    got = [None] * DIRECT
    for at in ORDER:
        mask = ((at >> 1) << (steps - 2)) | ((at & 1) << (steps - 1))
        got[at] = lax.ppermute(packets[at - 1], "cells", [(i, i ^ mask) for i in range(devices)])
    volume = 1.0 / (layers * devices * width_y * width_z)
    summed, sampled = pl.pallas_call(
        functools.partial(final_kernel, volume, steps, block),
        out_shape=(shape((size, MB), F32), shape((2 * count, MB), BF16)),
        in_specs=[VMEM] * (DIRECT + 2),
        out_specs=(VMEM,) * 2,
        compiler_params=LIMIT,
        name="finish",
    )(keep, keep_rows, *[got[at] for at in ORDER], table)
    galerkin = summed.reshape(own, params, MB)
    sampled = sampled.reshape(devices, rows, slots, MB)
    return (galerkin, jnp.transpose(sampled, (0, 2, 1, 3))[None])


def solution(mesh):
    return jax.shard_map(
        shards,
        mesh=mesh,
        in_specs=(
            P(None, ("groups", "cells"), None, None),
            P(None, None, ("groups", "cells"), None, None),
            P(None, None, ("groups", "cells"), None, None),
            P(None, None, ("groups", "cells"), None, None),
            P(None, ("groups", "cells"), None, None),
            P(("groups", "cells"), None, None),
            P(("groups", "cells"), None),
        ),
        out_specs=(
            P(("groups", "cells"), None, None),
            P(("groups", "cells"), None, None, None, None),
        ),
        check_vma=False,
    )
```

```python
import functools

import jax
import jax.numpy as jnp
import numpy as np
from jax import lax
from jax.experimental import pallas as pl
from jax.experimental.pallas import tpu as pltpu
from jax.sharding import PartitionSpec as P

MB = 128
SPLITS = 3
NARROW_STEPS = 1
DIRECT = 4
ORDER = (3, 2, 1)
BF16 = jnp.bfloat16
F32 = jnp.float32
I32 = jnp.int32
OFFSETS = 7
VMEM = pl.BlockSpec(memory_space=pltpu.VMEM)
SMALL = pl.CostEstimate(flops=1, bytes_accessed=1, transcendentals=0)
LIMIT = pltpu.CompilerParams(vmem_limit_bytes=20 * 1024 * 1024)


def nt_dot(left, right):
    return lax.dot_general(left, right, (((1,), (1,)), ((), ())), preferred_element_type=F32)


def picked(targets, start, count):
    lanes = lax.broadcasted_iota(I32, (1, count), 1) + start
    return jnp.where(targets == lanes, 1.0, 0.0).astype(BF16)


def column(row):
    size = row.shape[1]
    down = lax.broadcasted_iota(I32, (size, size), 0)
    across = lax.broadcasted_iota(I32, (size, size), 1)
    spread = jnp.where(down == across, row.astype(F32), 0.0)
    return jnp.sum(spread, axis=1, keepdims=True).astype(I32)


def round_up(value, multiple):
    return -(-value // multiple) * multiple


def halves(value):
    head = value.astype(BF16)
    return head, (value - head.astype(F32)).astype(BF16)


def core():
    return lax.rem(lax.axis_index("cells"), 2)


def face_parts(speed, diff, flag):
    parts = []
    for value in (jnp.where(flag == 1, speed, -speed), diff):
        for _ in range(SPLITS):
            head = value.astype(BF16)
            value = value - head.astype(F32)
            parts.append(head)
    return parts


def pack_kernel(dims, basis_ref, speed_ref, diff_ref, flag_ref, low_ref, high_ref, outer_ref, speed_buf, diff_buf, flag_buf, sems):
    params, layers = dims
    last = layers - 1
    half = MB // 2
    block = pl.ds(0, MB)
    low, high = pl.ds(0, half), pl.ds(half, half)
    beside = (1 - core()) * last
    layers_out = [
        pltpu.make_async_copy(basis_ref.at[block, core() * last], outer_ref.at[block], sems.at[0]),
        pltpu.make_async_copy(basis_ref.at[low, beside], low_ref.at[low], sems.at[1]),
        pltpu.make_async_copy(basis_ref.at[high, beside], high_ref, sems.at[5]),
    ]
    copies = [
        pltpu.make_async_copy(speed_ref.at[:, 0, last], speed_buf, sems.at[2]),
        pltpu.make_async_copy(diff_ref.at[:, 0, last], diff_buf, sems.at[3]),
        pltpu.make_async_copy(flag_ref.at[:, 0, last], flag_buf, sems.at[4]),
    ]
    for copy in copies + layers_out:
        copy.start()
    for copy in copies:
        copy.wait()
    for at, part in enumerate(face_parts(speed_buf[...], diff_buf[...], flag_buf[...])):
        low_ref[half + at * params : half + (at + 1) * params] = part
        outer_ref[MB + at * params : MB + (at + 1) * params] = part
    for copy in layers_out:
        copy.wait()


def load_kernel(basis_ref, cell_ref, count_ref, after_ref, basis_out, cell_out, count_out, sems):
    del after_ref
    pairs = ((basis_ref, basis_out), (cell_ref, cell_out), (count_ref, count_out))
    copies = [pltpu.make_async_copy(source, out, sems.at[at]) for at, (source, out) in enumerate(pairs)]
    for copy in copies:
        copy.start()
    for copy in copies:
        copy.wait()


def local_kernel(
    dims,
    flat_ref,
    speed_ref,
    diff_ref,
    flag_ref,
    react_ref,
    sampled_ref,
    count_ref,
    acc_ref,
    edge_ref,
    in_ref,
    center_ref,
    cell_ref,
    coef_ref,
    pick_ref,
):
    params, layers, width_y, width_z, plane, samples = dims
    y_at = lax.broadcasted_iota(I32, (width_y, width_z), 0)
    z_at = lax.broadcasted_iota(I32, (width_y, width_z), 1)
    for param in range(params):
        uppers, nexts = [], []
        for layer in range(layers):
            up_d, next_d = [], []
            for axis_d in range(3):
                forward = flag_ref[param, axis_d, layer] == 1
                speed = speed_ref[param, axis_d, layer]
                diff = diff_ref[param, axis_d, layer]
                up_d.append(jnp.where(forward, speed, 0.0) + diff)
                next_d.append(jnp.where(forward, 0.0, -speed) - diff)
            uppers.append(up_d)
            nexts.append(next_d)
        edge_ref[param] = nexts[layers - 1][0]
        for layer in range(layers):
            diag = react_ref[param, layer]
            diag = diag + uppers[layer][0] + uppers[layer][1] + uppers[layer][2]
            if layer > 0:
                diag = diag - nexts[layer - 1][0]
                coef_ref[param, layer, 2] = -uppers[layer - 1][0]
            coef_ref[param, layer, 1] = nexts[layer][0]
            for axis_d, at, shift_axis, size in ((1, y_at, 0, width_y), (2, z_at, 1, width_z)):
                up, following = uppers[layer][axis_d], nexts[layer][axis_d]
                low_up = jnp.where(at == 0, 0.0, pltpu.roll(up, 1, shift_axis))
                low_next = jnp.where(at == 0, 0.0, pltpu.roll(following, 1, shift_axis))
                diag = diag - low_next
                coef_ref[param, layer, 1 + 2 * axis_d] = jnp.where(at == size - 1, 0.0, following)
                coef_ref[param, layer, 2 + 2 * axis_d] = -low_up
            coef_ref[param, layer, 0] = diag

    def tile(layer, y):
        start = layer * plane + y * width_z
        return flat_ref[:MB, start : start + width_z].astype(F32)

    for layer in range(layers):
        for y in range(width_y):
            start = layer * plane + y * width_z
            state = tile(layer, y)
            terms = [(0, state), (5, pltpu.roll(state, width_z - 1, 1)), (6, pltpu.roll(state, 1, 1))]
            if layer < layers - 1:
                terms.append((1, tile(layer + 1, y)))
            if layer > 0:
                terms.append((2, tile(layer - 1, y)))
            if y < width_y - 1:
                terms.append((3, tile(layer, y + 1)))
            if y > 0:
                terms.append((4, tile(layer, y - 1)))
            for param in range(params):
                total = None
                for at, term in terms:
                    product = coef_ref[param, layer, at, y : y + 1, :] * term
                    total = product if total is None else total + product
                acc_ref[param * MB : (param + 1) * MB, start : start + width_z] = total

    count = column(count_ref[...])
    slots = sampled_ref.shape[0]
    held = []
    for slot in range(slots):
        held.append(jnp.where(slot < count, column(sampled_ref[slot : slot + 1]), -4 * layers * plane))
    cell = jnp.concatenate(held, axis=0)
    cell_ref[...] = cell
    z_of = lax.broadcasted_iota(I32, (1, width_z), 1)
    for layer in range(layers):
        for y in range(width_y):
            start = layer * plane + y * width_z
            away = z_of - (cell - start)
            hits = [away == 0, away == -plane, away == plane]
            hits.append(away == -width_z if y < width_y - 1 else None)
            hits.append(away == width_z if y > 0 else None)
            hits.append((away == -1) & (z_of < width_z - 1))
            hits.append((away == 1) & (z_of > 0))
            for at, hit in enumerate(hits):
                value = jnp.zeros((samples, width_z), BF16)
                if hit is not None:
                    value = jnp.where(hit, 1.0, 0.0).astype(BF16)
                pick_ref[at * samples : (at + 1) * samples, start : start + width_z] = value
    center_ref[...] = pick_ref[:samples]
    in_ref[...] = nt_dot(pick_ref[...], flat_ref[:MB, :]).astype(BF16)


def finish_layer(dims, from_next, layer, halo_refs, flat_ref, acc_ref, edge_ref, applied_ref, coef_ref, spread_ref, beside_ref):
    params, layers, width_y, width_z, plane = dims
    held = MB // len(halo_refs)
    faces = []
    for at in range(2 * SPLITS):
        part = halo_refs[0][held + at * params : held + (at + 1) * params].astype(F32)
        faces.append(part.reshape(params * width_y, width_z))
    signed = faces[0] + faces[1] + faces[2]
    diff = faces[3] + faces[4] + faces[5]
    edge = edge_ref[...].reshape(params * width_y, width_z)
    coef_ref[0] = jnp.where(from_next, edge, -(jnp.maximum(signed, 0.0) + diff))
    coef_ref[1] = jnp.where(from_next, 0.0, diff - jnp.minimum(signed, 0.0))
    size = held * width_y
    for at, halo_ref in enumerate(halo_refs):
        spread_ref[at * size : (at + 1) * size] = halo_ref[:held].astype(F32).reshape(size, width_z)
    for y in range(width_y):
        at = pl.multiple_of(layer * plane + y * width_z, width_z)
        lanes = slice(y * width_z, (y + 1) * width_z)
        state = flat_ref[:MB, pl.ds(at, width_z)].astype(F32)
        beside = spread_ref[pl.ds(y, MB, stride=width_y), :]
        beside_ref[:, lanes] = beside.astype(BF16)
        for param in range(params):
            modes = slice(param * MB, (param + 1) * MB)
            row = param * width_y + y
            total = acc_ref[modes, pl.ds(at, width_z)]
            total = total + coef_ref[1, row : row + 1, :] * state
            total = total + coef_ref[0, row : row + 1, :] * beside
            applied_ref[modes, lanes] = total.astype(BF16)


def near_kernel(dims, flat_ref, low_ref, high_ref, acc_ref, edge_ref, center_ref, cell_ref, sums_ref, picks_ref, side_ref, *scratch):
    params, layers, width_y, width_z, plane, samples = dims
    odd = core() == 1
    layer = (1 - core()) * (layers - 1)
    start = pl.multiple_of(layer * plane, plane)
    finish_layer(dims[:5], jnp.logical_not(odd), layer, (low_ref, high_ref), flat_ref, acc_ref, edge_ref, *scratch)
    applied_ref, beside_ref = scratch[0], scratch[3]
    sums_ref[...] = nt_dot(flat_ref[:, pl.ds(start, plane)], applied_ref[...])
    picks_ref[...] = nt_dot(center_ref[:, pl.ds(start, plane)], applied_ref[...])
    below = cell_ref[...]
    above = below - (layers - 1) * plane
    side_ref[...] = nt_dot(picked(jnp.where(odd, below, above), 0, plane), beside_ref[...]).astype(BF16)


def project_kernel(
    dims,
    relative,
    flat_ref,
    outer_ref,
    acc_ref,
    edge_ref,
    in_ref,
    center_ref,
    near_sums_ref,
    near_picks_ref,
    near_side_ref,
    cell_ref,
    table_ref,
    keep_ref,
    keep_rows_ref,
    packet_ref,
    sums_ref,
    *scratch,
):
    params, layers, width_y, width_z, plane, samples, devices, own = dims
    odd = core() == 1
    layer = core() * (layers - 1)
    lane = pl.multiple_of(layer * plane, plane)
    finish_layer(dims[:5], odd, layer, (outer_ref,), flat_ref, acc_ref, edge_ref, *scratch)
    applied_ref, beside_ref = scratch[0], scratch[3]

    sums = near_sums_ref[...] + nt_dot(flat_ref[:, pl.ds(lane, plane)], applied_ref[...])
    for param in range(params):
        sums_ref[pl.ds(param, sums.shape[0], stride=params), :] = sums[:, param * MB : (param + 1) * MB]
    size = own * params
    half = devices // 2
    me = lax.axis_index("cells")
    for place in range(devices):
        start = pl.multiple_of((me ^ relative[place]) * size, size)
        terms = sums_ref[pl.ds(start, size), :]
        if place < half:
            keep_ref[place * size : (place + 1) * size] = terms
        else:
            head, rest = halves(terms)
            at = (place - half) * size
            packet_ref[at : at + size] = head
            packet_ref[half * size + at : half * size + at + size] = rest

    picks = nt_dot(center_ref[:, pl.ds(lane, plane)], applied_ref[...])
    got_applied = (near_picks_ref[...] + picks).astype(BF16)
    below = cell_ref[...]
    above = below - (layers - 1) * plane
    far = nt_dot(picked(jnp.where(odd, above, below), 0, plane), beside_ref[...]).astype(BF16)
    near = near_side_ref[...]
    got_below = in_ref[samples : 2 * samples] + jnp.where(odd, near, far)
    got_above = in_ref[2 * samples : 3 * samples] + jnp.where(odd, far, near)
    pieces = [got_applied[:, param * MB : (param + 1) * MB] for param in range(params)]
    pieces += [in_ref[:samples], got_below, got_above, in_ref[3 * samples :]]
    gathered = jnp.concatenate(pieces, axis=0)
    total_rows = gathered.shape[0]
    order = picked((table_ref[:total_rows, 1:2] ^ me) + table_ref[:total_rows, 2:3], 0, gathered.shape[0])
    ordered = jnp.dot(order, gathered, preferred_element_type=F32).astype(BF16)
    count = ordered.shape[0] // 2
    keep_rows_ref[...] = ordered[:count]
    packet_ref[2 * half * size :] = ordered[count:]


def merge_kernel(wide_in, wide_out, keep_ref, keep_rows_ref, got_ref, table_ref, keep_out, rows_out, packet_out):
    size = keep_ref.shape[0]
    half = size // 2
    total = keep_ref[...] + got_ref[:size].astype(F32)
    if wide_in:
        total = total + got_ref[size : 2 * size].astype(F32)
    keep_out[...] = total[:half]
    if wide_out:
        head, rest = halves(total[half:])
        packet_out[:half] = head
        packet_out[half : 2 * half] = rest
    else:
        packet_out[:half] = total[half:].astype(BF16)
    count = keep_rows_ref.shape[0]
    rows = jnp.concatenate([keep_rows_ref[...], got_ref[got_ref.shape[0] - count :]], axis=0)
    order = picked(table_ref[: 2 * count, 0:1], 0, 2 * count)
    ordered = jnp.dot(order, rows, preferred_element_type=F32).astype(BF16)
    rows_out[...] = ordered[:count]
    packet_out[packet_out.shape[0] - count :] = ordered[count:]


def spread_kernel(wide_in, room, keep_ref, keep_rows_ref, got_ref, table_ref, keep_out, rows_out, *packets_out):
    size = keep_ref.shape[0]
    total = keep_ref[...] + got_ref[:size].astype(F32)
    if wide_in:
        total = total + got_ref[size : 2 * size].astype(F32)
    part = size // DIRECT
    count = keep_rows_ref.shape[0]
    rows = jnp.concatenate([keep_rows_ref[...], got_ref[got_ref.shape[0] - count :]], axis=0)
    order = picked(table_ref[: DIRECT * room, 5:6], 0, 2 * count)
    ordered = jnp.dot(order, rows, preferred_element_type=F32).astype(BF16)
    keep_out[...] = total[:part]
    rows_out[...] = ordered[:room]
    for at, packet_out in enumerate(packets_out, 1):
        packet_out[:part] = total[at * part : (at + 1) * part].astype(BF16)
        packet_out[part:] = ordered[at * room : (at + 1) * room]


def final_kernel(volume, steps, block, keep_ref, keep_rows_ref, *refs):
    got_refs, table_ref, sum_out, rows_out = refs[: DIRECT - 1], refs[-3], refs[-2], refs[-1]
    size = keep_ref.shape[0]
    room = keep_rows_ref.shape[0]
    total = keep_ref[...]
    rows = [keep_rows_ref[...]] + [None] * (DIRECT - 1)
    for at, got_ref in zip(ORDER, got_refs):
        total = total + got_ref[:size].astype(F32)
        rows[at] = got_ref[size:]
    sum_out[...] = volume * total
    me = lax.axis_index("cells")
    mine = 0
    for step, place in enumerate(places(steps)):
        mine = mine + (((me >> step) & 1) << place)
    came = table_ref[: rows_out.shape[0], 3:4] ^ mine
    low = steps - 2
    start = (came >> low) * room + (came & ((1 << low) - 1)) * block
    order = picked(start + table_ref[: rows_out.shape[0], 4:5], 0, DIRECT * room)
    rows_out[...] = jnp.dot(order, jnp.concatenate(rows, axis=0), preferred_element_type=F32).astype(BF16)


def places(steps):
    return [steps - 3 - step for step in range(steps - 2)] + [steps - 1, steps - 2]


def shape(dims, dtype):
    return jax.ShapeDtypeStruct(dims, dtype)


def shards(basis, face_speed, face_diffusion, upwind_flag, reaction, sample_cell, sample_count):
    modes, layers, width_y, width_z = basis.shape
    params = face_speed.shape[0]
    devices = lax.axis_size("cells")
    slots = sample_cell.shape[2]
    plane = width_y * width_z
    cells = layers * plane
    own = modes // devices
    rows = params + OFFSETS
    samples = devices * slots
    steps = devices.bit_length() - 1

    tail = params * width_y
    hbm = pl.BlockSpec(memory_space=pltpu.HBM)
    planes = 2 * SPLITS * params
    to_low, to_high, to_outer = pl.pallas_call(
        functools.partial(pack_kernel, (params, layers)),
        out_shape=(
            shape((MB // 2 + planes, width_y, width_z), BF16),
            shape((MB // 2, width_y, width_z), BF16),
            shape((MB + planes, width_y, width_z), BF16),
        ),
        in_specs=[hbm] * 4,
        out_specs=(VMEM,) * 3,
        scratch_shapes=[
            pltpu.VMEM((params, width_y, width_z), F32),
            pltpu.VMEM((params, width_y, width_z), F32),
            pltpu.VMEM((params, width_y, width_z), I32),
            pltpu.SemaphoreType.DMA((6,)),
        ],
        compiler_params=LIMIT,
        name="pack_halo",
    )(*[pltpu.with_memory_space_constraint(value, pltpu.HBM) for value in (basis, face_speed, face_diffusion, upwind_flag)])
    inner_pairs = [(i, i ^ 1) for i in range(devices)]
    outer_pairs = []
    for i in range(1, devices - 1, 2):
        outer_pairs += [(i, i + 1), (i + 1, i)]
    low = lax.ppermute(to_low, "cells", inner_pairs)
    high = lax.ppermute(to_high, "cells", inner_pairs)
    outer = lax.ppermute(to_outer, "cells", outer_pairs)

    loaded, cells_in, counts_in = pl.pallas_call(
        load_kernel,
        out_shape=(shape(basis.shape, BF16), shape((slots, devices), I32), shape((1, devices), I32)),
        in_specs=[hbm] * 3 + [VMEM],
        out_specs=(VMEM,) * 3,
        scratch_shapes=[pltpu.SemaphoreType.DMA((3,))],
        compiler_params=LIMIT,
        name="load",
    )(basis, sample_cell[0].T, sample_count, to_outer)
    flat = loaded.reshape(modes, cells)

    block = slots * rows
    relative = [sum(((place >> (steps - 1 - step)) & 1) << step for step in range(steps)) for place in range(devices)]
    block = slots * rows
    share = devices // DIRECT * block
    room = round_up(share, 16)
    table = np.full((DIRECT * room, 8), -1, np.int32)
    in_block = np.arange(block)
    for place in range(devices):
        turned = (((place & 1) << (steps - 1)) + (place >> 1)) * block + in_block
        at = slice(place * block, (place + 1) * block)
        table[at, 0] = turned
        table[at, 1] = relative[place]
        table[at, 2] = (in_block // slots) * samples + (in_block % slots) * devices
        table[at, 3] = sum(((place >> step) & 1) << to for step, to in enumerate(places(steps)))
        table[at, 4] = in_block
        start = place * block // share * room + place * block % share
        table[start : start + block, 5] = turned
    table = jnp.asarray(table)

    acc, edge, got_in, center, cell = pl.pallas_call(
        functools.partial(local_kernel, (params, layers, width_y, width_z, plane, samples)),
        out_shape=(
            shape((params * MB, cells), F32),
            shape((params, width_y, width_z), F32),
            shape((OFFSETS * samples, MB), BF16),
            shape((samples, cells), BF16),
            shape((samples, 1), I32),
        ),
        in_specs=[VMEM] * 7,
        out_specs=(VMEM,) * 5,
        scratch_shapes=[
            pltpu.VMEM((params, layers, OFFSETS, width_y, width_z), F32),
            pltpu.VMEM((OFFSETS * samples, cells), BF16),
        ],
        compiler_params=LIMIT,
        cost_estimate=SMALL,
        name="local_stencil",
    )(flat, face_speed, face_diffusion, upwind_flag, reaction, cells_in, counts_in)

    finish_scratch = [
        pltpu.VMEM((params * MB, plane), BF16),
        pltpu.VMEM((2, tail, width_z), F32),
        pltpu.VMEM((MB * width_y, width_z), F32),
        pltpu.VMEM((MB, plane), BF16),
    ]
    near_sums, near_picks, near_side = pl.pallas_call(
        functools.partial(near_kernel, (params, layers, width_y, width_z, plane, samples)),
        out_shape=(
            shape((modes, params * MB), F32),
            shape((samples, params * MB), F32),
            shape((samples, MB), BF16),
        ),
        in_specs=[VMEM] * 7,
        out_specs=(VMEM,) * 3,
        scratch_shapes=finish_scratch,
        compiler_params=LIMIT,
        cost_estimate=SMALL,
        name="near_layer",
    )(flat, low, high, acc, edge, center, cell)

    size = own * params
    half = devices // 2
    count = half * block
    keep, keep_rows, packet = pl.pallas_call(
        functools.partial(
            project_kernel,
            (params, layers, width_y, width_z, plane, samples, devices, own),
            relative,
        ),
        out_shape=(
            shape((half * size, MB), F32),
            shape((count, MB), BF16),
            shape((2 * half * size + count, MB), BF16),
        ),
        in_specs=[VMEM] * 11,
        out_specs=(VMEM,) * 3,
        scratch_shapes=[pltpu.VMEM((params * modes, MB), F32)] + finish_scratch,
        compiler_params=LIMIT,
        name="project",
    )(
        flat,
        outer,
        acc,
        edge,
        got_in,
        center,
        near_sums,
        near_picks,
        near_side,
        cell,
        table,
    )

    wide = True
    for step in range(steps - 2):
        got = lax.ppermute(packet, "cells", [(i, i ^ (1 << step)) for i in range(devices)])
        if step < steps - 3:
            next_wide = step + 1 > NARROW_STEPS
            half //= 2
            packet_rows = (2 if next_wide else 1) * half * size + count
            keep, keep_rows, packet = pl.pallas_call(
                functools.partial(merge_kernel, wide, next_wide),
                out_shape=(
                    shape((half * size, MB), F32),
                    shape((count, MB), BF16),
                    shape((packet_rows, MB), BF16),
                ),
                in_specs=[VMEM] * 4,
                out_specs=(VMEM,) * 3,
                compiler_params=LIMIT,
                name="merge",
            )(keep, keep_rows, got, table)
            wide = next_wide
    sent = shape((size + room, MB), BF16)
    keep, keep_rows, *packets = pl.pallas_call(
        functools.partial(spread_kernel, wide, room),
        out_shape=(shape((size, MB), F32), shape((room, MB), BF16)) + (sent,) * (DIRECT - 1),
        in_specs=[VMEM] * 4,
        out_specs=(VMEM,) * (DIRECT + 1),
        compiler_params=LIMIT,
        name="spread",
    )(keep, keep_rows, got, table)
    got = [None] * DIRECT
    for at in ORDER:
        mask = ((at >> 1) << (steps - 2)) | ((at & 1) << (steps - 1))
        got[at] = lax.ppermute(packets[at - 1], "cells", [(i, i ^ mask) for i in range(devices)])
    volume = 1.0 / (layers * devices * width_y * width_z)
    summed, sampled = pl.pallas_call(
        functools.partial(final_kernel, volume, steps, block),
        out_shape=(shape((size, MB), F32), shape((2 * count, MB), BF16)),
        in_specs=[VMEM] * (DIRECT + 2),
        out_specs=(VMEM,) * 2,
        compiler_params=LIMIT,
        name="finish",
    )(keep, keep_rows, *[got[at] for at in ORDER], table)
    galerkin = summed.reshape(own, params, MB)
    sampled = sampled.reshape(devices, rows, slots, MB)
    return (galerkin, jnp.transpose(sampled, (0, 2, 1, 3))[None])


def solution(mesh):
    return jax.shard_map(
        shards,
        mesh=mesh,
        in_specs=(
            P(None, ("groups", "cells"), None, None),
            P(None, None, ("groups", "cells"), None, None),
            P(None, None, ("groups", "cells"), None, None),
            P(None, None, ("groups", "cells"), None, None),
            P(None, ("groups", "cells"), None, None),
            P(("groups", "cells"), None, None),
            P(("groups", "cells"), None),
        ),
        out_specs=(
            P(("groups", "cells"), None, None),
            P(("groups", "cells"), None, None, None, None),
        ),
        check_vma=False,
    )
```

```python
import functools

import jax
import jax.numpy as jnp
import numpy as np
from jax import lax
from jax.experimental import pallas as pl
from jax.experimental.pallas import tpu as pltpu
from jax.sharding import PartitionSpec as P

MB = 128
SPLITS = 3
NARROW_STEPS = 1
DIRECT = 4
ORDER = (3, 2, 1)
BF16 = jnp.bfloat16
F32 = jnp.float32
I32 = jnp.int32
OFFSETS = 7
VMEM = pl.BlockSpec(memory_space=pltpu.VMEM)
SMALL = pl.CostEstimate(flops=1, bytes_accessed=1, transcendentals=0)
LIMIT = pltpu.CompilerParams(vmem_limit_bytes=20 * 1024 * 1024)


def nt_dot(left, right):
    return lax.dot_general(left, right, (((1,), (1,)), ((), ())), preferred_element_type=F32)


def picked(targets, start, count):
    lanes = lax.broadcasted_iota(I32, (1, count), 1) + start
    return jnp.where(targets == lanes, 1.0, 0.0).astype(BF16)


def column(row):
    size = row.shape[1]
    down = lax.broadcasted_iota(I32, (size, size), 0)
    across = lax.broadcasted_iota(I32, (size, size), 1)
    spread = jnp.where(down == across, row.astype(F32), 0.0)
    return jnp.sum(spread, axis=1, keepdims=True).astype(I32)


def round_up(value, multiple):
    return -(-value // multiple) * multiple


def halves(value):
    head = value.astype(BF16)
    return head, (value - head.astype(F32)).astype(BF16)


def core():
    return lax.rem(lax.axis_index("cells"), 2)


def face_parts(speed, diff, flag):
    parts = []
    for value in (jnp.where(flag == 1, speed, -speed), diff):
        for _ in range(SPLITS):
            head = value.astype(BF16)
            value = value - head.astype(F32)
            parts.append(head)
    return parts


def pack_kernel(dims, basis_ref, speed_ref, diff_ref, flag_ref, low_ref, high_ref, outer_ref, speed_buf, diff_buf, flag_buf, sems):
    params, layers = dims
    last = layers - 1
    half = MB // 2
    block = pl.ds(0, MB)
    low, high = pl.ds(0, half), pl.ds(half, half)
    beside = (1 - core()) * last
    layers_out = [
        pltpu.make_async_copy(basis_ref.at[block, core() * last], outer_ref.at[block], sems.at[0]),
        pltpu.make_async_copy(basis_ref.at[low, beside], low_ref.at[low], sems.at[1]),
        pltpu.make_async_copy(basis_ref.at[high, beside], high_ref, sems.at[5]),
    ]
    copies = [
        pltpu.make_async_copy(speed_ref.at[:, 0, last], speed_buf, sems.at[2]),
        pltpu.make_async_copy(diff_ref.at[:, 0, last], diff_buf, sems.at[3]),
        pltpu.make_async_copy(flag_ref.at[:, 0, last], flag_buf, sems.at[4]),
    ]
    for copy in copies + layers_out:
        copy.start()
    for copy in copies:
        copy.wait()
    for at, part in enumerate(face_parts(speed_buf[...], diff_buf[...], flag_buf[...])):
        low_ref[half + at * params : half + (at + 1) * params] = part
        outer_ref[MB + at * params : MB + (at + 1) * params] = part
    for copy in layers_out:
        copy.wait()


def load_kernel(basis_ref, cell_ref, count_ref, after_ref, basis_out, cell_out, count_out, sems):
    del after_ref
    pairs = ((basis_ref, basis_out), (cell_ref, cell_out), (count_ref, count_out))
    copies = [pltpu.make_async_copy(source, out, sems.at[at]) for at, (source, out) in enumerate(pairs)]
    for copy in copies:
        copy.start()
    for copy in copies:
        copy.wait()


def local_kernel(
    dims,
    flat_ref,
    speed_ref,
    diff_ref,
    flag_ref,
    react_ref,
    sampled_ref,
    count_ref,
    acc_ref,
    edge_ref,
    in_ref,
    center_ref,
    cell_ref,
    coef_ref,
    pick_ref,
):
    params, layers, width_y, width_z, plane, samples = dims
    y_at = lax.broadcasted_iota(I32, (width_y, width_z), 0)
    z_at = lax.broadcasted_iota(I32, (width_y, width_z), 1)
    for param in range(params):
        uppers, nexts = [], []
        for layer in range(layers):
            up_d, next_d = [], []
            for axis_d in range(3):
                forward = flag_ref[param, axis_d, layer] == 1
                speed = speed_ref[param, axis_d, layer]
                diff = diff_ref[param, axis_d, layer]
                up_d.append(jnp.where(forward, speed, 0.0) + diff)
                next_d.append(jnp.where(forward, 0.0, -speed) - diff)
            uppers.append(up_d)
            nexts.append(next_d)
        edge_ref[param] = nexts[layers - 1][0]
        for layer in range(layers):
            diag = react_ref[param, layer]
            diag = diag + uppers[layer][0] + uppers[layer][1] + uppers[layer][2]
            if layer > 0:
                diag = diag - nexts[layer - 1][0]
                coef_ref[param, layer, 2] = -uppers[layer - 1][0]
            coef_ref[param, layer, 1] = nexts[layer][0]
            for axis_d, at, shift_axis, size in ((1, y_at, 0, width_y), (2, z_at, 1, width_z)):
                up, following = uppers[layer][axis_d], nexts[layer][axis_d]
                low_up = jnp.where(at == 0, 0.0, pltpu.roll(up, 1, shift_axis))
                low_next = jnp.where(at == 0, 0.0, pltpu.roll(following, 1, shift_axis))
                diag = diag - low_next
                coef_ref[param, layer, 1 + 2 * axis_d] = jnp.where(at == size - 1, 0.0, following)
                coef_ref[param, layer, 2 + 2 * axis_d] = -low_up
            coef_ref[param, layer, 0] = diag

    def tile(layer, y):
        start = layer * plane + y * width_z
        return flat_ref[:MB, start : start + width_z].astype(F32)

    for layer in range(layers):
        for y in range(width_y):
            start = layer * plane + y * width_z
            state = tile(layer, y)
            terms = [(0, state), (5, pltpu.roll(state, width_z - 1, 1)), (6, pltpu.roll(state, 1, 1))]
            if layer < layers - 1:
                terms.append((1, tile(layer + 1, y)))
            if layer > 0:
                terms.append((2, tile(layer - 1, y)))
            if y < width_y - 1:
                terms.append((3, tile(layer, y + 1)))
            if y > 0:
                terms.append((4, tile(layer, y - 1)))
            for param in range(params):
                total = None
                for at, term in terms:
                    product = coef_ref[param, layer, at, y : y + 1, :] * term
                    total = product if total is None else total + product
                acc_ref[param * MB : (param + 1) * MB, start : start + width_z] = total

    count = column(count_ref[...])
    slots = sampled_ref.shape[0]
    held = []
    for slot in range(slots):
        held.append(jnp.where(slot < count, column(sampled_ref[slot : slot + 1]), -4 * layers * plane))
    cell = jnp.concatenate(held, axis=0)
    cell_ref[...] = cell
    z_of = lax.broadcasted_iota(I32, (1, width_z), 1)
    for layer in range(layers):
        for y in range(width_y):
            start = layer * plane + y * width_z
            away = z_of - (cell - start)
            hits = [away == 0, away == -plane, away == plane]
            hits.append(away == -width_z if y < width_y - 1 else None)
            hits.append(away == width_z if y > 0 else None)
            hits.append((away == -1) & (z_of < width_z - 1))
            hits.append((away == 1) & (z_of > 0))
            for at, hit in enumerate(hits):
                value = jnp.zeros((samples, width_z), BF16)
                if hit is not None:
                    value = jnp.where(hit, 1.0, 0.0).astype(BF16)
                pick_ref[at * samples : (at + 1) * samples, start : start + width_z] = value
    center_ref[...] = pick_ref[:samples]
    in_ref[...] = nt_dot(pick_ref[...], flat_ref[:MB, :]).astype(BF16)


def finish_layer(dims, from_next, layer, halo_refs, flat_ref, acc_ref, edge_ref, applied_ref, coef_ref, spread_ref, beside_ref):
    params, layers, width_y, width_z, plane = dims
    held = MB // len(halo_refs)
    faces = []
    for at in range(2 * SPLITS):
        part = halo_refs[0][held + at * params : held + (at + 1) * params].astype(F32)
        faces.append(part.reshape(params * width_y, width_z))
    signed = faces[0] + faces[1] + faces[2]
    diff = faces[3] + faces[4] + faces[5]
    edge = edge_ref[...].reshape(params * width_y, width_z)
    coef_ref[0] = jnp.where(from_next, edge, -(jnp.maximum(signed, 0.0) + diff))
    coef_ref[1] = jnp.where(from_next, 0.0, diff - jnp.minimum(signed, 0.0))
    size = held * width_y
    for at, halo_ref in enumerate(halo_refs):
        spread_ref[at * size : (at + 1) * size] = halo_ref[:held].astype(F32).reshape(size, width_z)
    for y in range(width_y):
        at = pl.multiple_of(layer * plane + y * width_z, width_z)
        lanes = slice(y * width_z, (y + 1) * width_z)
        state = flat_ref[:MB, pl.ds(at, width_z)].astype(F32)
        beside = spread_ref[pl.ds(y, MB, stride=width_y), :]
        beside_ref[:, lanes] = beside.astype(BF16)
        for param in range(params):
            modes = slice(param * MB, (param + 1) * MB)
            row = param * width_y + y
            total = acc_ref[modes, pl.ds(at, width_z)]
            total = total + coef_ref[1, row : row + 1, :] * state
            total = total + coef_ref[0, row : row + 1, :] * beside
            applied_ref[modes, lanes] = total.astype(BF16)


def near_kernel(dims, flat_ref, low_ref, high_ref, acc_ref, edge_ref, center_ref, cell_ref, sums_ref, picks_ref, side_ref, *scratch):
    params, layers, width_y, width_z, plane, samples = dims
    odd = core() == 1
    layer = (1 - core()) * (layers - 1)
    start = pl.multiple_of(layer * plane, plane)
    finish_layer(dims[:5], jnp.logical_not(odd), layer, (low_ref, high_ref), flat_ref, acc_ref, edge_ref, *scratch)
    applied_ref, beside_ref = scratch[0], scratch[3]
    sums_ref[...] = nt_dot(flat_ref[:, pl.ds(start, plane)], applied_ref[...])
    picks_ref[...] = nt_dot(center_ref[:, pl.ds(start, plane)], applied_ref[...])
    below = cell_ref[...]
    above = below - (layers - 1) * plane
    side_ref[...] = nt_dot(picked(jnp.where(odd, below, above), 0, plane), beside_ref[...]).astype(BF16)


def project_kernel(
    dims,
    relative,
    flat_ref,
    outer_ref,
    acc_ref,
    edge_ref,
    in_ref,
    center_ref,
    near_sums_ref,
    near_picks_ref,
    near_side_ref,
    cell_ref,
    table_ref,
    keep_ref,
    keep_rows_ref,
    packet_ref,
    sums_ref,
    *scratch,
):
    params, layers, width_y, width_z, plane, samples, devices, own = dims
    odd = core() == 1
    layer = core() * (layers - 1)
    lane = pl.multiple_of(layer * plane, plane)
    finish_layer(dims[:5], odd, layer, (outer_ref,), flat_ref, acc_ref, edge_ref, *scratch)
    applied_ref, beside_ref = scratch[0], scratch[3]

    sums = near_sums_ref[...] + nt_dot(flat_ref[:, pl.ds(lane, plane)], applied_ref[...])
    for param in range(params):
        sums_ref[pl.ds(param, sums.shape[0], stride=params), :] = sums[:, param * MB : (param + 1) * MB]
    size = own * params
    half = devices // 2
    me = lax.axis_index("cells")
    for place in range(devices):
        start = pl.multiple_of((me ^ relative[place]) * size, size)
        terms = sums_ref[pl.ds(start, size), :]
        if place < half:
            keep_ref[place * size : (place + 1) * size] = terms
        else:
            head, rest = halves(terms)
            at = (place - half) * size
            packet_ref[at : at + size] = head
            packet_ref[half * size + at : half * size + at + size] = rest

    picks = nt_dot(center_ref[:, pl.ds(lane, plane)], applied_ref[...])
    got_applied = (near_picks_ref[...] + picks).astype(BF16)
    below = cell_ref[...]
    above = below - (layers - 1) * plane
    far = nt_dot(picked(jnp.where(odd, above, below), 0, plane), beside_ref[...]).astype(BF16)
    near = near_side_ref[...]
    got_below = in_ref[samples : 2 * samples] + jnp.where(odd, near, far)
    got_above = in_ref[2 * samples : 3 * samples] + jnp.where(odd, far, near)
    pieces = [got_applied[:, param * MB : (param + 1) * MB] for param in range(params)]
    pieces += [in_ref[:samples], got_below, got_above, in_ref[3 * samples :]]
    gathered = jnp.concatenate(pieces, axis=0)
    total_rows = gathered.shape[0]
    order = picked((table_ref[:, 0:1] ^ me) + table_ref[:, 1:2], 0, gathered.shape[0])
    ordered = jnp.dot(order, gathered, preferred_element_type=F32).astype(BF16)
    count = ordered.shape[0] // 2
    keep_rows_ref[...] = ordered[:count]
    packet_ref[2 * half * size :] = ordered[count:]


def move_rows(rows, moves, from_ref, to_ref):
    block, pairs = moves
    from_ref[...] = rows.astype(F32)
    for new, old in pairs:
        to_ref[pl.ds(new, block), :] = from_ref[pl.ds(old, block), :]


def merge_kernel(wide_in, wide_out, moves, keep_ref, keep_rows_ref, got_ref, keep_out, rows_out, packet_out, from_ref, to_ref):
    size = keep_ref.shape[0]
    half = size // 2
    total = keep_ref[...] + got_ref[:size].astype(F32)
    if wide_in:
        total = total + got_ref[size : 2 * size].astype(F32)
    keep_out[...] = total[:half]
    if wide_out:
        head, rest = halves(total[half:])
        packet_out[:half] = head
        packet_out[half : 2 * half] = rest
    else:
        packet_out[:half] = total[half:].astype(BF16)
    count = keep_rows_ref.shape[0]
    rows = jnp.concatenate([keep_rows_ref[...], got_ref[got_ref.shape[0] - count :]], axis=0)
    move_rows(rows, moves, from_ref, to_ref)
    ordered = to_ref[...].astype(BF16)
    rows_out[...] = ordered[:count]
    packet_out[packet_out.shape[0] - count :] = ordered[count:]


def spread_kernel(wide_in, room, moves, keep_ref, keep_rows_ref, got_ref, keep_out, rows_out, *refs):
    size = keep_ref.shape[0]
    total = keep_ref[...] + got_ref[:size].astype(F32)
    if wide_in:
        total = total + got_ref[size : 2 * size].astype(F32)
    part = size // DIRECT
    count = keep_rows_ref.shape[0]
    rows = jnp.concatenate([keep_rows_ref[...], got_ref[got_ref.shape[0] - count :]], axis=0)
    packets_out, from_ref, to_ref = refs[:-2], refs[-2], refs[-1]
    to_ref[...] = jnp.zeros(to_ref.shape, F32)
    move_rows(rows, moves, from_ref, to_ref)
    ordered = to_ref[...].astype(BF16)
    keep_out[...] = total[:part]
    rows_out[...] = ordered[:room]
    for at, packet_out in enumerate(packets_out, 1):
        packet_out[:part] = total[at * part : (at + 1) * part].astype(BF16)
        packet_out[part:] = ordered[at * room : (at + 1) * room]


def final_kernel(volume, block, olds, keep_ref, keep_rows_ref, *refs):
    got_refs = refs[: DIRECT - 1]
    sum_out, rows_out, from_ref, to_ref = refs[DIRECT - 1 :]
    size = keep_ref.shape[0]
    total = keep_ref[...]
    rows = [keep_rows_ref[...]] + [None] * (DIRECT - 1)
    for at, got_ref in zip(ORDER, got_refs):
        total = total + got_ref[:size].astype(F32)
        rows[at] = got_ref[size:]
    sum_out[...] = volume * total
    me = lax.axis_index("cells")
    pairs = [((me ^ at) * block, old) for at, old in enumerate(olds)]
    move_rows(jnp.concatenate(rows, axis=0), (block, pairs), from_ref, to_ref)
    rows_out[...] = to_ref[...].astype(BF16)


def places(steps):
    return [steps - 3 - step for step in range(steps - 2)] + [steps - 1, steps - 2]


def shape(dims, dtype):
    return jax.ShapeDtypeStruct(dims, dtype)


def shards(basis, face_speed, face_diffusion, upwind_flag, reaction, sample_cell, sample_count):
    modes, layers, width_y, width_z = basis.shape
    params = face_speed.shape[0]
    devices = lax.axis_size("cells")
    slots = sample_cell.shape[2]
    plane = width_y * width_z
    cells = layers * plane
    own = modes // devices
    rows = params + OFFSETS
    samples = devices * slots
    steps = devices.bit_length() - 1

    tail = params * width_y
    hbm = pl.BlockSpec(memory_space=pltpu.HBM)
    planes = 2 * SPLITS * params
    to_low, to_high, to_outer = pl.pallas_call(
        functools.partial(pack_kernel, (params, layers)),
        out_shape=(
            shape((MB // 2 + planes, width_y, width_z), BF16),
            shape((MB // 2, width_y, width_z), BF16),
            shape((MB + planes, width_y, width_z), BF16),
        ),
        in_specs=[hbm] * 4,
        out_specs=(VMEM,) * 3,
        scratch_shapes=[
            pltpu.VMEM((params, width_y, width_z), F32),
            pltpu.VMEM((params, width_y, width_z), F32),
            pltpu.VMEM((params, width_y, width_z), I32),
            pltpu.SemaphoreType.DMA((6,)),
        ],
        compiler_params=LIMIT,
        name="pack_halo",
    )(*[pltpu.with_memory_space_constraint(value, pltpu.HBM) for value in (basis, face_speed, face_diffusion, upwind_flag)])
    inner_pairs = [(i, i ^ 1) for i in range(devices)]
    outer_pairs = []
    for i in range(1, devices - 1, 2):
        outer_pairs += [(i, i + 1), (i + 1, i)]
    low = lax.ppermute(to_low, "cells", inner_pairs)
    high = lax.ppermute(to_high, "cells", inner_pairs)
    outer = lax.ppermute(to_outer, "cells", outer_pairs)

    loaded, cells_in, counts_in = pl.pallas_call(
        load_kernel,
        out_shape=(shape(basis.shape, BF16), shape((slots, devices), I32), shape((1, devices), I32)),
        in_specs=[hbm] * 3 + [VMEM],
        out_specs=(VMEM,) * 3,
        scratch_shapes=[pltpu.SemaphoreType.DMA((3,))],
        compiler_params=LIMIT,
        name="load",
    )(pltpu.with_memory_space_constraint(basis, pltpu.HBM), sample_cell[0].T, sample_count, to_outer)
    flat = loaded.reshape(modes, cells)

    block = slots * rows
    relative = [sum(((place >> (steps - 1 - step)) & 1) << step for step in range(steps)) for place in range(devices)]
    block = slots * rows
    share = devices // DIRECT * block
    room = round_up(share, 16)
    in_block = np.arange(block)
    table = np.zeros((devices, block, 8), np.int32)
    turns, spreads, olds = [], [], []
    for place in range(devices):
        old = (((place & 1) << (steps - 1)) + (place >> 1)) * block
        turns.append((place * block, old))
        spreads.append((place * block // share * room + place * block % share, old))
        came = sum(((place >> step) & 1) << to for step, to in enumerate(places(steps)))
        olds.append(came * block // share * room + came * block % share)
        table[place, :, 0] = relative[place]
        table[place, :, 1] = (in_block // slots) * samples + (in_block % slots) * devices
    table = jnp.asarray(table.reshape(devices * block, 8))

    acc, edge, got_in, center, cell = pl.pallas_call(
        functools.partial(local_kernel, (params, layers, width_y, width_z, plane, samples)),
        out_shape=(
            shape((params * MB, cells), F32),
            shape((params, width_y, width_z), F32),
            shape((OFFSETS * samples, MB), BF16),
            shape((samples, cells), BF16),
            shape((samples, 1), I32),
        ),
        in_specs=[VMEM] * 7,
        out_specs=(VMEM,) * 5,
        scratch_shapes=[
            pltpu.VMEM((params, layers, OFFSETS, width_y, width_z), F32),
            pltpu.VMEM((OFFSETS * samples, cells), BF16),
        ],
        compiler_params=LIMIT,
        cost_estimate=SMALL,
        name="local_stencil",
    )(flat, face_speed, face_diffusion, upwind_flag, reaction, cells_in, counts_in)

    finish_scratch = [
        pltpu.VMEM((params * MB, plane), BF16),
        pltpu.VMEM((2, tail, width_z), F32),
        pltpu.VMEM((MB * width_y, width_z), F32),
        pltpu.VMEM((MB, plane), BF16),
    ]
    near_sums, near_picks, near_side = pl.pallas_call(
        functools.partial(near_kernel, (params, layers, width_y, width_z, plane, samples)),
        out_shape=(
            shape((modes, params * MB), F32),
            shape((samples, params * MB), F32),
            shape((samples, MB), BF16),
        ),
        in_specs=[VMEM] * 7,
        out_specs=(VMEM,) * 3,
        scratch_shapes=finish_scratch,
        compiler_params=LIMIT,
        cost_estimate=SMALL,
        name="near_layer",
    )(flat, low, high, acc, edge, center, cell)

    size = own * params
    half = devices // 2
    count = half * block
    keep, keep_rows, packet = pl.pallas_call(
        functools.partial(
            project_kernel,
            (params, layers, width_y, width_z, plane, samples, devices, own),
            relative,
        ),
        out_shape=(
            shape((half * size, MB), F32),
            shape((count, MB), BF16),
            shape((2 * half * size + count, MB), BF16),
        ),
        in_specs=[VMEM] * 11,
        out_specs=(VMEM,) * 3,
        scratch_shapes=[pltpu.VMEM((params * modes, MB), F32)] + finish_scratch,
        compiler_params=LIMIT,
        name="project",
    )(
        flat,
        outer,
        acc,
        edge,
        got_in,
        center,
        near_sums,
        near_picks,
        near_side,
        cell,
        table,
    )

    wide = True
    for step in range(steps - 2):
        got = lax.ppermute(packet, "cells", [(i, i ^ (1 << step)) for i in range(devices)])
        if step < steps - 3:
            next_wide = step + 1 > NARROW_STEPS
            half //= 2
            packet_rows = (2 if next_wide else 1) * half * size + count
            keep, keep_rows, packet = pl.pallas_call(
                functools.partial(merge_kernel, wide, next_wide, (block, turns)),
                out_shape=(
                    shape((half * size, MB), F32),
                    shape((count, MB), BF16),
                    shape((packet_rows, MB), BF16),
                ),
                in_specs=[VMEM] * 3,
                out_specs=(VMEM,) * 3,
                scratch_shapes=[pltpu.VMEM((2 * count, MB), F32), pltpu.VMEM((2 * count, MB), F32)],
                compiler_params=LIMIT,
                name="merge",
            )(keep, keep_rows, got)
            wide = next_wide
    sent = shape((size + room, MB), BF16)
    keep, keep_rows, *packets = pl.pallas_call(
        functools.partial(spread_kernel, wide, room, (block, spreads)),
        out_shape=(shape((size, MB), F32), shape((room, MB), BF16)) + (sent,) * (DIRECT - 1),
        in_specs=[VMEM] * 3,
        out_specs=(VMEM,) * (DIRECT + 1),
        scratch_shapes=[pltpu.VMEM((2 * count, MB), F32), pltpu.VMEM((DIRECT * room, MB), F32)],
        compiler_params=LIMIT,
        name="spread",
    )(keep, keep_rows, got)
    got = [None] * DIRECT
    for at in ORDER:
        mask = ((at >> 1) << (steps - 2)) | ((at & 1) << (steps - 1))
        got[at] = lax.ppermute(packets[at - 1], "cells", [(i, i ^ mask) for i in range(devices)])
    volume = 1.0 / (layers * devices * width_y * width_z)
    summed, sampled = pl.pallas_call(
        functools.partial(final_kernel, volume, block, olds),
        out_shape=(shape((size, MB), F32), shape((2 * count, MB), BF16)),
        in_specs=[VMEM] * (DIRECT + 1),
        out_specs=(VMEM,) * 2,
        scratch_shapes=[pltpu.VMEM((DIRECT * room, MB), F32), pltpu.VMEM((2 * count, MB), F32)],
        compiler_params=LIMIT,
        name="finish",
    )(keep, keep_rows, *[got[at] for at in ORDER])
    galerkin = summed.reshape(own, params, MB)
    sampled = sampled.reshape(devices, rows, slots, MB)
    return (galerkin, jnp.transpose(sampled, (0, 2, 1, 3))[None])


def solution(mesh):
    return jax.shard_map(
        shards,
        mesh=mesh,
        in_specs=(
            P(None, ("groups", "cells"), None, None),
            P(None, None, ("groups", "cells"), None, None),
            P(None, None, ("groups", "cells"), None, None),
            P(None, None, ("groups", "cells"), None, None),
            P(None, ("groups", "cells"), None, None),
            P(("groups", "cells"), None, None),
            P(("groups", "cells"), None),
        ),
        out_specs=(
            P(("groups", "cells"), None, None),
            P(("groups", "cells"), None, None, None, None),
        ),
        check_vma=False,
    )
```

```python
import functools

import jax
import jax.numpy as jnp
import numpy as np
from jax import lax
from jax.experimental import pallas as pl
from jax.experimental.pallas import tpu as pltpu
from jax.sharding import PartitionSpec as P

MB = 128
SPLITS = 3
NARROW_STEPS = 1
DIRECT = 4
ORDER = (3, 2, 1)
BF16 = jnp.bfloat16
F32 = jnp.float32
I32 = jnp.int32
OFFSETS = 7
VMEM = pl.BlockSpec(memory_space=pltpu.VMEM)
SMALL = pl.CostEstimate(flops=1, bytes_accessed=1, transcendentals=0)
LIMIT = pltpu.CompilerParams(vmem_limit_bytes=20 * 1024 * 1024)


def nt_dot(left, right):
    return lax.dot_general(left, right, (((1,), (1,)), ((), ())), preferred_element_type=F32)


def picked(targets, start, count):
    lanes = lax.broadcasted_iota(I32, (1, count), 1) + start
    return jnp.where(targets == lanes, 1.0, 0.0).astype(BF16)


def column(row):
    size = row.shape[1]
    down = lax.broadcasted_iota(I32, (size, size), 0)
    across = lax.broadcasted_iota(I32, (size, size), 1)
    spread = jnp.where(down == across, row.astype(F32), 0.0)
    return jnp.sum(spread, axis=1, keepdims=True).astype(I32)


def round_up(value, multiple):
    return -(-value // multiple) * multiple


def halves(value):
    head = value.astype(BF16)
    return head, (value - head.astype(F32)).astype(BF16)


def core():
    return lax.rem(lax.axis_index("cells"), 2)


def face_parts(speed, diff, flag):
    parts = []
    for value in (jnp.where(flag == 1, speed, -speed), diff):
        for _ in range(SPLITS):
            head = value.astype(BF16)
            value = value - head.astype(F32)
            parts.append(head)
    return parts


def pack_kernel(dims, basis_ref, speed_ref, diff_ref, flag_ref, low_ref, high_ref, outer_ref, speed_buf, diff_buf, flag_buf, sems):
    params, layers = dims
    last = layers - 1
    half = MB // 2
    block = pl.ds(0, MB)
    low, high = pl.ds(0, half), pl.ds(half, half)
    beside = (1 - core()) * last
    layers_out = [
        pltpu.make_async_copy(basis_ref.at[block, core() * last], outer_ref.at[block], sems.at[0]),
        pltpu.make_async_copy(basis_ref.at[low, beside], low_ref.at[low], sems.at[1]),
        pltpu.make_async_copy(basis_ref.at[high, beside], high_ref, sems.at[5]),
    ]
    copies = [
        pltpu.make_async_copy(speed_ref.at[:, 0, last], speed_buf, sems.at[2]),
        pltpu.make_async_copy(diff_ref.at[:, 0, last], diff_buf, sems.at[3]),
        pltpu.make_async_copy(flag_ref.at[:, 0, last], flag_buf, sems.at[4]),
    ]
    for copy in copies + layers_out:
        copy.start()
    for copy in copies:
        copy.wait()
    for at, part in enumerate(face_parts(speed_buf[...], diff_buf[...], flag_buf[...])):
        low_ref[half + at * params : half + (at + 1) * params] = part
        outer_ref[MB + at * params : MB + (at + 1) * params] = part
    for copy in layers_out:
        copy.wait()


def load_kernel(basis_ref, cell_ref, count_ref, after_ref, basis_out, cell_out, count_out, sems):
    del after_ref
    pairs = ((basis_ref, basis_out), (cell_ref, cell_out), (count_ref, count_out))
    copies = [pltpu.make_async_copy(source, out, sems.at[at]) for at, (source, out) in enumerate(pairs)]
    for copy in copies:
        copy.start()
    for copy in copies:
        copy.wait()


def local_kernel(
    dims,
    flat_ref,
    speed_ref,
    diff_ref,
    flag_ref,
    react_ref,
    sampled_ref,
    count_ref,
    acc_ref,
    edge_ref,
    in_ref,
    center_ref,
    cell_ref,
    coef_ref,
    pick_ref,
):
    params, layers, width_y, width_z, plane, samples = dims
    y_at = lax.broadcasted_iota(I32, (width_y, width_z), 0)
    z_at = lax.broadcasted_iota(I32, (width_y, width_z), 1)
    for param in range(params):
        uppers, nexts = [], []
        for layer in range(layers):
            up_d, next_d = [], []
            for axis_d in range(3):
                forward = flag_ref[param, axis_d, layer] == 1
                speed = speed_ref[param, axis_d, layer]
                diff = diff_ref[param, axis_d, layer]
                up_d.append(jnp.where(forward, speed, 0.0) + diff)
                next_d.append(jnp.where(forward, 0.0, -speed) - diff)
            uppers.append(up_d)
            nexts.append(next_d)
        edge_ref[param] = nexts[layers - 1][0]
        for layer in range(layers):
            diag = react_ref[param, layer]
            diag = diag + uppers[layer][0] + uppers[layer][1] + uppers[layer][2]
            if layer > 0:
                diag = diag - nexts[layer - 1][0]
                coef_ref[param, layer, 2] = -uppers[layer - 1][0]
            coef_ref[param, layer, 1] = nexts[layer][0]
            for axis_d, at, shift_axis, size in ((1, y_at, 0, width_y), (2, z_at, 1, width_z)):
                up, following = uppers[layer][axis_d], nexts[layer][axis_d]
                low_up = jnp.where(at == 0, 0.0, pltpu.roll(up, 1, shift_axis))
                low_next = jnp.where(at == 0, 0.0, pltpu.roll(following, 1, shift_axis))
                diag = diag - low_next
                coef_ref[param, layer, 1 + 2 * axis_d] = jnp.where(at == size - 1, 0.0, following)
                coef_ref[param, layer, 2 + 2 * axis_d] = -low_up
            coef_ref[param, layer, 0] = diag

    def tile(layer, y):
        start = layer * plane + y * width_z
        return flat_ref[:MB, start : start + width_z].astype(F32)

    for layer in range(layers):
        for y in range(width_y):
            start = layer * plane + y * width_z
            state = tile(layer, y)
            terms = [(0, state), (5, pltpu.roll(state, width_z - 1, 1)), (6, pltpu.roll(state, 1, 1))]
            if layer < layers - 1:
                terms.append((1, tile(layer + 1, y)))
            if layer > 0:
                terms.append((2, tile(layer - 1, y)))
            if y < width_y - 1:
                terms.append((3, tile(layer, y + 1)))
            if y > 0:
                terms.append((4, tile(layer, y - 1)))
            for param in range(params):
                total = None
                for at, term in terms:
                    product = coef_ref[param, layer, at, y : y + 1, :] * term
                    total = product if total is None else total + product
                acc_ref[param * MB : (param + 1) * MB, start : start + width_z] = total

    count = column(count_ref[...])
    slots = sampled_ref.shape[0]
    held = []
    for slot in range(slots):
        held.append(jnp.where(slot < count, column(sampled_ref[slot : slot + 1]), -4 * layers * plane))
    cell = jnp.concatenate(held, axis=0)
    cell_ref[...] = cell
    z_of = lax.broadcasted_iota(I32, (1, width_z), 1)
    for layer in range(layers):
        for y in range(width_y):
            start = layer * plane + y * width_z
            away = z_of - (cell - start)
            hits = [away == 0, away == -plane, away == plane]
            hits.append(away == -width_z if y < width_y - 1 else None)
            hits.append(away == width_z if y > 0 else None)
            hits.append((away == -1) & (z_of < width_z - 1))
            hits.append((away == 1) & (z_of > 0))
            for at, hit in enumerate(hits):
                value = jnp.zeros((samples, width_z), BF16)
                if hit is not None:
                    value = jnp.where(hit, 1.0, 0.0).astype(BF16)
                pick_ref[at * samples : (at + 1) * samples, start : start + width_z] = value
    center_ref[...] = pick_ref[:samples]
    in_ref[...] = nt_dot(pick_ref[...], flat_ref[:MB, :]).astype(BF16)


def finish_layer(dims, from_next, layer, halo_refs, flat_ref, acc_ref, edge_ref, applied_ref, coef_ref, spread_ref, beside_ref):
    params, layers, width_y, width_z, plane = dims
    held = MB // len(halo_refs)
    faces = []
    for at in range(2 * SPLITS):
        part = halo_refs[0][held + at * params : held + (at + 1) * params].astype(F32)
        faces.append(part.reshape(params * width_y, width_z))
    signed = faces[0] + faces[1] + faces[2]
    diff = faces[3] + faces[4] + faces[5]
    edge = edge_ref[...].reshape(params * width_y, width_z)
    coef_ref[0] = jnp.where(from_next, edge, -(jnp.maximum(signed, 0.0) + diff))
    coef_ref[1] = jnp.where(from_next, 0.0, diff - jnp.minimum(signed, 0.0))
    size = held * width_y
    for at, halo_ref in enumerate(halo_refs):
        spread_ref[at * size : (at + 1) * size] = halo_ref[:held].astype(F32).reshape(size, width_z)
    for y in range(width_y):
        at = pl.multiple_of(layer * plane + y * width_z, width_z)
        lanes = slice(y * width_z, (y + 1) * width_z)
        state = flat_ref[:MB, pl.ds(at, width_z)].astype(F32)
        beside = spread_ref[pl.ds(y, MB, stride=width_y), :]
        beside_ref[:, lanes] = beside.astype(BF16)
        for param in range(params):
            modes = slice(param * MB, (param + 1) * MB)
            row = param * width_y + y
            total = acc_ref[modes, pl.ds(at, width_z)]
            total = total + coef_ref[1, row : row + 1, :] * state
            total = total + coef_ref[0, row : row + 1, :] * beside
            applied_ref[modes, lanes] = total.astype(BF16)


def near_kernel(dims, flat_ref, low_ref, high_ref, acc_ref, edge_ref, center_ref, cell_ref, sums_ref, picks_ref, side_ref, *scratch):
    params, layers, width_y, width_z, plane, samples = dims
    odd = core() == 1
    layer = (1 - core()) * (layers - 1)
    start = pl.multiple_of(layer * plane, plane)
    finish_layer(dims[:5], jnp.logical_not(odd), layer, (low_ref, high_ref), flat_ref, acc_ref, edge_ref, *scratch)
    applied_ref, beside_ref = scratch[0], scratch[3]
    sums_ref[...] = nt_dot(flat_ref[:, pl.ds(start, plane)], applied_ref[...])
    picks_ref[...] = nt_dot(center_ref[:, pl.ds(start, plane)], applied_ref[...])
    below = cell_ref[...]
    above = below - (layers - 1) * plane
    side_ref[...] = nt_dot(picked(jnp.where(odd, below, above), 0, plane), beside_ref[...]).astype(BF16)


def project_kernel(
    dims,
    relative,
    flat_ref,
    outer_ref,
    acc_ref,
    edge_ref,
    in_ref,
    center_ref,
    near_sums_ref,
    near_picks_ref,
    near_side_ref,
    cell_ref,
    table_ref,
    keep_ref,
    keep_rows_ref,
    packet_ref,
    sums_ref,
    *scratch,
):
    params, layers, width_y, width_z, plane, samples, devices, own = dims
    odd = core() == 1
    layer = core() * (layers - 1)
    lane = pl.multiple_of(layer * plane, plane)
    finish_layer(dims[:5], odd, layer, (outer_ref,), flat_ref, acc_ref, edge_ref, *scratch)
    applied_ref, beside_ref = scratch[0], scratch[3]

    sums = near_sums_ref[...] + nt_dot(flat_ref[:, pl.ds(lane, plane)], applied_ref[...])
    for param in range(params):
        sums_ref[pl.ds(param, sums.shape[0], stride=params), :] = sums[:, param * MB : (param + 1) * MB]
    size = own * params
    half = devices // 2
    me = lax.axis_index("cells")
    for place in range(devices):
        start = pl.multiple_of((me ^ relative[place]) * size, size)
        terms = sums_ref[pl.ds(start, size), :]
        if place < half:
            keep_ref[place * size : (place + 1) * size] = terms
        else:
            at = (place - half) * size
            packet_ref[at : at + size] = terms.astype(BF16)

    picks = nt_dot(center_ref[:, pl.ds(lane, plane)], applied_ref[...])
    got_applied = (near_picks_ref[...] + picks).astype(BF16)
    below = cell_ref[...]
    above = below - (layers - 1) * plane
    far = nt_dot(picked(jnp.where(odd, above, below), 0, plane), beside_ref[...]).astype(BF16)
    near = near_side_ref[...]
    got_below = in_ref[samples : 2 * samples] + jnp.where(odd, near, far)
    got_above = in_ref[2 * samples : 3 * samples] + jnp.where(odd, far, near)
    pieces = [got_applied[:, param * MB : (param + 1) * MB] for param in range(params)]
    pieces += [in_ref[:samples], got_below, got_above, in_ref[3 * samples :]]
    gathered = jnp.concatenate(pieces, axis=0)
    total_rows = gathered.shape[0]
    order = picked((table_ref[:, 0:1] ^ me) + table_ref[:, 1:2], 0, gathered.shape[0])
    ordered = jnp.dot(order, gathered, preferred_element_type=F32).astype(BF16)
    count = ordered.shape[0] // 2
    keep_rows_ref[...] = ordered[:count]
    packet_ref[half * size :] = ordered[count:]


def move_rows(rows, moves, from_ref, to_ref):
    block, pairs = moves
    from_ref[...] = rows.astype(F32)
    for new, old in pairs:
        to_ref[pl.ds(new, block), :] = from_ref[pl.ds(old, block), :]


def merge_kernel(wide_in, wide_out, moves, keep_ref, keep_rows_ref, got_ref, keep_out, rows_out, packet_out, from_ref, to_ref):
    size = keep_ref.shape[0]
    half = size // 2
    total = keep_ref[...] + got_ref[:size].astype(F32)
    if wide_in:
        total = total + got_ref[size : 2 * size].astype(F32)
    keep_out[...] = total[:half]
    if wide_out:
        head, rest = halves(total[half:])
        packet_out[:half] = head
        packet_out[half : 2 * half] = rest
    else:
        packet_out[:half] = total[half:].astype(BF16)
    count = keep_rows_ref.shape[0]
    rows = jnp.concatenate([keep_rows_ref[...], got_ref[got_ref.shape[0] - count :]], axis=0)
    move_rows(rows, moves, from_ref, to_ref)
    ordered = to_ref[...].astype(BF16)
    rows_out[...] = ordered[:count]
    packet_out[packet_out.shape[0] - count :] = ordered[count:]


def spread_kernel(wide_in, room, moves, keep_ref, keep_rows_ref, got_ref, keep_out, rows_out, *refs):
    size = keep_ref.shape[0]
    total = keep_ref[...] + got_ref[:size].astype(F32)
    if wide_in:
        total = total + got_ref[size : 2 * size].astype(F32)
    part = size // DIRECT
    count = keep_rows_ref.shape[0]
    rows = jnp.concatenate([keep_rows_ref[...], got_ref[got_ref.shape[0] - count :]], axis=0)
    packets_out, from_ref, to_ref = refs[:-2], refs[-2], refs[-1]
    to_ref[...] = jnp.zeros(to_ref.shape, F32)
    move_rows(rows, moves, from_ref, to_ref)
    ordered = to_ref[...].astype(BF16)
    keep_out[...] = total[:part]
    rows_out[...] = ordered[:room]
    for at, packet_out in enumerate(packets_out, 1):
        packet_out[:part] = total[at * part : (at + 1) * part].astype(BF16)
        packet_out[part:] = ordered[at * room : (at + 1) * room]


def final_kernel(volume, block, olds, keep_ref, keep_rows_ref, *refs):
    got_refs = refs[: DIRECT - 1]
    sum_out, rows_out, from_ref, to_ref = refs[DIRECT - 1 :]
    size = keep_ref.shape[0]
    total = keep_ref[...]
    rows = [keep_rows_ref[...]] + [None] * (DIRECT - 1)
    for at, got_ref in zip(ORDER, got_refs):
        total = total + got_ref[:size].astype(F32)
        rows[at] = got_ref[size:]
    sum_out[...] = volume * total
    me = lax.axis_index("cells")
    pairs = [((me ^ at) * block, old) for at, old in enumerate(olds)]
    move_rows(jnp.concatenate(rows, axis=0), (block, pairs), from_ref, to_ref)
    rows_out[...] = to_ref[...].astype(BF16)


def places(steps):
    return [steps - 3 - step for step in range(steps - 2)] + [steps - 1, steps - 2]


def shape(dims, dtype):
    return jax.ShapeDtypeStruct(dims, dtype)


def shards(basis, face_speed, face_diffusion, upwind_flag, reaction, sample_cell, sample_count):
    modes, layers, width_y, width_z = basis.shape
    params = face_speed.shape[0]
    devices = lax.axis_size("cells")
    slots = sample_cell.shape[2]
    plane = width_y * width_z
    cells = layers * plane
    own = modes // devices
    rows = params + OFFSETS
    samples = devices * slots
    steps = devices.bit_length() - 1

    tail = params * width_y
    hbm = pl.BlockSpec(memory_space=pltpu.HBM)
    planes = 2 * SPLITS * params
    to_low, to_high, to_outer = pl.pallas_call(
        functools.partial(pack_kernel, (params, layers)),
        out_shape=(
            shape((MB // 2 + planes, width_y, width_z), BF16),
            shape((MB // 2, width_y, width_z), BF16),
            shape((MB + planes, width_y, width_z), BF16),
        ),
        in_specs=[hbm] * 4,
        out_specs=(VMEM,) * 3,
        scratch_shapes=[
            pltpu.VMEM((params, width_y, width_z), F32),
            pltpu.VMEM((params, width_y, width_z), F32),
            pltpu.VMEM((params, width_y, width_z), I32),
            pltpu.SemaphoreType.DMA((6,)),
        ],
        compiler_params=LIMIT,
        name="pack_halo",
    )(*[pltpu.with_memory_space_constraint(value, pltpu.HBM) for value in (basis, face_speed, face_diffusion, upwind_flag)])
    inner_pairs = [(i, i ^ 1) for i in range(devices)]
    outer_pairs = []
    for i in range(1, devices - 1, 2):
        outer_pairs += [(i, i + 1), (i + 1, i)]
    low = lax.ppermute(to_low, "cells", inner_pairs)
    high = lax.ppermute(to_high, "cells", inner_pairs)
    outer = lax.ppermute(to_outer, "cells", outer_pairs)

    loaded, cells_in, counts_in = pl.pallas_call(
        load_kernel,
        out_shape=(shape(basis.shape, BF16), shape((slots, devices), I32), shape((1, devices), I32)),
        in_specs=[hbm] * 3 + [VMEM],
        out_specs=(VMEM,) * 3,
        scratch_shapes=[pltpu.SemaphoreType.DMA((3,))],
        compiler_params=LIMIT,
        name="load",
    )(pltpu.with_memory_space_constraint(basis, pltpu.HBM), sample_cell[0].T, sample_count, to_outer)
    flat = loaded.reshape(modes, cells)

    block = slots * rows
    relative = [sum(((place >> (steps - 1 - step)) & 1) << step for step in range(steps)) for place in range(devices)]
    block = slots * rows
    share = devices // DIRECT * block
    room = round_up(share, 16)
    in_block = np.arange(block)
    table = np.zeros((devices, block, 8), np.int32)
    turns, spreads, olds = [], [], []
    for place in range(devices):
        old = (((place & 1) << (steps - 1)) + (place >> 1)) * block
        turns.append((place * block, old))
        spreads.append((place * block // share * room + place * block % share, old))
        came = sum(((place >> step) & 1) << to for step, to in enumerate(places(steps)))
        olds.append(came * block // share * room + came * block % share)
        table[place, :, 0] = relative[place]
        table[place, :, 1] = (in_block // slots) * samples + (in_block % slots) * devices
    table = jnp.asarray(table.reshape(devices * block, 8))

    acc, edge, got_in, center, cell = pl.pallas_call(
        functools.partial(local_kernel, (params, layers, width_y, width_z, plane, samples)),
        out_shape=(
            shape((params * MB, cells), F32),
            shape((params, width_y, width_z), F32),
            shape((OFFSETS * samples, MB), BF16),
            shape((samples, cells), BF16),
            shape((samples, 1), I32),
        ),
        in_specs=[VMEM] * 7,
        out_specs=(VMEM,) * 5,
        scratch_shapes=[
            pltpu.VMEM((params, layers, OFFSETS, width_y, width_z), F32),
            pltpu.VMEM((OFFSETS * samples, cells), BF16),
        ],
        compiler_params=LIMIT,
        cost_estimate=SMALL,
        name="local_stencil",
    )(flat, face_speed, face_diffusion, upwind_flag, reaction, cells_in, counts_in)

    finish_scratch = [
        pltpu.VMEM((params * MB, plane), BF16),
        pltpu.VMEM((2, tail, width_z), F32),
        pltpu.VMEM((MB * width_y, width_z), F32),
        pltpu.VMEM((MB, plane), BF16),
    ]
    near_sums, near_picks, near_side = pl.pallas_call(
        functools.partial(near_kernel, (params, layers, width_y, width_z, plane, samples)),
        out_shape=(
            shape((modes, params * MB), F32),
            shape((samples, params * MB), F32),
            shape((samples, MB), BF16),
        ),
        in_specs=[VMEM] * 7,
        out_specs=(VMEM,) * 3,
        scratch_shapes=finish_scratch,
        compiler_params=LIMIT,
        cost_estimate=SMALL,
        name="near_layer",
    )(flat, low, high, acc, edge, center, cell)

    size = own * params
    half = devices // 2
    count = half * block
    keep, keep_rows, packet = pl.pallas_call(
        functools.partial(
            project_kernel,
            (params, layers, width_y, width_z, plane, samples, devices, own),
            relative,
        ),
        out_shape=(
            shape((half * size, MB), F32),
            shape((count, MB), BF16),
            shape((half * size + count, MB), BF16),
        ),
        in_specs=[VMEM] * 11,
        out_specs=(VMEM,) * 3,
        scratch_shapes=[pltpu.VMEM((params * modes, MB), F32)] + finish_scratch,
        compiler_params=LIMIT,
        name="project",
    )(
        flat,
        outer,
        acc,
        edge,
        got_in,
        center,
        near_sums,
        near_picks,
        near_side,
        cell,
        table,
    )

    wide = False
    for step in range(steps - 2):
        got = lax.ppermute(packet, "cells", [(i, i ^ (1 << step)) for i in range(devices)])
        if step < steps - 3:
            next_wide = step + 1 > NARROW_STEPS
            half //= 2
            packet_rows = (2 if next_wide else 1) * half * size + count
            keep, keep_rows, packet = pl.pallas_call(
                functools.partial(merge_kernel, wide, next_wide, (block, turns)),
                out_shape=(
                    shape((half * size, MB), F32),
                    shape((count, MB), BF16),
                    shape((packet_rows, MB), BF16),
                ),
                in_specs=[VMEM] * 3,
                out_specs=(VMEM,) * 3,
                scratch_shapes=[pltpu.VMEM((2 * count, MB), F32), pltpu.VMEM((2 * count, MB), F32)],
                compiler_params=LIMIT,
                name="merge",
            )(keep, keep_rows, got)
            wide = next_wide
    sent = shape((size + room, MB), BF16)
    keep, keep_rows, *packets = pl.pallas_call(
        functools.partial(spread_kernel, wide, room, (block, spreads)),
        out_shape=(shape((size, MB), F32), shape((room, MB), BF16)) + (sent,) * (DIRECT - 1),
        in_specs=[VMEM] * 3,
        out_specs=(VMEM,) * (DIRECT + 1),
        scratch_shapes=[pltpu.VMEM((2 * count, MB), F32), pltpu.VMEM((DIRECT * room, MB), F32)],
        compiler_params=LIMIT,
        name="spread",
    )(keep, keep_rows, got)
    got = [None] * DIRECT
    for at in ORDER:
        mask = ((at >> 1) << (steps - 2)) | ((at & 1) << (steps - 1))
        got[at] = lax.ppermute(packets[at - 1], "cells", [(i, i ^ mask) for i in range(devices)])
    volume = 1.0 / (layers * devices * width_y * width_z)
    summed, sampled = pl.pallas_call(
        functools.partial(final_kernel, volume, block, olds),
        out_shape=(shape((size, MB), F32), shape((2 * count, MB), BF16)),
        in_specs=[VMEM] * (DIRECT + 1),
        out_specs=(VMEM,) * 2,
        scratch_shapes=[pltpu.VMEM((DIRECT * room, MB), F32), pltpu.VMEM((2 * count, MB), F32)],
        compiler_params=LIMIT,
        name="finish",
    )(keep, keep_rows, *[got[at] for at in ORDER])
    galerkin = summed.reshape(own, params, MB)
    sampled = sampled.reshape(devices, rows, slots, MB)
    return (galerkin, jnp.transpose(sampled, (0, 2, 1, 3))[None])


def solution(mesh):
    return jax.shard_map(
        shards,
        mesh=mesh,
        in_specs=(
            P(None, ("groups", "cells"), None, None),
            P(None, None, ("groups", "cells"), None, None),
            P(None, None, ("groups", "cells"), None, None),
            P(None, None, ("groups", "cells"), None, None),
            P(None, ("groups", "cells"), None, None),
            P(("groups", "cells"), None, None),
            P(("groups", "cells"), None),
        ),
        out_specs=(
            P(("groups", "cells"), None, None),
            P(("groups", "cells"), None, None, None, None),
        ),
        check_vma=False,
    )
```

```python
import functools

import jax
import jax.numpy as jnp
import numpy as np
from jax import lax
from jax.experimental import pallas as pl
from jax.experimental.pallas import tpu as pltpu
from jax.sharding import PartitionSpec as P

MB = 128
SPLITS = 2
NARROW_STEPS = 1
DIRECT = 4
ORDER = (3, 2, 1)
BF16 = jnp.bfloat16
F32 = jnp.float32
I32 = jnp.int32
OFFSETS = 7
VMEM = pl.BlockSpec(memory_space=pltpu.VMEM)
SMALL = pl.CostEstimate(flops=1, bytes_accessed=1, transcendentals=0)
LIMIT = pltpu.CompilerParams(vmem_limit_bytes=20 * 1024 * 1024)


def nt_dot(left, right):
    return lax.dot_general(left, right, (((1,), (1,)), ((), ())), preferred_element_type=F32)


def picked(targets, start, count):
    lanes = lax.broadcasted_iota(I32, (1, count), 1) + start
    return jnp.where(targets == lanes, 1.0, 0.0).astype(BF16)


def column(row):
    size = row.shape[1]
    down = lax.broadcasted_iota(I32, (size, size), 0)
    across = lax.broadcasted_iota(I32, (size, size), 1)
    spread = jnp.where(down == across, row.astype(F32), 0.0)
    return jnp.sum(spread, axis=1, keepdims=True).astype(I32)


def round_up(value, multiple):
    return -(-value // multiple) * multiple


def halves(value):
    head = value.astype(BF16)
    return head, (value - head.astype(F32)).astype(BF16)


def core():
    return lax.rem(lax.axis_index("cells"), 2)


def face_parts(speed, diff, flag):
    parts = []
    for value in (jnp.where(flag == 1, speed, -speed), diff):
        for _ in range(SPLITS):
            head = value.astype(BF16)
            value = value - head.astype(F32)
            parts.append(head)
    return parts


def pack_kernel(dims, basis_ref, speed_ref, diff_ref, flag_ref, low_ref, high_ref, outer_ref, speed_buf, diff_buf, flag_buf, sems):
    params, layers = dims
    last = layers - 1
    half = MB // 2
    block = pl.ds(0, MB)
    low, high = pl.ds(0, half), pl.ds(half, half)
    beside = (1 - core()) * last
    layers_out = [
        pltpu.make_async_copy(basis_ref.at[block, core() * last], outer_ref.at[block], sems.at[0]),
        pltpu.make_async_copy(basis_ref.at[low, beside], low_ref.at[low], sems.at[1]),
        pltpu.make_async_copy(basis_ref.at[high, beside], high_ref, sems.at[5]),
    ]
    copies = [
        pltpu.make_async_copy(speed_ref.at[:, 0, last], speed_buf, sems.at[2]),
        pltpu.make_async_copy(diff_ref.at[:, 0, last], diff_buf, sems.at[3]),
        pltpu.make_async_copy(flag_ref.at[:, 0, last], flag_buf, sems.at[4]),
    ]
    for copy in copies + layers_out:
        copy.start()
    for copy in copies:
        copy.wait()
    for at, part in enumerate(face_parts(speed_buf[...], diff_buf[...], flag_buf[...])):
        low_ref[half + at * params : half + (at + 1) * params] = part
        outer_ref[MB + at * params : MB + (at + 1) * params] = part
    for copy in layers_out:
        copy.wait()


def load_kernel(basis_ref, cell_ref, count_ref, after_ref, basis_out, cell_out, count_out, sems):
    del after_ref
    pairs = ((basis_ref, basis_out), (cell_ref, cell_out), (count_ref, count_out))
    copies = [pltpu.make_async_copy(source, out, sems.at[at]) for at, (source, out) in enumerate(pairs)]
    for copy in copies:
        copy.start()
    for copy in copies:
        copy.wait()


def local_kernel(
    dims,
    flat_ref,
    speed_ref,
    diff_ref,
    flag_ref,
    react_ref,
    sampled_ref,
    count_ref,
    acc_ref,
    edge_ref,
    in_ref,
    center_ref,
    cell_ref,
    coef_ref,
    pick_ref,
):
    params, layers, width_y, width_z, plane, samples = dims
    y_at = lax.broadcasted_iota(I32, (width_y, width_z), 0)
    z_at = lax.broadcasted_iota(I32, (width_y, width_z), 1)
    for param in range(params):
        uppers, nexts = [], []
        for layer in range(layers):
            up_d, next_d = [], []
            for axis_d in range(3):
                forward = flag_ref[param, axis_d, layer] == 1
                speed = speed_ref[param, axis_d, layer]
                diff = diff_ref[param, axis_d, layer]
                up_d.append(jnp.where(forward, speed, 0.0) + diff)
                next_d.append(jnp.where(forward, 0.0, -speed) - diff)
            uppers.append(up_d)
            nexts.append(next_d)
        edge_ref[param] = nexts[layers - 1][0]
        for layer in range(layers):
            diag = react_ref[param, layer]
            diag = diag + uppers[layer][0] + uppers[layer][1] + uppers[layer][2]
            if layer > 0:
                diag = diag - nexts[layer - 1][0]
                coef_ref[param, layer, 2] = -uppers[layer - 1][0]
            coef_ref[param, layer, 1] = nexts[layer][0]
            for axis_d, at, shift_axis, size in ((1, y_at, 0, width_y), (2, z_at, 1, width_z)):
                up, following = uppers[layer][axis_d], nexts[layer][axis_d]
                low_up = jnp.where(at == 0, 0.0, pltpu.roll(up, 1, shift_axis))
                low_next = jnp.where(at == 0, 0.0, pltpu.roll(following, 1, shift_axis))
                diag = diag - low_next
                coef_ref[param, layer, 1 + 2 * axis_d] = jnp.where(at == size - 1, 0.0, following)
                coef_ref[param, layer, 2 + 2 * axis_d] = -low_up
            coef_ref[param, layer, 0] = diag

    def tile(layer, y):
        start = layer * plane + y * width_z
        return flat_ref[:MB, start : start + width_z].astype(F32)

    for layer in range(layers):
        for y in range(width_y):
            start = layer * plane + y * width_z
            state = tile(layer, y)
            terms = [(0, state), (5, pltpu.roll(state, width_z - 1, 1)), (6, pltpu.roll(state, 1, 1))]
            if layer < layers - 1:
                terms.append((1, tile(layer + 1, y)))
            if layer > 0:
                terms.append((2, tile(layer - 1, y)))
            if y < width_y - 1:
                terms.append((3, tile(layer, y + 1)))
            if y > 0:
                terms.append((4, tile(layer, y - 1)))
            for param in range(params):
                total = None
                for at, term in terms:
                    product = coef_ref[param, layer, at, y : y + 1, :] * term
                    total = product if total is None else total + product
                acc_ref[param * MB : (param + 1) * MB, start : start + width_z] = total

    count = column(count_ref[...])
    slots = sampled_ref.shape[0]
    held = []
    for slot in range(slots):
        held.append(jnp.where(slot < count, column(sampled_ref[slot : slot + 1]), -4 * layers * plane))
    cell = jnp.concatenate(held, axis=0)
    cell_ref[...] = cell
    z_of = lax.broadcasted_iota(I32, (1, width_z), 1)
    for layer in range(layers):
        for y in range(width_y):
            start = layer * plane + y * width_z
            away = z_of - (cell - start)
            hits = [away == 0, away == -plane, away == plane]
            hits.append(away == -width_z if y < width_y - 1 else None)
            hits.append(away == width_z if y > 0 else None)
            hits.append((away == -1) & (z_of < width_z - 1))
            hits.append((away == 1) & (z_of > 0))
            for at, hit in enumerate(hits):
                value = jnp.zeros((samples, width_z), BF16)
                if hit is not None:
                    value = jnp.where(hit, 1.0, 0.0).astype(BF16)
                pick_ref[at * samples : (at + 1) * samples, start : start + width_z] = value
    center_ref[...] = pick_ref[:samples]
    in_ref[...] = nt_dot(pick_ref[...], flat_ref[:MB, :]).astype(BF16)


def finish_layer(dims, from_next, layer, halo_refs, flat_ref, acc_ref, edge_ref, applied_ref, coef_ref, spread_ref, beside_ref):
    params, layers, width_y, width_z, plane = dims
    held = MB // len(halo_refs)
    faces = []
    for at in range(2 * SPLITS):
        part = halo_refs[0][held + at * params : held + (at + 1) * params].astype(F32)
        faces.append(part.reshape(params * width_y, width_z))
    signed = faces[0] + faces[1]
    diff = faces[2] + faces[3]
    edge = edge_ref[...].reshape(params * width_y, width_z)
    coef_ref[0] = jnp.where(from_next, edge, -(jnp.maximum(signed, 0.0) + diff))
    coef_ref[1] = jnp.where(from_next, 0.0, diff - jnp.minimum(signed, 0.0))
    size = held * width_y
    for at, halo_ref in enumerate(halo_refs):
        spread_ref[at * size : (at + 1) * size] = halo_ref[:held].astype(F32).reshape(size, width_z)
    for y in range(width_y):
        at = pl.multiple_of(layer * plane + y * width_z, width_z)
        lanes = slice(y * width_z, (y + 1) * width_z)
        state = flat_ref[:MB, pl.ds(at, width_z)].astype(F32)
        beside = spread_ref[pl.ds(y, MB, stride=width_y), :]
        beside_ref[:, lanes] = beside.astype(BF16)
        for param in range(params):
            modes = slice(param * MB, (param + 1) * MB)
            row = param * width_y + y
            total = acc_ref[modes, pl.ds(at, width_z)]
            total = total + coef_ref[1, row : row + 1, :] * state
            total = total + coef_ref[0, row : row + 1, :] * beside
            applied_ref[modes, lanes] = total.astype(BF16)


def near_kernel(dims, flat_ref, low_ref, high_ref, acc_ref, edge_ref, center_ref, cell_ref, sums_ref, picks_ref, side_ref, *scratch):
    params, layers, width_y, width_z, plane, samples = dims
    odd = core() == 1
    layer = (1 - core()) * (layers - 1)
    start = pl.multiple_of(layer * plane, plane)
    finish_layer(dims[:5], jnp.logical_not(odd), layer, (low_ref, high_ref), flat_ref, acc_ref, edge_ref, *scratch)
    applied_ref, beside_ref = scratch[0], scratch[3]
    sums_ref[...] = nt_dot(flat_ref[:, pl.ds(start, plane)], applied_ref[...])
    picks_ref[...] = nt_dot(center_ref[:, pl.ds(start, plane)], applied_ref[...])
    below = cell_ref[...]
    above = below - (layers - 1) * plane
    side_ref[...] = nt_dot(picked(jnp.where(odd, below, above), 0, plane), beside_ref[...]).astype(BF16)


def project_kernel(
    dims,
    relative,
    flat_ref,
    outer_ref,
    acc_ref,
    edge_ref,
    in_ref,
    center_ref,
    near_sums_ref,
    near_picks_ref,
    near_side_ref,
    cell_ref,
    table_ref,
    keep_ref,
    keep_rows_ref,
    packet_ref,
    sums_ref,
    *scratch,
):
    params, layers, width_y, width_z, plane, samples, devices, own = dims
    odd = core() == 1
    layer = core() * (layers - 1)
    lane = pl.multiple_of(layer * plane, plane)
    finish_layer(dims[:5], odd, layer, (outer_ref,), flat_ref, acc_ref, edge_ref, *scratch)
    applied_ref, beside_ref = scratch[0], scratch[3]

    sums = near_sums_ref[...] + nt_dot(flat_ref[:, pl.ds(lane, plane)], applied_ref[...])
    for param in range(params):
        sums_ref[pl.ds(param, sums.shape[0], stride=params), :] = sums[:, param * MB : (param + 1) * MB]
    size = own * params
    half = devices // 2
    me = lax.axis_index("cells")
    for place in range(devices):
        start = pl.multiple_of((me ^ relative[place]) * size, size)
        terms = sums_ref[pl.ds(start, size), :]
        if place < half:
            keep_ref[place * size : (place + 1) * size] = terms
        else:
            at = (place - half) * size
            packet_ref[at : at + size] = terms.astype(BF16)

    picks = nt_dot(center_ref[:, pl.ds(lane, plane)], applied_ref[...])
    got_applied = (near_picks_ref[...] + picks).astype(BF16)
    below = cell_ref[...]
    above = below - (layers - 1) * plane
    far = nt_dot(picked(jnp.where(odd, above, below), 0, plane), beside_ref[...]).astype(BF16)
    near = near_side_ref[...]
    got_below = in_ref[samples : 2 * samples] + jnp.where(odd, near, far)
    got_above = in_ref[2 * samples : 3 * samples] + jnp.where(odd, far, near)
    pieces = [got_applied[:, param * MB : (param + 1) * MB] for param in range(params)]
    pieces += [in_ref[:samples], got_below, got_above, in_ref[3 * samples :]]
    gathered = jnp.concatenate(pieces, axis=0)
    total_rows = gathered.shape[0]
    order = picked((table_ref[:, 0:1] ^ me) + table_ref[:, 1:2], 0, gathered.shape[0])
    ordered = jnp.dot(order, gathered, preferred_element_type=F32).astype(BF16)
    count = ordered.shape[0] // 2
    keep_rows_ref[...] = ordered[:count]
    packet_ref[half * size :] = ordered[count:]


def move_rows(rows, moves, from_ref, to_ref):
    block, pairs = moves
    from_ref[...] = rows.astype(F32)
    for new, old in pairs:
        to_ref[pl.ds(new, block), :] = from_ref[pl.ds(old, block), :]


def merge_kernel(wide_in, wide_out, moves, keep_ref, keep_rows_ref, got_ref, keep_out, rows_out, packet_out, from_ref, to_ref):
    size = keep_ref.shape[0]
    half = size // 2
    total = keep_ref[...] + got_ref[:size].astype(F32)
    if wide_in:
        total = total + got_ref[size : 2 * size].astype(F32)
    keep_out[...] = total[:half]
    if wide_out:
        head, rest = halves(total[half:])
        packet_out[:half] = head
        packet_out[half : 2 * half] = rest
    else:
        packet_out[:half] = total[half:].astype(BF16)
    count = keep_rows_ref.shape[0]
    rows = jnp.concatenate([keep_rows_ref[...], got_ref[got_ref.shape[0] - count :]], axis=0)
    move_rows(rows, moves, from_ref, to_ref)
    ordered = to_ref[...].astype(BF16)
    rows_out[...] = ordered[:count]
    packet_out[packet_out.shape[0] - count :] = ordered[count:]


def spread_kernel(wide_in, room, moves, keep_ref, keep_rows_ref, got_ref, keep_out, rows_out, *refs):
    size = keep_ref.shape[0]
    total = keep_ref[...] + got_ref[:size].astype(F32)
    if wide_in:
        total = total + got_ref[size : 2 * size].astype(F32)
    part = size // DIRECT
    count = keep_rows_ref.shape[0]
    rows = jnp.concatenate([keep_rows_ref[...], got_ref[got_ref.shape[0] - count :]], axis=0)
    packets_out, from_ref, to_ref = refs[:-2], refs[-2], refs[-1]
    to_ref[...] = jnp.zeros(to_ref.shape, F32)
    move_rows(rows, moves, from_ref, to_ref)
    ordered = to_ref[...].astype(BF16)
    keep_out[...] = total[:part]
    rows_out[...] = ordered[:room]
    for at, packet_out in enumerate(packets_out, 1):
        packet_out[:part] = total[at * part : (at + 1) * part].astype(BF16)
        packet_out[part:] = ordered[at * room : (at + 1) * room]


def final_kernel(volume, block, olds, keep_ref, keep_rows_ref, *refs):
    got_refs = refs[: DIRECT - 1]
    sum_out, rows_out, from_ref, to_ref = refs[DIRECT - 1 :]
    size = keep_ref.shape[0]
    total = keep_ref[...]
    rows = [keep_rows_ref[...]] + [None] * (DIRECT - 1)
    for at, got_ref in zip(ORDER, got_refs):
        total = total + got_ref[:size].astype(F32)
        rows[at] = got_ref[size:]
    sum_out[...] = volume * total
    me = lax.axis_index("cells")
    pairs = [((me ^ at) * block, old) for at, old in enumerate(olds)]
    move_rows(jnp.concatenate(rows, axis=0), (block, pairs), from_ref, to_ref)
    rows_out[...] = to_ref[...].astype(BF16)


def places(steps):
    return [steps - 3 - step for step in range(steps - 2)] + [steps - 1, steps - 2]


def shape(dims, dtype):
    return jax.ShapeDtypeStruct(dims, dtype)


def shards(basis, face_speed, face_diffusion, upwind_flag, reaction, sample_cell, sample_count):
    modes, layers, width_y, width_z = basis.shape
    params = face_speed.shape[0]
    devices = lax.axis_size("cells")
    slots = sample_cell.shape[2]
    plane = width_y * width_z
    cells = layers * plane
    own = modes // devices
    rows = params + OFFSETS
    samples = devices * slots
    steps = devices.bit_length() - 1

    tail = params * width_y
    hbm = pl.BlockSpec(memory_space=pltpu.HBM)
    planes = 2 * SPLITS * params
    to_low, to_high, to_outer = pl.pallas_call(
        functools.partial(pack_kernel, (params, layers)),
        out_shape=(
            shape((MB // 2 + planes, width_y, width_z), BF16),
            shape((MB // 2, width_y, width_z), BF16),
            shape((MB + planes, width_y, width_z), BF16),
        ),
        in_specs=[hbm] * 4,
        out_specs=(VMEM,) * 3,
        scratch_shapes=[
            pltpu.VMEM((params, width_y, width_z), F32),
            pltpu.VMEM((params, width_y, width_z), F32),
            pltpu.VMEM((params, width_y, width_z), I32),
            pltpu.SemaphoreType.DMA((6,)),
        ],
        compiler_params=LIMIT,
        name="pack_halo",
    )(*[pltpu.with_memory_space_constraint(value, pltpu.HBM) for value in (basis, face_speed, face_diffusion, upwind_flag)])
    inner_pairs = [(i, i ^ 1) for i in range(devices)]
    outer_pairs = []
    for i in range(1, devices - 1, 2):
        outer_pairs += [(i, i + 1), (i + 1, i)]
    low = lax.ppermute(to_low, "cells", inner_pairs)
    high = lax.ppermute(to_high, "cells", inner_pairs)
    outer = lax.ppermute(to_outer, "cells", outer_pairs)

    loaded, cells_in, counts_in = pl.pallas_call(
        load_kernel,
        out_shape=(shape(basis.shape, BF16), shape((slots, devices), I32), shape((1, devices), I32)),
        in_specs=[hbm] * 3 + [VMEM],
        out_specs=(VMEM,) * 3,
        scratch_shapes=[pltpu.SemaphoreType.DMA((3,))],
        compiler_params=LIMIT,
        name="load",
    )(pltpu.with_memory_space_constraint(basis, pltpu.HBM), sample_cell[0].T, sample_count, to_outer)
    flat = loaded.reshape(modes, cells)

    block = slots * rows
    relative = [sum(((place >> (steps - 1 - step)) & 1) << step for step in range(steps)) for place in range(devices)]
    block = slots * rows
    share = devices // DIRECT * block
    room = round_up(share, 16)
    in_block = np.arange(block)
    table = np.zeros((devices, block, 8), np.int32)
    turns, spreads, olds = [], [], []
    for place in range(devices):
        old = (((place & 1) << (steps - 1)) + (place >> 1)) * block
        turns.append((place * block, old))
        spreads.append((place * block // share * room + place * block % share, old))
        came = sum(((place >> step) & 1) << to for step, to in enumerate(places(steps)))
        olds.append(came * block // share * room + came * block % share)
        table[place, :, 0] = relative[place]
        table[place, :, 1] = (in_block // slots) * samples + (in_block % slots) * devices
    table = jnp.asarray(table.reshape(devices * block, 8))

    acc, edge, got_in, center, cell = pl.pallas_call(
        functools.partial(local_kernel, (params, layers, width_y, width_z, plane, samples)),
        out_shape=(
            shape((params * MB, cells), F32),
            shape((params, width_y, width_z), F32),
            shape((OFFSETS * samples, MB), BF16),
            shape((samples, cells), BF16),
            shape((samples, 1), I32),
        ),
        in_specs=[VMEM] * 7,
        out_specs=(VMEM,) * 5,
        scratch_shapes=[
            pltpu.VMEM((params, layers, OFFSETS, width_y, width_z), F32),
            pltpu.VMEM((OFFSETS * samples, cells), BF16),
        ],
        compiler_params=LIMIT,
        cost_estimate=SMALL,
        name="local_stencil",
    )(flat, face_speed, face_diffusion, upwind_flag, reaction, cells_in, counts_in)

    finish_scratch = [
        pltpu.VMEM((params * MB, plane), BF16),
        pltpu.VMEM((2, tail, width_z), F32),
        pltpu.VMEM((MB * width_y, width_z), F32),
        pltpu.VMEM((MB, plane), BF16),
    ]
    near_sums, near_picks, near_side = pl.pallas_call(
        functools.partial(near_kernel, (params, layers, width_y, width_z, plane, samples)),
        out_shape=(
            shape((modes, params * MB), F32),
            shape((samples, params * MB), F32),
            shape((samples, MB), BF16),
        ),
        in_specs=[VMEM] * 7,
        out_specs=(VMEM,) * 3,
        scratch_shapes=finish_scratch,
        compiler_params=LIMIT,
        cost_estimate=SMALL,
        name="near_layer",
    )(flat, low, high, acc, edge, center, cell)

    size = own * params
    half = devices // 2
    count = half * block
    keep, keep_rows, packet = pl.pallas_call(
        functools.partial(
            project_kernel,
            (params, layers, width_y, width_z, plane, samples, devices, own),
            relative,
        ),
        out_shape=(
            shape((half * size, MB), F32),
            shape((count, MB), BF16),
            shape((half * size + count, MB), BF16),
        ),
        in_specs=[VMEM] * 11,
        out_specs=(VMEM,) * 3,
        scratch_shapes=[pltpu.VMEM((params * modes, MB), F32)] + finish_scratch,
        compiler_params=LIMIT,
        name="project",
    )(
        flat,
        outer,
        acc,
        edge,
        got_in,
        center,
        near_sums,
        near_picks,
        near_side,
        cell,
        table,
    )

    wide = False
    for step in range(steps - 2):
        got = lax.ppermute(packet, "cells", [(i, i ^ (1 << step)) for i in range(devices)])
        if step < steps - 3:
            next_wide = step + 1 > NARROW_STEPS
            half //= 2
            packet_rows = (2 if next_wide else 1) * half * size + count
            keep, keep_rows, packet = pl.pallas_call(
                functools.partial(merge_kernel, wide, next_wide, (block, turns)),
                out_shape=(
                    shape((half * size, MB), F32),
                    shape((count, MB), BF16),
                    shape((packet_rows, MB), BF16),
                ),
                in_specs=[VMEM] * 3,
                out_specs=(VMEM,) * 3,
                scratch_shapes=[pltpu.VMEM((2 * count, MB), F32), pltpu.VMEM((2 * count, MB), F32)],
                compiler_params=LIMIT,
                name="merge",
            )(keep, keep_rows, got)
            wide = next_wide
    sent = shape((size + room, MB), BF16)
    keep, keep_rows, *packets = pl.pallas_call(
        functools.partial(spread_kernel, wide, room, (block, spreads)),
        out_shape=(shape((size, MB), F32), shape((room, MB), BF16)) + (sent,) * (DIRECT - 1),
        in_specs=[VMEM] * 3,
        out_specs=(VMEM,) * (DIRECT + 1),
        scratch_shapes=[pltpu.VMEM((2 * count, MB), F32), pltpu.VMEM((DIRECT * room, MB), F32)],
        compiler_params=LIMIT,
        name="spread",
    )(keep, keep_rows, got)
    got = [None] * DIRECT
    for at in ORDER:
        mask = ((at >> 1) << (steps - 2)) | ((at & 1) << (steps - 1))
        got[at] = lax.ppermute(packets[at - 1], "cells", [(i, i ^ mask) for i in range(devices)])
    volume = 1.0 / (layers * devices * width_y * width_z)
    summed, sampled = pl.pallas_call(
        functools.partial(final_kernel, volume, block, olds),
        out_shape=(shape((size, MB), F32), shape((2 * count, MB), BF16)),
        in_specs=[VMEM] * (DIRECT + 1),
        out_specs=(VMEM,) * 2,
        scratch_shapes=[pltpu.VMEM((DIRECT * room, MB), F32), pltpu.VMEM((2 * count, MB), F32)],
        compiler_params=LIMIT,
        name="finish",
    )(keep, keep_rows, *[got[at] for at in ORDER])
    galerkin = summed.reshape(own, params, MB)
    sampled = sampled.reshape(devices, rows, slots, MB)
    return (galerkin, jnp.transpose(sampled, (0, 2, 1, 3))[None])


def solution(mesh):
    return jax.shard_map(
        shards,
        mesh=mesh,
        in_specs=(
            P(None, ("groups", "cells"), None, None),
            P(None, None, ("groups", "cells"), None, None),
            P(None, None, ("groups", "cells"), None, None),
            P(None, None, ("groups", "cells"), None, None),
            P(None, ("groups", "cells"), None, None),
            P(("groups", "cells"), None, None),
            P(("groups", "cells"), None),
        ),
        out_specs=(
            P(("groups", "cells"), None, None),
            P(("groups", "cells"), None, None, None, None),
        ),
        check_vma=False,
    )
```

```python
import functools

import jax
import jax.numpy as jnp
import numpy as np
from jax import lax
from jax.experimental import pallas as pl
from jax.experimental.pallas import tpu as pltpu
from jax.sharding import PartitionSpec as P

MB = 128
SPLITS = 2
NARROW_STEPS = 1
DIRECT = 4
ORDER = (3, 2, 1)
BF16 = jnp.bfloat16
F32 = jnp.float32
I32 = jnp.int32
OFFSETS = 7
VMEM = pl.BlockSpec(memory_space=pltpu.VMEM)
SMALL = pl.CostEstimate(flops=1, bytes_accessed=1, transcendentals=0)
LIMIT = pltpu.CompilerParams(vmem_limit_bytes=20 * 1024 * 1024)


def nt_dot(left, right):
    return lax.dot_general(left, right, (((1,), (1,)), ((), ())), preferred_element_type=F32)


def picked(targets, start, count):
    lanes = lax.broadcasted_iota(I32, (1, count), 1) + start
    return jnp.where(targets == lanes, 1.0, 0.0).astype(BF16)


def column(row):
    size = row.shape[1]
    down = lax.broadcasted_iota(I32, (size, size), 0)
    across = lax.broadcasted_iota(I32, (size, size), 1)
    spread = jnp.where(down == across, row.astype(F32), 0.0)
    return jnp.sum(spread, axis=1, keepdims=True).astype(I32)


def round_up(value, multiple):
    return -(-value // multiple) * multiple


def halves(value):
    head = value.astype(BF16)
    return head, (value - head.astype(F32)).astype(BF16)


def core():
    return lax.rem(lax.axis_index("cells"), 2)


def face_parts(speed, diff, flag):
    parts = []
    for value in (jnp.where(flag == 1, speed, -speed), diff):
        for _ in range(SPLITS):
            head = value.astype(BF16)
            value = value - head.astype(F32)
            parts.append(head)
    return parts


def pack_kernel(dims, basis_ref, speed_ref, diff_ref, flag_ref, outer_ref, speed_buf, diff_buf, flag_buf, sems):
    params, layers = dims
    last = layers - 1
    block = pl.ds(0, MB)
    outer = pltpu.make_async_copy(basis_ref.at[block, core() * last], outer_ref.at[block], sems.at[0])
    copies = [
        pltpu.make_async_copy(speed_ref.at[:, 0, last], speed_buf, sems.at[1]),
        pltpu.make_async_copy(diff_ref.at[:, 0, last], diff_buf, sems.at[2]),
        pltpu.make_async_copy(flag_ref.at[:, 0, last], flag_buf, sems.at[3]),
    ]
    for copy in copies + [outer]:
        copy.start()
    for copy in copies:
        copy.wait()
    for at, part in enumerate(face_parts(speed_buf[...], diff_buf[...], flag_buf[...])):
        outer_ref[MB + at * params : MB + (at + 1) * params] = part
    outer.wait()


def load_kernel(last, basis_ref, cell_ref, count_ref, outer_ref, basis_out, cell_out, count_out, low_ref, high_ref, sems):
    half = MB // 2
    low, high = pl.ds(0, half), pl.ds(half, half)
    beside = (1 - core()) * last
    pairs = (
        (basis_ref.at[low, beside], low_ref.at[low]),
        (basis_ref.at[high, beside], high_ref),
        (basis_ref, basis_out),
        (cell_ref, cell_out),
        (count_ref, count_out),
    )
    copies = [pltpu.make_async_copy(source, out, sems.at[at]) for at, (source, out) in enumerate(pairs)]
    for copy in copies:
        copy.start()
    low_ref[half:] = outer_ref[MB:]
    for copy in copies:
        copy.wait()


def local_kernel(
    dims,
    flat_ref,
    speed_ref,
    diff_ref,
    flag_ref,
    react_ref,
    sampled_ref,
    count_ref,
    acc_ref,
    edge_ref,
    in_ref,
    center_ref,
    cell_ref,
    coef_ref,
    pick_ref,
):
    params, layers, width_y, width_z, plane, samples = dims
    y_at = lax.broadcasted_iota(I32, (width_y, width_z), 0)
    z_at = lax.broadcasted_iota(I32, (width_y, width_z), 1)
    for param in range(params):
        uppers, nexts = [], []
        for layer in range(layers):
            up_d, next_d = [], []
            for axis_d in range(3):
                forward = flag_ref[param, axis_d, layer] == 1
                speed = speed_ref[param, axis_d, layer]
                diff = diff_ref[param, axis_d, layer]
                up_d.append(jnp.where(forward, speed, 0.0) + diff)
                next_d.append(jnp.where(forward, 0.0, -speed) - diff)
            uppers.append(up_d)
            nexts.append(next_d)
        edge_ref[param] = nexts[layers - 1][0]
        for layer in range(layers):
            diag = react_ref[param, layer]
            diag = diag + uppers[layer][0] + uppers[layer][1] + uppers[layer][2]
            if layer > 0:
                diag = diag - nexts[layer - 1][0]
                coef_ref[param, layer, 2] = -uppers[layer - 1][0]
            coef_ref[param, layer, 1] = nexts[layer][0]
            for axis_d, at, shift_axis, size in ((1, y_at, 0, width_y), (2, z_at, 1, width_z)):
                up, following = uppers[layer][axis_d], nexts[layer][axis_d]
                low_up = jnp.where(at == 0, 0.0, pltpu.roll(up, 1, shift_axis))
                low_next = jnp.where(at == 0, 0.0, pltpu.roll(following, 1, shift_axis))
                diag = diag - low_next
                coef_ref[param, layer, 1 + 2 * axis_d] = jnp.where(at == size - 1, 0.0, following)
                coef_ref[param, layer, 2 + 2 * axis_d] = -low_up
            coef_ref[param, layer, 0] = diag

    def tile(layer, y):
        start = layer * plane + y * width_z
        return flat_ref[:MB, start : start + width_z].astype(F32)

    for layer in range(layers):
        for y in range(width_y):
            start = layer * plane + y * width_z
            state = tile(layer, y)
            terms = [(0, state), (5, pltpu.roll(state, width_z - 1, 1)), (6, pltpu.roll(state, 1, 1))]
            if layer < layers - 1:
                terms.append((1, tile(layer + 1, y)))
            if layer > 0:
                terms.append((2, tile(layer - 1, y)))
            if y < width_y - 1:
                terms.append((3, tile(layer, y + 1)))
            if y > 0:
                terms.append((4, tile(layer, y - 1)))
            for param in range(params):
                total = None
                for at, term in terms:
                    product = coef_ref[param, layer, at, y : y + 1, :] * term
                    total = product if total is None else total + product
                acc_ref[param * MB : (param + 1) * MB, start : start + width_z] = total

    count = column(count_ref[...])
    slots = sampled_ref.shape[0]
    held = []
    for slot in range(slots):
        held.append(jnp.where(slot < count, column(sampled_ref[slot : slot + 1]), -4 * layers * plane))
    cell = jnp.concatenate(held, axis=0)
    cell_ref[...] = cell
    z_of = lax.broadcasted_iota(I32, (1, width_z), 1)
    for layer in range(layers):
        for y in range(width_y):
            start = layer * plane + y * width_z
            away = z_of - (cell - start)
            hits = [away == 0, away == -plane, away == plane]
            hits.append(away == -width_z if y < width_y - 1 else None)
            hits.append(away == width_z if y > 0 else None)
            hits.append((away == -1) & (z_of < width_z - 1))
            hits.append((away == 1) & (z_of > 0))
            for at, hit in enumerate(hits):
                value = jnp.zeros((samples, width_z), BF16)
                if hit is not None:
                    value = jnp.where(hit, 1.0, 0.0).astype(BF16)
                pick_ref[at * samples : (at + 1) * samples, start : start + width_z] = value
    center_ref[...] = pick_ref[:samples]
    in_ref[...] = nt_dot(pick_ref[...], flat_ref[:MB, :]).astype(BF16)


def finish_layer(dims, from_next, layer, halo_refs, flat_ref, acc_ref, edge_ref, applied_ref, coef_ref, spread_ref, beside_ref):
    params, layers, width_y, width_z, plane = dims
    held = MB // len(halo_refs)
    faces = []
    for at in range(2 * SPLITS):
        part = halo_refs[0][held + at * params : held + (at + 1) * params].astype(F32)
        faces.append(part.reshape(params * width_y, width_z))
    signed = faces[0] + faces[1]
    diff = faces[2] + faces[3]
    edge = edge_ref[...].reshape(params * width_y, width_z)
    coef_ref[0] = jnp.where(from_next, edge, -(jnp.maximum(signed, 0.0) + diff))
    coef_ref[1] = jnp.where(from_next, 0.0, diff - jnp.minimum(signed, 0.0))
    size = held * width_y
    for at, halo_ref in enumerate(halo_refs):
        spread_ref[at * size : (at + 1) * size] = halo_ref[:held].astype(F32).reshape(size, width_z)
    for y in range(width_y):
        at = pl.multiple_of(layer * plane + y * width_z, width_z)
        lanes = slice(y * width_z, (y + 1) * width_z)
        state = flat_ref[:MB, pl.ds(at, width_z)].astype(F32)
        beside = spread_ref[pl.ds(y, MB, stride=width_y), :]
        beside_ref[:, lanes] = beside.astype(BF16)
        for param in range(params):
            modes = slice(param * MB, (param + 1) * MB)
            row = param * width_y + y
            total = acc_ref[modes, pl.ds(at, width_z)]
            total = total + coef_ref[1, row : row + 1, :] * state
            total = total + coef_ref[0, row : row + 1, :] * beside
            applied_ref[modes, lanes] = total.astype(BF16)


def near_kernel(dims, flat_ref, low_ref, high_ref, acc_ref, edge_ref, center_ref, cell_ref, sums_ref, picks_ref, side_ref, *scratch):
    params, layers, width_y, width_z, plane, samples = dims
    odd = core() == 1
    layer = (1 - core()) * (layers - 1)
    start = pl.multiple_of(layer * plane, plane)
    finish_layer(dims[:5], jnp.logical_not(odd), layer, (low_ref, high_ref), flat_ref, acc_ref, edge_ref, *scratch)
    applied_ref, beside_ref = scratch[0], scratch[3]
    sums_ref[...] = nt_dot(flat_ref[:, pl.ds(start, plane)], applied_ref[...])
    picks_ref[...] = nt_dot(center_ref[:, pl.ds(start, plane)], applied_ref[...])
    below = cell_ref[...]
    above = below - (layers - 1) * plane
    side_ref[...] = nt_dot(picked(jnp.where(odd, below, above), 0, plane), beside_ref[...]).astype(BF16)


def project_kernel(
    dims,
    relative,
    flat_ref,
    outer_ref,
    acc_ref,
    edge_ref,
    in_ref,
    center_ref,
    near_sums_ref,
    near_picks_ref,
    near_side_ref,
    cell_ref,
    table_ref,
    keep_ref,
    keep_rows_ref,
    packet_ref,
    sums_ref,
    *scratch,
):
    params, layers, width_y, width_z, plane, samples, devices, own = dims
    odd = core() == 1
    layer = core() * (layers - 1)
    lane = pl.multiple_of(layer * plane, plane)
    finish_layer(dims[:5], odd, layer, (outer_ref,), flat_ref, acc_ref, edge_ref, *scratch)
    applied_ref, beside_ref = scratch[0], scratch[3]

    sums = near_sums_ref[...] + nt_dot(flat_ref[:, pl.ds(lane, plane)], applied_ref[...])
    for param in range(params):
        sums_ref[pl.ds(param, sums.shape[0], stride=params), :] = sums[:, param * MB : (param + 1) * MB]
    size = own * params
    half = devices // 2
    me = lax.axis_index("cells")
    for place in range(devices):
        start = pl.multiple_of((me ^ relative[place]) * size, size)
        terms = sums_ref[pl.ds(start, size), :]
        if place < half:
            keep_ref[place * size : (place + 1) * size] = terms
        else:
            at = (place - half) * size
            packet_ref[at : at + size] = terms.astype(BF16)

    picks = nt_dot(center_ref[:, pl.ds(lane, plane)], applied_ref[...])
    got_applied = (near_picks_ref[...] + picks).astype(BF16)
    below = cell_ref[...]
    above = below - (layers - 1) * plane
    far = nt_dot(picked(jnp.where(odd, above, below), 0, plane), beside_ref[...]).astype(BF16)
    near = near_side_ref[...]
    got_below = in_ref[samples : 2 * samples] + jnp.where(odd, near, far)
    got_above = in_ref[2 * samples : 3 * samples] + jnp.where(odd, far, near)
    pieces = [got_applied[:, param * MB : (param + 1) * MB] for param in range(params)]
    pieces += [in_ref[:samples], got_below, got_above, in_ref[3 * samples :]]
    gathered = jnp.concatenate(pieces, axis=0)
    total_rows = gathered.shape[0]
    order = picked((table_ref[:, 0:1] ^ me) + table_ref[:, 1:2], 0, gathered.shape[0])
    ordered = jnp.dot(order, gathered, preferred_element_type=F32).astype(BF16)
    count = ordered.shape[0] // 2
    keep_rows_ref[...] = ordered[:count]
    packet_ref[half * size :] = ordered[count:]


def move_rows(rows, moves, from_ref, to_ref):
    block, pairs = moves
    from_ref[...] = rows.astype(F32)
    for new, old in pairs:
        to_ref[pl.ds(new, block), :] = from_ref[pl.ds(old, block), :]


def merge_kernel(wide_in, wide_out, moves, keep_ref, keep_rows_ref, got_ref, keep_out, rows_out, packet_out, from_ref, to_ref):
    size = keep_ref.shape[0]
    half = size // 2
    total = keep_ref[...] + got_ref[:size].astype(F32)
    if wide_in:
        total = total + got_ref[size : 2 * size].astype(F32)
    keep_out[...] = total[:half]
    if wide_out:
        head, rest = halves(total[half:])
        packet_out[:half] = head
        packet_out[half : 2 * half] = rest
    else:
        packet_out[:half] = total[half:].astype(BF16)
    count = keep_rows_ref.shape[0]
    rows = jnp.concatenate([keep_rows_ref[...], got_ref[got_ref.shape[0] - count :]], axis=0)
    move_rows(rows, moves, from_ref, to_ref)
    ordered = to_ref[...].astype(BF16)
    rows_out[...] = ordered[:count]
    packet_out[packet_out.shape[0] - count :] = ordered[count:]


def spread_kernel(wide_in, room, moves, keep_ref, keep_rows_ref, got_ref, keep_out, rows_out, *refs):
    size = keep_ref.shape[0]
    total = keep_ref[...] + got_ref[:size].astype(F32)
    if wide_in:
        total = total + got_ref[size : 2 * size].astype(F32)
    part = size // DIRECT
    count = keep_rows_ref.shape[0]
    rows = jnp.concatenate([keep_rows_ref[...], got_ref[got_ref.shape[0] - count :]], axis=0)
    packets_out, from_ref, to_ref = refs[:-2], refs[-2], refs[-1]
    to_ref[...] = jnp.zeros(to_ref.shape, F32)
    move_rows(rows, moves, from_ref, to_ref)
    ordered = to_ref[...].astype(BF16)
    keep_out[...] = total[:part]
    rows_out[...] = ordered[:room]
    for at, packet_out in enumerate(packets_out, 1):
        packet_out[:part] = total[at * part : (at + 1) * part].astype(BF16)
        packet_out[part:] = ordered[at * room : (at + 1) * room]


def final_kernel(volume, block, olds, keep_ref, keep_rows_ref, *refs):
    got_refs = refs[: DIRECT - 1]
    sum_out, rows_out, from_ref, to_ref = refs[DIRECT - 1 :]
    size = keep_ref.shape[0]
    total = keep_ref[...]
    rows = [keep_rows_ref[...]] + [None] * (DIRECT - 1)
    for at, got_ref in zip(ORDER, got_refs):
        total = total + got_ref[:size].astype(F32)
        rows[at] = got_ref[size:]
    sum_out[...] = volume * total
    me = lax.axis_index("cells")
    pairs = [((me ^ at) * block, old) for at, old in enumerate(olds)]
    move_rows(jnp.concatenate(rows, axis=0), (block, pairs), from_ref, to_ref)
    rows_out[...] = to_ref[...].astype(BF16)


def places(steps):
    return [steps - 3 - step for step in range(steps - 2)] + [steps - 1, steps - 2]


def shape(dims, dtype):
    return jax.ShapeDtypeStruct(dims, dtype)


def shards(basis, face_speed, face_diffusion, upwind_flag, reaction, sample_cell, sample_count):
    modes, layers, width_y, width_z = basis.shape
    params = face_speed.shape[0]
    devices = lax.axis_size("cells")
    slots = sample_cell.shape[2]
    plane = width_y * width_z
    cells = layers * plane
    own = modes // devices
    rows = params + OFFSETS
    samples = devices * slots
    steps = devices.bit_length() - 1

    tail = params * width_y
    hbm = pl.BlockSpec(memory_space=pltpu.HBM)
    planes = 2 * SPLITS * params
    to_outer = pl.pallas_call(
        functools.partial(pack_kernel, (params, layers)),
        out_shape=shape((MB + planes, width_y, width_z), BF16),
        in_specs=[hbm] * 4,
        out_specs=VMEM,
        scratch_shapes=[
            pltpu.VMEM((params, width_y, width_z), F32),
            pltpu.VMEM((params, width_y, width_z), F32),
            pltpu.VMEM((params, width_y, width_z), I32),
            pltpu.SemaphoreType.DMA((4,)),
        ],
        compiler_params=LIMIT,
        name="pack_halo",
    )(*[pltpu.with_memory_space_constraint(value, pltpu.HBM) for value in (basis, face_speed, face_diffusion, upwind_flag)])
    inner_pairs = [(i, i ^ 1) for i in range(devices)]
    outer_pairs = []
    for i in range(1, devices - 1, 2):
        outer_pairs += [(i, i + 1), (i + 1, i)]
    outer = lax.ppermute(to_outer, "cells", outer_pairs)

    loaded, cells_in, counts_in, to_low, to_high = pl.pallas_call(
        functools.partial(load_kernel, layers - 1),
        out_shape=(
            shape(basis.shape, BF16),
            shape((slots, devices), I32),
            shape((1, devices), I32),
            shape((MB // 2 + planes, width_y, width_z), BF16),
            shape((MB // 2, width_y, width_z), BF16),
        ),
        in_specs=[hbm] * 3 + [VMEM],
        out_specs=(VMEM,) * 5,
        scratch_shapes=[pltpu.SemaphoreType.DMA((5,))],
        compiler_params=LIMIT,
        name="load",
    )(pltpu.with_memory_space_constraint(basis, pltpu.HBM), sample_cell[0].T, sample_count, to_outer)
    flat = loaded.reshape(modes, cells)
    low = lax.ppermute(to_low, "cells", inner_pairs)
    high = lax.ppermute(to_high, "cells", inner_pairs)

    block = slots * rows
    relative = [sum(((place >> (steps - 1 - step)) & 1) << step for step in range(steps)) for place in range(devices)]
    block = slots * rows
    share = devices // DIRECT * block
    room = round_up(share, 16)
    in_block = np.arange(block)
    table = np.zeros((devices, block, 8), np.int32)
    turns, spreads, olds = [], [], []
    for place in range(devices):
        old = (((place & 1) << (steps - 1)) + (place >> 1)) * block
        turns.append((place * block, old))
        spreads.append((place * block // share * room + place * block % share, old))
        came = sum(((place >> step) & 1) << to for step, to in enumerate(places(steps)))
        olds.append(came * block // share * room + came * block % share)
        table[place, :, 0] = relative[place]
        table[place, :, 1] = (in_block // slots) * samples + (in_block % slots) * devices
    table = jnp.asarray(table.reshape(devices * block, 8))

    acc, edge, got_in, center, cell = pl.pallas_call(
        functools.partial(local_kernel, (params, layers, width_y, width_z, plane, samples)),
        out_shape=(
            shape((params * MB, cells), F32),
            shape((params, width_y, width_z), F32),
            shape((OFFSETS * samples, MB), BF16),
            shape((samples, cells), BF16),
            shape((samples, 1), I32),
        ),
        in_specs=[VMEM] * 7,
        out_specs=(VMEM,) * 5,
        scratch_shapes=[
            pltpu.VMEM((params, layers, OFFSETS, width_y, width_z), F32),
            pltpu.VMEM((OFFSETS * samples, cells), BF16),
        ],
        compiler_params=LIMIT,
        cost_estimate=SMALL,
        name="local_stencil",
    )(flat, face_speed, face_diffusion, upwind_flag, reaction, cells_in, counts_in)

    finish_scratch = [
        pltpu.VMEM((params * MB, plane), BF16),
        pltpu.VMEM((2, tail, width_z), F32),
        pltpu.VMEM((MB * width_y, width_z), F32),
        pltpu.VMEM((MB, plane), BF16),
    ]
    near_sums, near_picks, near_side = pl.pallas_call(
        functools.partial(near_kernel, (params, layers, width_y, width_z, plane, samples)),
        out_shape=(
            shape((modes, params * MB), F32),
            shape((samples, params * MB), F32),
            shape((samples, MB), BF16),
        ),
        in_specs=[VMEM] * 7,
        out_specs=(VMEM,) * 3,
        scratch_shapes=finish_scratch,
        compiler_params=LIMIT,
        cost_estimate=SMALL,
        name="near_layer",
    )(flat, low, high, acc, edge, center, cell)

    size = own * params
    half = devices // 2
    count = half * block
    keep, keep_rows, packet = pl.pallas_call(
        functools.partial(
            project_kernel,
            (params, layers, width_y, width_z, plane, samples, devices, own),
            relative,
        ),
        out_shape=(
            shape((half * size, MB), F32),
            shape((count, MB), BF16),
            shape((half * size + count, MB), BF16),
        ),
        in_specs=[VMEM] * 11,
        out_specs=(VMEM,) * 3,
        scratch_shapes=[pltpu.VMEM((params * modes, MB), F32)] + finish_scratch,
        compiler_params=LIMIT,
        name="project",
    )(
        flat,
        outer,
        acc,
        edge,
        got_in,
        center,
        near_sums,
        near_picks,
        near_side,
        cell,
        table,
    )

    wide = False
    for step in range(steps - 2):
        got = lax.ppermute(packet, "cells", [(i, i ^ (1 << step)) for i in range(devices)])
        if step < steps - 3:
            next_wide = step + 1 > NARROW_STEPS
            half //= 2
            packet_rows = (2 if next_wide else 1) * half * size + count
            keep, keep_rows, packet = pl.pallas_call(
                functools.partial(merge_kernel, wide, next_wide, (block, turns)),
                out_shape=(
                    shape((half * size, MB), F32),
                    shape((count, MB), BF16),
                    shape((packet_rows, MB), BF16),
                ),
                in_specs=[VMEM] * 3,
                out_specs=(VMEM,) * 3,
                scratch_shapes=[pltpu.VMEM((2 * count, MB), F32), pltpu.VMEM((2 * count, MB), F32)],
                compiler_params=LIMIT,
                name="merge",
            )(keep, keep_rows, got)
            wide = next_wide
    sent = shape((size + room, MB), BF16)
    keep, keep_rows, *packets = pl.pallas_call(
        functools.partial(spread_kernel, wide, room, (block, spreads)),
        out_shape=(shape((size, MB), F32), shape((room, MB), BF16)) + (sent,) * (DIRECT - 1),
        in_specs=[VMEM] * 3,
        out_specs=(VMEM,) * (DIRECT + 1),
        scratch_shapes=[pltpu.VMEM((2 * count, MB), F32), pltpu.VMEM((DIRECT * room, MB), F32)],
        compiler_params=LIMIT,
        name="spread",
    )(keep, keep_rows, got)
    got = [None] * DIRECT
    for at in ORDER:
        mask = ((at >> 1) << (steps - 2)) | ((at & 1) << (steps - 1))
        got[at] = lax.ppermute(packets[at - 1], "cells", [(i, i ^ mask) for i in range(devices)])
    volume = 1.0 / (layers * devices * width_y * width_z)
    summed, sampled = pl.pallas_call(
        functools.partial(final_kernel, volume, block, olds),
        out_shape=(shape((size, MB), F32), shape((2 * count, MB), BF16)),
        in_specs=[VMEM] * (DIRECT + 1),
        out_specs=(VMEM,) * 2,
        scratch_shapes=[pltpu.VMEM((DIRECT * room, MB), F32), pltpu.VMEM((2 * count, MB), F32)],
        compiler_params=LIMIT,
        name="finish",
    )(keep, keep_rows, *[got[at] for at in ORDER])
    galerkin = summed.reshape(own, params, MB)
    sampled = sampled.reshape(devices, rows, slots, MB)
    return (galerkin, jnp.transpose(sampled, (0, 2, 1, 3))[None])


def solution(mesh):
    return jax.shard_map(
        shards,
        mesh=mesh,
        in_specs=(
            P(None, ("groups", "cells"), None, None),
            P(None, None, ("groups", "cells"), None, None),
            P(None, None, ("groups", "cells"), None, None),
            P(None, None, ("groups", "cells"), None, None),
            P(None, ("groups", "cells"), None, None),
            P(("groups", "cells"), None, None),
            P(("groups", "cells"), None),
        ),
        out_specs=(
            P(("groups", "cells"), None, None),
            P(("groups", "cells"), None, None, None, None),
        ),
        check_vma=False,
    )
```
